512 devices in a mesh: dp: 32 (over z_lo, x), mp: 16 (over y, z_hi, core).
Axes of the slice: x: 4, y: 4, z: 16 (z_hi: 2, z_lo: 8; z = z_hi * 8 + z_lo), core: 2. Of those that a mesh axis runs over, the one named last changes fastest.
Arguments:
- queries: bfloat16 [32, 512, 2048], P('dp', 'mp'), may hold values from -6 to 6
- keys: bfloat16 [32, 512, 1024], P('dp'), may hold values from -6 to 6
- values: bfloat16 [32, 512, 1024], P('dp'), may hold values from -6 to 6
- stream: bfloat16 [32, 512, 3584], P('dp', None, 'mp'), may hold values from -6 to 6
- out_proj: bfloat16 [2048, 3584], P(None, 'mp'), may hold values from -0.125 to 0.125
- norm_gain: float32 [3584], P('mp'), may hold values from 0.1 to 1.9
- tag_proj: bfloat16 [3584, 128], P('mp'), may hold values from -0.03125 to 0.03125
- direction: float32 [2048, 3584], P('dp', 'mp'), may hold values from -120 to 120
- starts: int32 [32, 4], P('dp'), may hold values from 0 to 511, as said below
- tags: int32 [32, 512], P('dp'), may hold values from 0 to 127
Outputs:
- iterate: float32 [2048, 3584], P('dp', 'mp')
The draws below stay inside these ranges and needn't reach their ends.
Inputs may be any that keep to these rules, and one draw needn't show every extreme that they name: `starts`: each sequence's first entry is 0 and the entries rise strictly, so every file holds one token or more.
All inputs are finite; a program needn't handle non-finite values.
Results may differ from the reference program's by a relative error of at most 0.0032.
Values may be sent and summed in bfloat16 or wider, within the bound.
No kernel may reach another device: no remote copies, remote signals or barrier semaphores. Data moves between devices by JAX's collectives and lax.ppermute only.
A program may use at most 64 MiB of HBM per device.

```python
import jax
import jax.numpy as jnp
from jax import lax

D = 3584
HD = 256
HQ = 8
HK = 4
TAGS = 128
WINDOW = 256
FILES = 4
ITERS = 2
LEN = 512
SEQS = 32


def draw_direction(key, part):
    key = jax.random.fold_in(key, 11)
    k_base, k_rows, k_cols = jax.random.split(key, 3)
    rows = HQ * HD
    rising = 3.0 ** (jnp.arange(rows, dtype=jnp.float32)[:, None] / rows)
    row_scale = rising * jnp.exp(jax.random.uniform(k_rows, (rows, 1), jnp.float32, 0.0, jnp.log(10.0)))
    col_scale = jnp.exp(jax.random.uniform(k_cols, (1, D), jnp.float32, 0.0, jnp.log(10.0)))
    base = jnp.clip(jax.random.normal(k_base, (rows, D), jnp.float32), -4.0, 4.0)
    return (0.1 * base * row_scale * col_scale).astype(jnp.float32)


def draw_starts(key, part):
    key = jax.random.fold_in(key, 12)
    seq_keys = jax.random.split(key, SEQS)

    def one(seq_key):
        cuts = jax.random.permutation(seq_key, LEN - 1)[:FILES - 1] + 1
        cuts = jnp.sort(cuts.astype(jnp.int32))
        return jnp.concatenate([jnp.zeros((1,), jnp.int32), cuts])
    return jax.vmap(one)(seq_keys).astype(jnp.int32)


def set_ends(values, own_key, low, largest):
    shape = values.shape
    place = [jax.random.randint(jax.random.fold_in(own_key, axis), (), 0, shape[axis]) for axis in range(len(shape))]
    values = values.at[tuple(place)].set(low)
    longest = shape.index(max(shape))
    place[longest] = (place[longest] + 1) % shape[longest]
    return values.at[tuple(place)].set(largest)


def steps_of(stream_key, extent, cuts, low, largest):
    factor_of = 1.0
    for position, shards_of in cuts:
        steps = jax.random.uniform(jax.random.fold_in(jax.random.fold_in(stream_key, 6), position), (shards_of,), jnp.float32, low / len(cuts), largest / len(cuts))
        factor_of = factor_of * jnp.repeat(jnp.exp(steps), extent[position] // shards_of).reshape((-1,) + (1,) * (len(extent) - 1 - position))
    return factor_of


def normal_values(own_key, shape, deviation, bound, pieces=(), kind=jnp.bfloat16):
    loudness = steps_of(own_key, shape, pieces, -0.22, 0.18) if pieces else 1.0
    array = jax.random.normal(own_key, shape, jnp.float32) * deviation * loudness
    return jnp.minimum(jnp.maximum(array, -bound), bound).astype(kind)


def setup_inputs(seed: int = 0) -> dict:
    streams_of = jax.random.split(jax.random.key(seed), 11)
    queries = normal_values(streams_of[0], (SEQS, LEN, HQ * HD), 1.0, 6.0, ((0, 32), (1, 16)))
    keys = normal_values(streams_of[1], (SEQS, LEN, HK * HD), 1.0, 6.0, ((0, 32),))
    values = normal_values(streams_of[2], (SEQS, LEN, HK * HD), 1.0, 6.0, ((0, 32),))
    stream = normal_values(streams_of[3], (SEQS, LEN, D), 1.0, 6.0, ((0, 32), (2, 16)))
    out_proj = normal_values(streams_of[4], (HQ * HD, D), (HQ * HD) ** -0.5, 0.125, ((1, 16),))
    norm_gain = jnp.clip(1.0 + 0.18 * jax.random.normal(streams_of[5], (D,), jnp.float32), 0.1, 1.9)
    tag_proj = normal_values(streams_of[6], (D, TAGS), (8 * D) ** -0.5, 0.03125, ((0, 16),))
    direction = draw_direction(jax.random.fold_in(streams_of[10], 71), 0)
    starts = draw_starts(jax.random.fold_in(streams_of[10], 71), 0)
    tags = set_ends(jax.random.randint(streams_of[9], (SEQS, LEN), 0, TAGS), jax.random.fold_in(streams_of[9], 1), 0, TAGS - 1).astype(jnp.int32)
    return {"queries": queries, "keys": keys, "values": values, "stream": stream, "out_proj": out_proj, "norm_gain": norm_gain, "tag_proj": tag_proj, "direction": direction, "starts": starts, "tags": tags}


DAMP = 0.01
NORM_EPS = 1e-06
MEAN_EPS = 1e-06

def attend(query, key, value, start, offset):
    num_q = query.shape[0]
    num_k = key.shape[0]
    group = HQ // HK
    q_heads = query.reshape(num_q, HK, group, HD)
    k_heads = key.reshape(num_k, HK, HD)
    v_heads = value.reshape(num_k, HK, HD)
    scores = jnp.einsum('qgrd,kgd->grqk', q_heads.astype(jnp.float32), k_heads.astype(jnp.float32)) / jnp.sqrt(jnp.float32(HD))
    scores = 50.0 * jnp.tanh(scores / 50.0)
    q_pos = offset + jnp.arange(num_q, dtype=jnp.int32)
    k_pos = jnp.arange(num_k, dtype=jnp.int32)
    q_file = lax.optimization_barrier(jnp.sum((start[None, :] <= q_pos[:, None]).astype(jnp.int32), 1)) - 1
    k_file = lax.optimization_barrier(jnp.sum((start[None, :] <= k_pos[:, None]).astype(jnp.int32), 1)) - 1
    allowed = (q_file[:, None] == k_file[None, :]) & (k_pos[None, :] <= q_pos[:, None]) & (q_pos[:, None] - k_pos[None, :] < WINDOW)
    expo = jnp.where(allowed[None, None], jnp.exp(scores), 0.0)
    weights = (expo / lax.optimization_barrier(jnp.sum(expo, -1, keepdims=True))).astype(jnp.bfloat16)
    out = jnp.einsum('grqk,kgd->qgrd', weights.astype(jnp.float32), v_heads.astype(jnp.float32))
    return out.reshape(num_q, HQ * HD).astype(jnp.bfloat16)

def reference(queries, keys, values, stream, out_proj, norm_gain, tag_proj, direction, starts, tags):
    attn = lax.map(lambda item: attend(item[0], item[1], item[2], item[3], 0), (queries, keys, values, starts))
    flat = attn.reshape(-1, HQ * HD)
    h_all = stream.astype(jnp.float32).reshape(-1, D) + jnp.dot(flat, out_proj, preferred_element_type=jnp.float32)
    wide = tag_proj.astype(jnp.float32)
    tag_ids = jnp.arange(TAGS, dtype=jnp.int32)

    def token_loss(hh, target):
        sumsq = lax.optimization_barrier(jnp.sum(hh * hh, -1))
        rscale = (sumsq / D + NORM_EPS) ** (-0.5)
        zval = jnp.dot(hh * norm_gain, wide, precision=lax.Precision.HIGHEST)
        logits = 30.0 * jnp.tanh(rscale[:, None] * zval / 30.0)
        total = jnp.log(lax.optimization_barrier(jnp.sum(jnp.exp(logits), -1)))
        picked = lax.optimization_barrier(jnp.sum(jnp.where(target[:, None] == tag_ids[None, :], logits, 0.0), -1))
        return jnp.sum(total - picked)

    def curvature(hdot):

        def one(item):
            hh, hd, target = item
            grad_fn = jax.grad(lambda x: token_loss(x, target))
            return jax.jvp(grad_fn, (hh,), (hd,))[1]
        out = lax.map(one, (h_all.reshape(SEQS, LEN, D), hdot.reshape(SEQS, LEN, D), tags))
        return out.reshape(-1, D).astype(jnp.bfloat16)

    def product(u):
        hdot = jnp.dot(flat, u.astype(jnp.bfloat16), preferred_element_type=jnp.float32)
        gdot = curvature(hdot)
        return lax.dot_general(flat, gdot, (((0,), (0,)), ((), ())), preferred_element_type=jnp.float32)
    count = HQ * HD * D
    u = direction
    sigma = jnp.float32(1.0)
    for step in range(ITERS):
        hvp = product(u)
        if step == 0:
            sigma = 2.0 * jnp.sqrt((jnp.sum(hvp * hvp) / count + MEAN_EPS) / (jnp.sum(direction * direction) / count + MEAN_EPS))
        u = direction + (1.0 - DAMP) * u - hvp / sigma
    return u
```

```python
import jax
import jax.numpy as jnp
from jax import lax
from jax.sharding import Mesh, PartitionSpec as P

D = 3584
HD = 256
HQ = 8
HK = 4
TAGS = 128
WINDOW = 256
DAMP = 0.01
NORM_EPS = 1e-06
MEAN_EPS = 1e-06
ZL, X, Y, ZH, C = 8, 4, 4, 2, 2
BF = jnp.bfloat16
F32 = jnp.float32


def attend(query, key, value, start, offset):
    num_q = query.shape[0]
    num_k = key.shape[0]
    group = HQ // HK
    q_heads = query.reshape(num_q, HK, group, HD)
    k_heads = key.reshape(num_k, HK, HD)
    v_heads = value.reshape(num_k, HK, HD)
    scores = jnp.einsum(
        "qgrd,kgd->grqk", q_heads, k_heads, preferred_element_type=F32
    ) / jnp.sqrt(F32(HD))
    scores = 50.0 * jnp.tanh(scores / 50.0)
    q_pos = offset + jnp.arange(num_q, dtype=jnp.int32)
    k_pos = jnp.arange(num_k, dtype=jnp.int32)
    q_file = jnp.sum((start[None, :] <= q_pos[:, None]).astype(jnp.int32), 1) - 1
    k_file = jnp.sum((start[None, :] <= k_pos[:, None]).astype(jnp.int32), 1) - 1
    allowed = (
        (q_file[:, None] == k_file[None, :])
        & (k_pos[None, :] <= q_pos[:, None])
        & (q_pos[:, None] - k_pos[None, :] < WINDOW)
    )
    expo = jnp.where(allowed[None, None], jnp.exp(scores), 0.0)
    weights = (expo / jnp.sum(expo, -1, keepdims=True)).astype(BF)
    out = jnp.einsum("grqk,kgd->qgrd", weights, v_heads, preferred_element_type=F32)
    return out.reshape(num_q, HQ * HD).astype(BF)


def swap(x, axis):
    return lax.ppermute(x, axis, [(0, 1), (1, 0)])


def spread(x, axis, n):
    return lax.all_to_all(jnp.broadcast_to(x[None], (n,) + x.shape), axis, 0, 0, tiled=True)


def deal(x, axis):
    return lax.all_to_all(x, axis, 0, 0, tiled=True)


def paired(mine, theirs, axis):
    first = lax.axis_index(axis) == 0
    return jnp.stack([jnp.where(first, mine, theirs), jnp.where(first, theirs, mine)])


def dot(a, b):
    return jnp.dot(a, b, preferred_element_type=F32)


def split2(x):
    hi = x.astype(BF)
    return hi, (x - hi.astype(F32)).astype(BF)


def gather_rows(block, total):
    hi, lo = split2(total)
    mid, low = hi, lo
    row = jnp.concatenate([jnp.full((1, 112), mid, BF), jnp.full((1, 112), low, BF)], 1)
    load = jnp.concatenate([block.astype(BF), jnp.broadcast_to(row, (16, 224))], 0)
    by_zl = spread(load, "zl", ZL)
    by_all = spread(by_zl, "x", X)
    rows = by_all[:, :, :64].transpose(1, 0, 2, 3).reshape(2048, 224)
    sums = by_all[:, :, 64].astype(F32)
    return rows, jnp.sum(sums[..., 0] + sums[..., 112])


def scatter_rows(product):
    by_x = product.astype(BF).reshape(ZL, X, 64, 224).transpose(1, 0, 2, 3)
    part = jnp.sum(deal(by_x, "x").astype(F32), 0)
    return jnp.sum(deal(part.astype(BF), "zl").astype(F32), 0)


def tokens_sum(load):
    part = jnp.sum(deal(load, ("c", "y")), 0)
    return part + swap(part, "zh")


def local(queries, keys, values, stream, out_proj, norm_gain, tag_proj, direction, starts, tags):
    core = lax.axis_index("c")
    ypos = lax.axis_index("y")
    mp_index = (ypos * ZH + lax.axis_index("zh")) * C + core
    count = HQ * HD * D
    u0, early_norm = gather_rows(direction, jnp.sum(direction * direction))

    mine = attend(queries[0], keys[0], values[0], starts[0], mp_index * 32)
    pair = paired(mine, swap(mine, "zh"), "zh").reshape(64, 2048)
    half = spread(pair, "y", Y).reshape(256, 2048)
    attn = paired(half, swap(half, "c"), "c").reshape(512, 2048)
    toks = stream[0].reshape(Y, ZH, C, 32, 224).transpose(2, 0, 1, 3, 4).reshape(512, 224)
    tag_own = tags[0].reshape(Y, ZH, C, 32).transpose(2, 0, 1, 3).reshape(C * Y, 64)[core * Y + ypos]

    wide = tag_proj.astype(F32)
    gained = norm_gain[:, None] * wide

    def sums(h, hd):
        return jnp.sum(h * hd, -1).reshape(8, 1, 64)

    def tag_scores(hd):
        return jnp.dot(hd, gained, precision=lax.Precision.HIGHEST).reshape(8, 64, TAGS)

    h_loc = toks.astype(F32) + dot(attn, out_proj)
    hdot0 = dot(attn, u0)
    load = jnp.concatenate(
        [
            tag_scores(h_loc),
            tag_scores(hdot0),
            jnp.pad(jnp.concatenate([sums(h_loc, h_loc), sums(h_loc, hdot0)], 2), ((0, 0), (0, 7), (0, 0))),
        ],
        1,
    )
    total = tokens_sum(load)
    zval, zdot0 = total[:64], total[64:128]
    sumsq, along0 = total[128, :64], total[128, 64:]

    rscale = (sumsq / D + NORM_EPS) ** (-0.5)
    tanh_val = jnp.tanh(rscale[:, None] * zval / 30.0)
    slope = 1.0 - tanh_val * tanh_val
    expo = jnp.exp(30.0 * tanh_val)
    probs = expo / jnp.sum(expo, -1, keepdims=True)
    onehot = (tag_own[:, None] == jnp.arange(TAGS, dtype=jnp.int32)[None, :]).astype(F32)
    dlogit = probs - onehot
    wgrad = dlogit * slope
    rho = jnp.sum(wgrad * zval, -1)
    cube = rscale**3 / D

    def backward(along, zdot, hdot):
        rdot = -cube * along
        mdot = rdot[:, None] * zval + rscale[:, None] * zdot
        ldot = slope * mdot
        pdot = probs * (ldot - jnp.sum(probs * ldot, -1, keepdims=True))
        wdot = pdot * slope - dlogit * 2.0 * tanh_val * slope * mdot / 30.0
        rhodot = jnp.sum(wdot * zval + wgrad * zdot, -1)
        mixed = rdot[:, None] * wgrad + rscale[:, None] * wdot
        coeff = rhodot * cube + 3.0 * rho * rscale * rscale * rdot / D
        row = jnp.concatenate([coeff, rho * cube])[None]
        out = spread(jnp.concatenate([mixed, jnp.pad(row, ((0, 7), (0, 0)))], 0), ("c", "y"), 8)
        mixed_all = out[:, :64].reshape(512, TAGS)
        coeff_all = out[:, 64, :64].reshape(512, 1)
        rc_all = out[:, 64, 64:].reshape(512, 1)
        back = jnp.dot(mixed_all, gained.T, precision=lax.Precision.HIGHEST)
        gdot = (back - coeff_all * h_loc - rc_all * hdot).astype(BF)
        return scatter_rows(
            lax.dot_general(attn, gdot, (((0,), (0,)), ((), ())), preferred_element_type=F32)
        )

    rows0 = backward(along0, zdot0, hdot0)
    full0, row_sq = gather_rows(rows0, jnp.sum(rows0 * rows0))
    moved = dot(attn, full0)
    lane = jnp.arange(64)[None, None, :]
    scalars = jnp.where(lane == 0, row_sq, jnp.where(lane == 1, early_norm, 0.0))
    load = jnp.concatenate(
        [
            tag_scores(moved),
            jnp.pad(
                jnp.concatenate([sums(h_loc, moved), jnp.broadcast_to(scalars, (8, 1, 64))], 2),
                ((0, 0), (0, 7), (0, 0)),
            ),
        ],
        1,
    )
    total = tokens_sum(load)
    product_sq, norm_sq = total[64, 64], total[64, 65]
    sigma = 2.0 * jnp.sqrt((product_sq / count + MEAN_EPS) / (norm_sq / count + MEAN_EPS))
    inv = 1.0 / sigma
    keep = 2.0 - DAMP
    rows1 = backward(
        keep * along0 - total[64, :64] * inv,
        keep * zdot0 - total[:64] * inv,
        keep * hdot0 - moved * inv,
    )
    damp = 1.0 - DAMP
    return (1.0 + damp * keep) * direction - (damp * rows0 + rows1) * inv


def solution(mesh):
    fine = Mesh(mesh.devices.reshape(ZL, X, Y, ZH, C), ("zl", "x", "y", "zh", "c"))
    dp, mp = ("zl", "x"), ("y", "zh", "c")
    return jax.shard_map(
        local,
        mesh=fine,
        in_specs=(
            P(dp, mp, None),
            P(dp, None, None),
            P(dp, None, None),
            P(dp, None, mp),
            P(None, mp),
            P(mp),
            P(mp, None),
            P(dp, mp),
            P(dp, None),
            P(dp, None),
        ),
        out_specs=P(dp, mp),
        check_vma=False,
    )
```

```python
import jax
import jax.numpy as jnp
from jax import lax
from jax.sharding import Mesh, PartitionSpec as P

D = 3584
HD = 256
HQ = 8
HK = 4
TAGS = 128
WINDOW = 256
DAMP = 0.01
NORM_EPS = 1e-06
MEAN_EPS = 1e-06
ZL, X, Y, ZH, C = 8, 4, 4, 2, 2
BF = jnp.bfloat16
F32 = jnp.float32


def attend(query, key, value, start, offset):
    num_q = query.shape[0]
    num_k = key.shape[0]
    group = HQ // HK
    q_heads = query.reshape(num_q, HK, group, HD)
    k_heads = key.reshape(num_k, HK, HD)
    v_heads = value.reshape(num_k, HK, HD)
    scores = jnp.einsum(
        "qgrd,kgd->grqk", q_heads, k_heads, preferred_element_type=F32
    ) / jnp.sqrt(F32(HD))
    scores = 50.0 * jnp.tanh(scores / 50.0)
    q_pos = offset + jnp.arange(num_q, dtype=jnp.int32)
    k_pos = jnp.arange(num_k, dtype=jnp.int32)
    q_file = jnp.sum((start[None, :] <= q_pos[:, None]).astype(jnp.int32), 1) - 1
    k_file = jnp.sum((start[None, :] <= k_pos[:, None]).astype(jnp.int32), 1) - 1
    allowed = (
        (q_file[:, None] == k_file[None, :])
        & (k_pos[None, :] <= q_pos[:, None])
        & (q_pos[:, None] - k_pos[None, :] < WINDOW)
    )
    expo = jnp.where(allowed[None, None], jnp.exp(scores), 0.0)
    weights = (expo / jnp.sum(expo, -1, keepdims=True)).astype(BF)
    out = jnp.einsum("grqk,kgd->qgrd", weights, v_heads, preferred_element_type=F32)
    return out.reshape(num_q, HQ * HD).astype(BF)


def swap(x, axis):
    return lax.ppermute(x, axis, [(0, 1), (1, 0)])


def spread(x, axis, n):
    return lax.all_to_all(jnp.broadcast_to(x[None], (n,) + x.shape), axis, 0, 0, tiled=True)


def deal(x, axis):
    return lax.all_to_all(x, axis, 0, 0, tiled=True)


def paired(mine, theirs, axis):
    first = lax.axis_index(axis) == 0
    return jnp.stack([jnp.where(first, mine, theirs), jnp.where(first, theirs, mine)])


def dot(a, b):
    return jnp.dot(a, b, preferred_element_type=F32)


def split2(x):
    hi = x.astype(BF)
    return hi, (x - hi.astype(F32)).astype(BF)


def row_load(block):
    hi, lo = split2(jnp.sum(block * block, -1, keepdims=True))
    return jnp.concatenate([block.astype(BF), hi, lo, jnp.zeros((64, 30), BF)], 1)


def whole_rows(by_all):
    rows = by_all[..., :224].transpose(1, 0, 2, 3).reshape(2048, 224)
    return rows, jnp.sum(by_all[..., 224:226].astype(F32))


def scatter_rows(product):
    by_x = product.astype(BF).reshape(ZL, X, 64, 224).transpose(1, 0, 2, 3)
    part = jnp.sum(deal(by_x, "x").astype(F32), 0)
    return jnp.sum(deal(part.astype(BF), "zl").astype(F32), 0)


def tokens_sum(load):
    part = jnp.sum(deal(load, ("c", "y")), 0)
    return part + swap(part, "zh")


def local(queries, keys, values, stream, out_proj, norm_gain, tag_proj, direction, starts, tags):
    core = lax.axis_index("c")
    ypos = lax.axis_index("y")
    mp_index = (ypos * ZH + lax.axis_index("zh")) * C + core
    count = HQ * HD * D
    by_zl = spread(row_load(direction), "zl", ZL)
    mine = attend(queries[0], keys[0], values[0], starts[0], mp_index * 32)
    mine, by_zl = lax.optimization_barrier((mine, by_zl))
    theirs, by_all = lax.optimization_barrier((swap(mine, "zh"), spread(by_zl, "x", X)))
    u0, early_norm = whole_rows(by_all)
    pair = paired(mine, theirs, "zh").reshape(64, 2048)
    half = spread(pair, "y", Y).reshape(256, 2048)
    attn = paired(half, swap(half, "c"), "c").reshape(512, 2048)
    toks = stream[0].reshape(Y, ZH, C, 32, 224).transpose(2, 0, 1, 3, 4).reshape(512, 224)
    tag_own = tags[0].reshape(Y, ZH, C, 32).transpose(2, 0, 1, 3).reshape(C * Y, 64)[core * Y + ypos]

    wide = tag_proj.astype(F32)
    gained = norm_gain[:, None] * wide

    def sums(h, hd):
        return jnp.sum(h * hd, -1).reshape(8, 1, 64)

    def tag_scores(hd):
        return jnp.dot(hd, gained, precision=lax.Precision.HIGHEST).reshape(8, 64, TAGS)

    h_loc = toks.astype(F32) + dot(attn, out_proj)
    hdot0 = dot(attn, u0)
    load = jnp.concatenate(
        [
            tag_scores(h_loc),
            tag_scores(hdot0),
            jnp.pad(jnp.concatenate([sums(h_loc, h_loc), sums(h_loc, hdot0)], 2), ((0, 0), (0, 7), (0, 0))),
        ],
        1,
    )
    total = tokens_sum(load)
    zval, zdot0 = total[:64], total[64:128]
    sumsq, along0 = total[128, :64], total[128, 64:]

    rscale = (sumsq / D + NORM_EPS) ** (-0.5)
    tanh_val = jnp.tanh(rscale[:, None] * zval / 30.0)
    slope = 1.0 - tanh_val * tanh_val
    expo = jnp.exp(30.0 * tanh_val)
    probs = expo / jnp.sum(expo, -1, keepdims=True)
    onehot = (tag_own[:, None] == jnp.arange(TAGS, dtype=jnp.int32)[None, :]).astype(F32)
    dlogit = probs - onehot
    wgrad = dlogit * slope
    rho = jnp.sum(wgrad * zval, -1)
    cube = rscale**3 / D

    def backward(along, zdot, hdot):
        rdot = -cube * along
        mdot = rdot[:, None] * zval + rscale[:, None] * zdot
        ldot = slope * mdot
        pdot = probs * (ldot - jnp.sum(probs * ldot, -1, keepdims=True))
        wdot = pdot * slope - dlogit * 2.0 * tanh_val * slope * mdot / 30.0
        rhodot = jnp.sum(wdot * zval + wgrad * zdot, -1)
        mixed = rdot[:, None] * wgrad + rscale[:, None] * wdot
        coeff = rhodot * cube + 3.0 * rho * rscale * rscale * rdot / D
        row = jnp.concatenate([coeff, rho * cube])[None]
        out = spread(jnp.concatenate([mixed, jnp.pad(row, ((0, 7), (0, 0)))], 0), ("c", "y"), 8)
        mixed_all = out[:, :64].reshape(512, TAGS)
        coeff_all = out[:, 64, :64].reshape(512, 1)
        rc_all = out[:, 64, 64:].reshape(512, 1)
        back = jnp.dot(mixed_all, gained.T, precision=lax.Precision.HIGHEST)
        gdot = (back - coeff_all * h_loc - rc_all * hdot).astype(BF)
        return scatter_rows(
            lax.dot_general(attn, gdot, (((0,), (0,)), ((), ())), preferred_element_type=F32)
        )

    rows0 = backward(along0, zdot0, hdot0)
    full0, row_sq = whole_rows(spread(spread(row_load(rows0), "zl", ZL), "x", X))
    moved = dot(attn, full0)
    lane = jnp.arange(64)[None, None, :]
    scalars = jnp.where(lane == 0, row_sq, jnp.where(lane == 1, early_norm, 0.0))
    load = jnp.concatenate(
        [
            tag_scores(moved),
            jnp.pad(
                jnp.concatenate([sums(h_loc, moved), jnp.broadcast_to(scalars, (8, 1, 64))], 2),
                ((0, 0), (0, 7), (0, 0)),
            ),
        ],
        1,
    )
    total = tokens_sum(load)
    product_sq, norm_sq = total[64, 64], total[64, 65]
    sigma = 2.0 * jnp.sqrt((product_sq / count + MEAN_EPS) / (norm_sq / count + MEAN_EPS))
    inv = 1.0 / sigma
    keep = 2.0 - DAMP
    rows1 = backward(
        keep * along0 - total[64, :64] * inv,
        keep * zdot0 - total[:64] * inv,
        keep * hdot0 - moved * inv,
    )
    damp = 1.0 - DAMP
    return (1.0 + damp * keep) * direction - (damp * rows0 + rows1) * inv


def solution(mesh):
    fine = Mesh(mesh.devices.reshape(ZL, X, Y, ZH, C), ("zl", "x", "y", "zh", "c"))
    dp, mp = ("zl", "x"), ("y", "zh", "c")
    return jax.shard_map(
        local,
        mesh=fine,
        in_specs=(
            P(dp, mp, None),
            P(dp, None, None),
            P(dp, None, None),
            P(dp, None, mp),
            P(None, mp),
            P(mp),
            P(mp, None),
            P(dp, mp),
            P(dp, None),
            P(dp, None),
        ),
        out_specs=P(dp, mp),
        check_vma=False,
    )
```

```python
import functools

import jax
import jax.numpy as jnp
from jax import lax
from jax.experimental import pallas as pl
from jax.experimental.pallas import tpu as pltpu
from jax.sharding import Mesh, PartitionSpec as P

D = 3584
HD = 256
HQ = 8
HK = 4
TAGS = 128
WINDOW = 256
DAMP = 0.01
KEEP = 2.0 - DAMP
NORM_EPS = 1e-06
MEAN_EPS = 1e-06
ZL, X, Y, ZH, C = 8, 4, 4, 2, 2
ROWS = HQ * HD
COLS = 224
WIDE = 256
COUNT = HQ * HD * D
SPAN = 288
BF = jnp.bfloat16
F32 = jnp.float32
CONTRACT0 = (((0,), (0,)), ((), ()))
CONTRACT1 = (((1,), (1,)), ((), ()))


def call(kernel, out_shape, *args, smem=0):
    specs = [pl.BlockSpec(memory_space=pltpu.SMEM)] * smem
    specs += [pl.BlockSpec(memory_space=pltpu.VMEM)] * (len(args) - smem)
    scratch = kernel.keywords.pop("scratch", ()) if isinstance(kernel, functools.partial) else ()
    many = isinstance(out_shape, (tuple, list))
    vmem = pl.BlockSpec(memory_space=pltpu.VMEM)
    return pl.pallas_call(
        kernel,
        out_shape=out_shape,
        in_specs=specs,
        out_specs=[vmem] * len(out_shape) if many else vmem,
        scratch_shapes=scratch,
        compiler_params=pltpu.CompilerParams(vmem_limit_bytes=40 * 2**20),
    )(*args)


def shape(*dims, dtype=F32):
    return jax.ShapeDtypeStruct(dims, dtype)


def dot(a, b):
    return jnp.dot(a, b, preferred_element_type=F32)


def three(x):
    a = x.astype(BF)
    rest = x - a.astype(F32)
    b = rest.astype(BF)
    return a, b, (rest - b.astype(F32)).astype(BF)


def attend_kernel(place, starts, q_ref, k_ref, v_ref, o_ref):
    offset = place[1]
    first = pl.multiple_of(jnp.maximum(offset - WINDOW, 0), 32)
    q_row = lax.broadcasted_iota(jnp.int32, (64, 1), 0)
    q_pos = offset + jnp.where(q_row < 32, q_row, q_row - 32)
    k_pos = first + lax.broadcasted_iota(jnp.int32, (1, SPAN), 1)
    q_file = jnp.zeros((64, 1), jnp.int32)
    k_file = jnp.zeros((1, SPAN), jnp.int32)
    for f in range(4):
        q_file += jnp.where(starts[0, f] <= q_pos, 1, 0)
        k_file += jnp.where(starts[0, f] <= k_pos, 1, 0)
    allowed = (q_file == k_file) & (k_pos <= q_pos) & (q_pos - k_pos < WINDOW)
    for g in range(HK):
        q = jnp.concatenate(
            [q_ref[:, (2 * g + r) * HD : (2 * g + r + 1) * HD] for r in range(2)], 0
        )
        cols = slice(g * HD, (g + 1) * HD)
        scores = lax.dot_general(
            q, k_ref[pl.ds(first, SPAN), cols], CONTRACT1, preferred_element_type=F32
        )
        scores = 50.0 * jnp.tanh(scores * (1.0 / 16.0) / 50.0)
        expo = jnp.where(allowed, jnp.exp(scores), 0.0)
        weights = (expo / jnp.sum(expo, -1, keepdims=True)).astype(BF)
        out = dot(weights, v_ref[pl.ds(first, SPAN), cols]).astype(BF)
        for r in range(2):
            o_ref[:, (2 * g + r) * HD : (2 * g + r + 1) * HD] = out[r * 32 : r * 32 + 32]


def row_block(block):
    total = jnp.sum(block * block, -1, keepdims=True)
    hi = total.astype(BF)
    lo = (total - hi.astype(F32)).astype(BF)
    lane = lax.broadcasted_iota(jnp.int32, (64, WIDE - COLS), 1)
    tail = jnp.where(lane == 0, hi.astype(F32), jnp.where(lane == 1, lo.astype(F32), 0.0))
    return jnp.concatenate([block, tail], 1).astype(BF)


def direction_kernel(d_ref, o_ref):
    load = row_block(d_ref[...])
    for i in range(ZL):
        o_ref[i] = load


def sum_x_kernel(i_ref, o_ref):
    total = i_ref[0].astype(F32)
    for i in range(1, X):
        total += i_ref[i].astype(F32)
    o_ref[...] = total.astype(BF)


def sum_zl(i_ref):
    total = i_ref[0].astype(F32)
    for i in range(1, ZL):
        total += i_ref[i].astype(F32)
    return total


def sum_rows_kernel(i_ref, rows_ref, o_ref):
    total = sum_zl(i_ref)
    rows_ref[...] = total
    load = row_block(total)
    for i in range(ZL):
        o_ref[i] = load


def last_kernel(i_ref, rows_ref, d_ref, inv_ref, o_ref):
    damp = 1.0 - DAMP
    inv = inv_ref[0:1, 0:1]
    o_ref[...] = (1.0 + damp * KEEP) * d_ref[...] - (
        damp * rows_ref[...] + sum_zl(i_ref)
    ) * inv


def natural_rows(u_ref, rows_ref):
    for zl in range(ZL):
        for x in range(X):
            at = (zl * X + x) * 64
            rows_ref[at : at + 64, :] = u_ref[x, zl]
    return jnp.sum(rows_ref[:, COLS : COLS + 2].astype(F32))


def scores_of(x, gain, tag_ref):
    return sum(dot(part, tag_ref[...]) for part in three(x * gain))


def put_sums(load_ref, block, row, sums, scalar):
    lane = lax.broadcasted_iota(jnp.int32, (256, 128), 1)
    table = jnp.full((256, 128), scalar, F32)
    for i, s in enumerate(sums):
        table = jnp.where(lane == i, s, table)
    table = table.T
    for i in range(Y):
        load_ref[block + i, row : row + 8, 0:64] = table[0:8, i * 64 : (i + 1) * 64]
        load_ref[block + i, row : row + 8, 64:128] = table[0:8, 0:64]


def first_kernel(
    place, own_ref, oth_ref, u_ref, proj_ref, s_ref, gain_ref, tag_ref, h_ref, hd_ref, load_ref, rows_ref
):
    norm = natural_rows(u_ref, rows_ref)
    gain = gain_ref[...]
    for half, a_ref in enumerate((own_ref, oth_ref)):
        c = place[0] if half == 0 else 1 - place[0]
        at = pl.multiple_of(c * 256, 256)
        a = a_ref[...].reshape(256, ROWS)
        s = jnp.concatenate(
            [s_ref[y, zh, pl.ds(c, 1)][0] for y in range(Y) for zh in range(ZH)], 0
        )
        h = s.astype(F32) + dot(a, proj_ref[...])
        hd = dot(a, rows_ref[...])[:, :COLS]
        h_ref[pl.ds(at, 256), :] = h
        hd_ref[pl.ds(at, 256), :] = hd
        z = scores_of(h, gain, tag_ref)
        zd = scores_of(hd, gain, tag_ref)
        for i in range(Y):
            load_ref[c * Y + i, 0:64, :] = z[i * 64 : i * 64 + 64]
            load_ref[c * Y + i, 64:128, :] = zd[i * 64 : i * 64 + 64]
        sums = (jnp.sum(h * h, -1, keepdims=True), jnp.sum(h * hd, -1, keepdims=True))
        put_sums(load_ref, c * Y, 128, sums, norm)


def moved_kernel(place, own_ref, oth_ref, u_ref, h_ref, gain_ref, tag_ref, mv_ref, load_ref, rows_ref):
    norm = natural_rows(u_ref, rows_ref)
    gain = gain_ref[...]
    for half, a_ref in enumerate((own_ref, oth_ref)):
        c = place[0] if half == 0 else 1 - place[0]
        at = pl.multiple_of(c * 256, 256)
        moved = dot(a_ref[...].reshape(256, ROWS), rows_ref[...])[:, :COLS]
        mv_ref[pl.ds(at, 256), :] = moved
        z = scores_of(moved, gain, tag_ref)
        for i in range(Y):
            load_ref[c * Y + i, 0:64, :] = z[i * 64 : i * 64 + 64]
        sums = (jnp.sum(h_ref[pl.ds(at, 256), :] * moved, -1, keepdims=True),)
        put_sums(load_ref, c * Y, 64, sums, norm)


def sum_parts_kernel(i_ref, o_ref):
    total = i_ref[0]
    for i in range(1, 8):
        total += i_ref[i]
    o_ref[...] = total


def columns_of(rows):
    return jnp.concatenate([rows, jnp.zeros((120, 128), F32)], 0).T[:64]


def backward(zval, sumsq, tags, along, zdot, o_ref):
    rscale = lax.rsqrt(sumsq / D + NORM_EPS)
    tanh_val = jnp.tanh(rscale * zval / 30.0)
    slope = 1.0 - tanh_val * tanh_val
    expo = jnp.exp(30.0 * tanh_val)
    probs = expo / jnp.sum(expo, -1, keepdims=True)
    onehot = (tags == lax.broadcasted_iota(jnp.int32, (64, TAGS), 1)).astype(F32)
    dlogit = probs - onehot
    wgrad = dlogit * slope
    rho = jnp.sum(wgrad * zval, -1, keepdims=True)
    cube = rscale * rscale * rscale / D
    rdot = -cube * along
    mdot = rdot * zval + rscale * zdot
    ldot = slope * mdot
    pdot = probs * (ldot - jnp.sum(probs * ldot, -1, keepdims=True))
    wdot = pdot * slope - dlogit * 2.0 * tanh_val * slope * mdot / 30.0
    rhodot = jnp.sum(wdot * zval + wgrad * zdot, -1, keepdims=True)
    mixed = rdot * wgrad + rscale * wdot
    coeff = rhodot * cube + 3.0 * rho * rscale * rscale * rdot / D
    lane = lax.broadcasted_iota(jnp.int32, (64, 128), 1)
    table = jnp.where(lane == 0, coeff, jnp.where(lane == 1, rho * cube, 0.0))
    tail = jnp.concatenate([table, jnp.zeros((64, 128), F32)], 0).T[0:8]
    for i in range(8):
        o_ref[i, 0:64, :] = mixed
        o_ref[i, 64:72, :] = tail


def tokens0_kernel(mine_ref, their_ref, tag_ref, total_ref, o_ref):
    total_ref[...] = mine_ref[...] + their_ref[...]
    columns = columns_of(total_ref[128:136, :])
    backward(
        total_ref[0:64, :], columns[:, 0:1], tag_ref[...], columns[:, 1:2], total_ref[64:128, :], o_ref
    )


def tokens1_kernel(mine_ref, their_ref, total_ref, tag_ref, o_ref, inv_ref):
    moved = mine_ref[...] + their_ref[...]
    product_sq = moved[65:66, 0:1]
    norm_sq = total_ref[130:131, 0:1]
    sigma = 2.0 * jnp.sqrt((product_sq / COUNT + MEAN_EPS) / (norm_sq / COUNT + MEAN_EPS))
    inv = 1.0 / sigma
    inv_ref[...] = jnp.broadcast_to(inv, (8, 128))
    columns0 = columns_of(total_ref[128:136, :])
    columns1 = columns_of(moved[64:72])
    along = KEEP * columns0[:, 1:2] - columns1[:, 0:1] * inv
    zdot = KEEP * total_ref[64:128, :] - moved[0:64] * inv
    backward(total_ref[0:64, :], columns0[:, 0:1], tag_ref[...], along, zdot, o_ref)


def product_kernel(second, place, m_ref, h_ref, hd_ref, *rest):
    if second:
        mv_ref, inv_ref, *rest = rest
    own_ref, oth_ref, gain_ref, tag_ref, o_ref, g_ref = rest
    gain = gain_ref[...]
    for c in range(C):
        span = slice(c * 256, c * 256 + 256)
        mixed = jnp.concatenate([m_ref[c * Y + i, 0:64, :] for i in range(Y)], 0)
        back = sum(
            lax.dot_general(part, tag_ref[...], CONTRACT1, preferred_element_type=F32)
            for part in three(mixed)
        )
        columns = jnp.concatenate([columns_of(m_ref[c * Y + i, 64:72, :]) for i in range(Y)], 0)
        hd = hd_ref[span, :]
        if second:
            hd = KEEP * hd - mv_ref[span, :] * inv_ref[0:1, 0:1]
        g = back * gain - columns[:, 0:1] * h_ref[span, :] - columns[:, 1:2] * hd
        g_ref[span, :] = g.astype(BF)
    own_at = pl.multiple_of(place[0] * 256, 256)
    oth_at = pl.multiple_of((1 - place[0]) * 256, 256)
    g_own = g_ref[pl.ds(own_at, 256), :]
    g_oth = g_ref[pl.ds(oth_at, 256), :]
    for zl in range(ZL):
        cols = slice(zl * 256, zl * 256 + 256)
        part = lax.dot_general(
            own_ref[:, :, cols].reshape(256, 256), g_own, CONTRACT0, preferred_element_type=F32
        ) + lax.dot_general(
            oth_ref[:, :, cols].reshape(256, 256), g_oth, CONTRACT0, preferred_element_type=F32
        )
        for x in range(X):
            o_ref[x, zl] = part[x * 64 : x * 64 + 64].astype(BF)


def swap(x, axis):
    return lax.ppermute(x, axis, [(0, 1), (1, 0)])


def deal(x, axis):
    return lax.all_to_all(x, axis, 0, 0, tiled=True)


def spread(x, axis, n):
    return deal(jnp.broadcast_to(x[None], (n,) + x.shape), axis)


def local(queries, keys, values, stream, out_proj, norm_gain, tag_proj, direction, starts, tags):
    core = lax.axis_index("c")
    ypos = lax.axis_index("y")
    zhpos = lax.axis_index("zh")
    place = jnp.stack([core, ((ypos * ZH + zhpos) * C + core) * 32]).astype(jnp.int32)
    own_tags = tags[0].reshape(Y, ZH, C, 32).transpose(2, 0, 1, 3).reshape(C * Y, 64)[core * Y + ypos]
    own_tags = own_tags[:, None]
    toks = stream[0].reshape(Y, ZH, C, 32, COLS)
    gain = norm_gain[None]

    by_zl = deal(call(direction_kernel, shape(ZL, 64, WIDE, dtype=BF), direction), "zl")
    mine = call(
        attend_kernel, shape(32, ROWS, dtype=BF), place, starts, queries[0], keys[0], values[0], smem=2
    )
    mine, by_zl = lax.optimization_barrier((mine, by_zl))
    theirs, u0 = lax.optimization_barrier(
        (swap(mine, "zh"), spread(by_zl.reshape(ZL * 64, WIDE), "x", X).reshape(X, ZL, 64, WIDE))
    )
    low = zhpos == 0
    pair = jnp.stack([jnp.where(low, mine, theirs), jnp.where(low, theirs, mine)])
    own = spread(pair.reshape(64, ROWS), "y", Y)
    other = swap(own, "c")

    def product(second, *args):
        sent = call(
            functools.partial(product_kernel, second, scratch=[pltpu.VMEM((512, COLS), BF)]),
            shape(X, ZL, 64, COLS, dtype=BF),
            place,
            *args,
            own,
            other,
            gain,
            tag_proj,
            smem=1,
        )
        part = call(sum_x_kernel, shape(ZL, 64, COLS, dtype=BF), deal(sent, "x"))
        return deal(part, "zl")

    def token_sum(load, kernel, outs, *args):
        part = call(sum_parts_kernel, shape(load.shape[1], 128), deal(load, ("c", "y")))
        return call(kernel, outs, part, swap(part, "zh"), *args, own_tags)

    rows_scratch = [pltpu.VMEM((ROWS, WIDE), BF)]
    h_loc, hdot0, load = call(
        functools.partial(first_kernel, scratch=rows_scratch),
        (shape(512, COLS), shape(512, COLS), shape(8, 136, 128)),
        place,
        own,
        other,
        u0,
        out_proj,
        toks,
        gain,
        tag_proj,
        smem=1,
    )
    total, mixed = token_sum(load, tokens0_kernel, (shape(136, 128), shape(8, 72, 128)))
    rows0, sent = call(
        sum_rows_kernel,
        (shape(64, COLS), shape(ZL, 64, WIDE, dtype=BF)),
        product(False, deal(mixed, ("c", "y")), h_loc, hdot0),
    )
    full0 = spread(deal(sent, "zl").reshape(ZL * 64, WIDE), "x", X).reshape(X, ZL, 64, WIDE)
    moved, load = call(
        functools.partial(moved_kernel, scratch=rows_scratch),
        (shape(512, COLS), shape(8, 72, 128)),
        place,
        own,
        other,
        full0,
        h_loc,
        gain,
        tag_proj,
        smem=1,
    )
    mixed, inv = token_sum(load, tokens1_kernel, (shape(8, 72, 128), shape(8, 128)), total)
    arrived = product(True, deal(mixed, ("c", "y")), h_loc, hdot0, moved, inv)
    return call(last_kernel, shape(64, COLS), arrived, rows0, direction, inv)


def solution(mesh):
    fine = Mesh(mesh.devices.reshape(ZL, X, Y, ZH, C), ("zl", "x", "y", "zh", "c"))
    dp, mp = ("zl", "x"), ("y", "zh", "c")
    return jax.shard_map(
        local,
        mesh=fine,
        in_specs=(
            P(dp, mp, None),
            P(dp, None, None),
            P(dp, None, None),
            P(dp, None, mp),
            P(None, mp),
            P(mp),
            P(mp, None),
            P(dp, mp),
            P(dp, None),
            P(dp, None),
        ),
        out_specs=P(dp, mp),
        check_vma=False,
    )
```

```python
import functools

import jax
import jax.numpy as jnp
from jax import lax
from jax.experimental import pallas as pl
from jax.experimental.pallas import tpu as pltpu
from jax.sharding import Mesh, PartitionSpec as P

D = 3584
HD = 256
HQ = 8
HK = 4
TAGS = 128
WINDOW = 256
DAMP = 0.01
KEEP = 2.0 - DAMP
NORM_EPS = 1e-06
MEAN_EPS = 1e-06
ZL, X, Y, ZH, C = 8, 4, 4, 2, 2
ROWS = HQ * HD
COLS = 224
WIDE = 256
COUNT = HQ * HD * D
SPAN = 288
BF = jnp.bfloat16
F32 = jnp.float32
CONTRACT0 = (((0,), (0,)), ((), ()))
CONTRACT1 = (((1,), (1,)), ((), ()))


def call(kernel, out_shape, *args, smem=0, far=0):
    specs = [pl.BlockSpec(memory_space=pltpu.SMEM)] * smem
    specs += [pl.BlockSpec(memory_space=pl.ANY)] * far
    specs += [pl.BlockSpec(memory_space=pltpu.VMEM)] * (len(args) - smem - far)
    scratch = kernel.keywords.pop("scratch", ()) if isinstance(kernel, functools.partial) else ()
    many = isinstance(out_shape, (tuple, list))
    vmem = pl.BlockSpec(memory_space=pltpu.VMEM)
    return pl.pallas_call(
        kernel,
        out_shape=out_shape,
        in_specs=specs,
        out_specs=[vmem] * len(out_shape) if many else vmem,
        scratch_shapes=scratch,
        compiler_params=pltpu.CompilerParams(vmem_limit_bytes=40 * 2**20),
    )(*args)


def shape(*dims, dtype=F32):
    return jax.ShapeDtypeStruct(dims, dtype)


def dot(a, b):
    return jnp.dot(a, b, preferred_element_type=F32)


def three(x):
    a = x.astype(BF)
    rest = x - a.astype(F32)
    b = rest.astype(BF)
    return a, b, (rest - b.astype(F32)).astype(BF)


def attend_kernel(place, starts, q_ref, k_ref, v_ref, o_ref):
    offset = place[1]
    first = pl.multiple_of(jnp.maximum(offset - WINDOW, 0), 32)
    q_row = lax.broadcasted_iota(jnp.int32, (64, 1), 0)
    q_pos = offset + jnp.where(q_row < 32, q_row, q_row - 32)
    k_pos = first + lax.broadcasted_iota(jnp.int32, (1, SPAN), 1)
    q_file = jnp.zeros((64, 1), jnp.int32)
    k_file = jnp.zeros((1, SPAN), jnp.int32)
    for f in range(4):
        q_file += jnp.where(starts[0, f] <= q_pos, 1, 0)
        k_file += jnp.where(starts[0, f] <= k_pos, 1, 0)
    allowed = (q_file == k_file) & (k_pos <= q_pos) & (q_pos - k_pos < WINDOW)
    for g in range(HK):
        q = jnp.concatenate(
            [q_ref[:, (2 * g + r) * HD : (2 * g + r + 1) * HD] for r in range(2)], 0
        )
        cols = slice(g * HD, (g + 1) * HD)
        scores = lax.dot_general(
            q, k_ref[pl.ds(first, SPAN), cols], CONTRACT1, preferred_element_type=F32
        )
        scores = 50.0 * jnp.tanh(scores * (1.0 / 16.0) / 50.0)
        expo = jnp.where(allowed, jnp.exp(scores), 0.0)
        weights = (expo / jnp.sum(expo, -1, keepdims=True)).astype(BF)
        out = dot(weights, v_ref[pl.ds(first, SPAN), cols]).astype(BF)
        for r in range(2):
            o_ref[:, (2 * g + r) * HD : (2 * g + r + 1) * HD] = out[r * 32 : r * 32 + 32]


def row_block(block):
    total = jnp.sum(block * block, -1, keepdims=True)
    hi = total.astype(BF)
    lo = (total - hi.astype(F32)).astype(BF)
    lane = lax.broadcasted_iota(jnp.int32, (64, WIDE - COLS), 1)
    tail = jnp.where(lane == 0, hi.astype(F32), jnp.where(lane == 1, lo.astype(F32), 0.0))
    return jnp.concatenate([block, tail], 1).astype(BF)


def direction_kernel(d_ref, o_ref):
    load = row_block(d_ref[...])
    for i in range(ZL):
        o_ref[i] = load


def sum_x_kernel(i_ref, o_ref):
    total = i_ref[0].astype(F32)
    for i in range(1, X):
        total += i_ref[i].astype(F32)
    o_ref[...] = total.astype(BF)


def sum_zl(i_ref):
    total = i_ref[0].astype(F32)
    for i in range(1, ZL):
        total += i_ref[i].astype(F32)
    return total


def sum_rows_kernel(i_ref, rows_ref, o_ref):
    total = sum_zl(i_ref)
    rows_ref[...] = total
    load = row_block(total)
    for i in range(ZL):
        o_ref[i] = load


def last_kernel(i_ref, rows_ref, d_ref, inv_ref, o_ref):
    damp = 1.0 - DAMP
    inv = inv_ref[0:1, 0:1]
    o_ref[...] = (1.0 + damp * KEEP) * d_ref[...] - (
        damp * rows_ref[...] + sum_zl(i_ref)
    ) * inv


def start_rows(u_refs, xs, rows_ref, sems):
    copies = [
        pltpu.make_async_copy(u, rows_ref.at[:, x], sems.at[i]) for i, (u, x) in enumerate(zip(u_refs, xs))
    ]
    for copy in copies:
        copy.start()
    return copies


def await_rows(copies, rows_ref):
    for copy in copies:
        copy.wait()
    return (
        rows_ref[...].reshape(ROWS, WIDE),
        jnp.sum(rows_ref[:, :, :, COLS : COLS + 2].astype(F32)),
    )


def scores_of(x, gain, tag_ref):
    return sum(dot(part, tag_ref[...]) for part in three(x * gain))


def put_sums(load_ref, block, row, sums, scalar):
    lane = lax.broadcasted_iota(jnp.int32, (256, 128), 1)
    table = jnp.full((256, 128), scalar, F32)
    for i, s in enumerate(sums):
        table = jnp.where(lane == i, s, table)
    table = table.T
    for i in range(Y):
        load_ref[block + i, row : row + 8, 0:64] = table[0:8, i * 64 : (i + 1) * 64]
        load_ref[block + i, row : row + 8, 64:128] = table[0:8, 0:64]


def first_kernel(
    place, u0, u1, u2, u3, own_ref, oth_ref, proj_ref, s_ref, gain_ref, tag_ref, h_ref, hd_ref, load_ref,
    rows_ref, sems,
):
    xs = [lax.rem(place[2] + X - r, X) for r in range(X)]
    copies = start_rows((u0, u1, u2, u3), xs, rows_ref, sems)
    gain = gain_ref[...]
    halves = []
    for half, a_ref in enumerate((own_ref, oth_ref)):
        c = place[0] if half == 0 else 1 - place[0]
        at = pl.multiple_of(c * 256, 256)
        a = a_ref[...].reshape(256, ROWS)
        s = jnp.concatenate(
            [s_ref[y, zh, pl.ds(c, 1)][0] for y in range(Y) for zh in range(ZH)], 0
        )
        h = s.astype(F32) + lax.dot_general(a, proj_ref[...], CONTRACT1, preferred_element_type=F32)
        h_ref[pl.ds(at, 256), :] = h
        z = scores_of(h, gain, tag_ref)
        for i in range(Y):
            load_ref[c * Y + i, 0:64, :] = z[i * 64 : i * 64 + 64]
        halves.append((c, at, a_ref))
    rows, norm = await_rows(copies, rows_ref)
    for c, at, a_ref in halves:
        h = h_ref[pl.ds(at, 256), :]
        hd = dot(a_ref[...].reshape(256, ROWS), rows)[:, :COLS]
        hd_ref[pl.ds(at, 256), :] = hd
        zd = scores_of(hd, gain, tag_ref)
        for i in range(Y):
            load_ref[c * Y + i, 64:128, :] = zd[i * 64 : i * 64 + 64]
        sums = (jnp.sum(h * h, -1, keepdims=True), jnp.sum(h * hd, -1, keepdims=True))
        put_sums(load_ref, c * Y, 128, sums, norm)


def moved_kernel(
    place, u_ref, own_ref, oth_ref, h_ref, gain_ref, tag_ref, mv_ref, load_ref, rows_ref, sems
):
    copies = start_rows([u_ref.at[x] for x in range(X)], range(X), rows_ref, sems)
    rows, norm = await_rows(copies, rows_ref)
    gain = gain_ref[...]
    for half, a_ref in enumerate((own_ref, oth_ref)):
        c = place[0] if half == 0 else 1 - place[0]
        at = pl.multiple_of(c * 256, 256)
        moved = dot(a_ref[...].reshape(256, ROWS), rows)[:, :COLS]
        mv_ref[pl.ds(at, 256), :] = moved
        z = scores_of(moved, gain, tag_ref)
        for i in range(Y):
            load_ref[c * Y + i, 0:64, :] = z[i * 64 : i * 64 + 64]
        sums = (jnp.sum(h_ref[pl.ds(at, 256), :] * moved, -1, keepdims=True),)
        put_sums(load_ref, c * Y, 64, sums, norm)


def sum_parts_kernel(i_ref, o_ref):
    total = i_ref[0]
    for i in range(1, 8):
        total += i_ref[i]
    o_ref[...] = total


def columns_of(rows):
    return jnp.concatenate([rows, jnp.zeros((120, 128), F32)], 0).T[:64]


def backward(zval, sumsq, tags, along, zdot, o_ref):
    rscale = lax.rsqrt(sumsq / D + NORM_EPS)
    tanh_val = jnp.tanh(rscale * zval / 30.0)
    slope = 1.0 - tanh_val * tanh_val
    expo = jnp.exp(30.0 * tanh_val)
    probs = expo / jnp.sum(expo, -1, keepdims=True)
    onehot = (tags == lax.broadcasted_iota(jnp.int32, (64, TAGS), 1)).astype(F32)
    dlogit = probs - onehot
    wgrad = dlogit * slope
    rho = jnp.sum(wgrad * zval, -1, keepdims=True)
    cube = rscale * rscale * rscale / D
    rdot = -cube * along
    mdot = rdot * zval + rscale * zdot
    ldot = slope * mdot
    pdot = probs * (ldot - jnp.sum(probs * ldot, -1, keepdims=True))
    wdot = pdot * slope - dlogit * 2.0 * tanh_val * slope * mdot / 30.0
    rhodot = jnp.sum(wdot * zval + wgrad * zdot, -1, keepdims=True)
    mixed = rdot * wgrad + rscale * wdot
    coeff = rhodot * cube + 3.0 * rho * rscale * rscale * rdot / D
    lane = lax.broadcasted_iota(jnp.int32, (64, 128), 1)
    table = jnp.where(lane == 0, coeff, jnp.where(lane == 1, rho * cube, 0.0))
    tail = jnp.concatenate([table, jnp.zeros((64, 128), F32)], 0).T[0:8]
    for i in range(8):
        o_ref[i, 0:64, :] = mixed
        o_ref[i, 64:72, :] = tail


def tokens0_kernel(mine_ref, their_ref, tag_ref, total_ref, o_ref):
    total_ref[...] = mine_ref[...] + their_ref[...]
    columns = columns_of(total_ref[128:136, :])
    backward(
        total_ref[0:64, :], columns[:, 0:1], tag_ref[...], columns[:, 1:2], total_ref[64:128, :], o_ref
    )


def tokens1_kernel(mine_ref, their_ref, total_ref, tag_ref, o_ref, inv_ref):
    moved = mine_ref[...] + their_ref[...]
    product_sq = moved[65:66, 0:1]
    norm_sq = total_ref[130:131, 0:1]
    sigma = 2.0 * jnp.sqrt((product_sq / COUNT + MEAN_EPS) / (norm_sq / COUNT + MEAN_EPS))
    inv = 1.0 / sigma
    inv_ref[...] = jnp.broadcast_to(inv, (8, 128))
    columns0 = columns_of(total_ref[128:136, :])
    columns1 = columns_of(moved[64:72])
    along = KEEP * columns0[:, 1:2] - columns1[:, 0:1] * inv
    zdot = KEEP * total_ref[64:128, :] - moved[0:64] * inv
    backward(total_ref[0:64, :], columns0[:, 0:1], tag_ref[...], along, zdot, o_ref)


def product_kernel(second, place, m_ref, h_ref, hd_ref, *rest):
    if second:
        mv_ref, inv_ref, *rest = rest
    own_ref, oth_ref, gain_ref, tag_ref, o_ref, g_ref = rest
    gain = gain_ref[...]
    for c in range(C):
        span = slice(c * 256, c * 256 + 256)
        mixed = jnp.concatenate([m_ref[c * Y + i, 0:64, :] for i in range(Y)], 0)
        back = sum(
            lax.dot_general(part, tag_ref[...], CONTRACT1, preferred_element_type=F32)
            for part in three(mixed)
        )
        columns = jnp.concatenate([columns_of(m_ref[c * Y + i, 64:72, :]) for i in range(Y)], 0)
        hd = hd_ref[span, :]
        if second:
            hd = KEEP * hd - mv_ref[span, :] * inv_ref[0:1, 0:1]
        g = back * gain - columns[:, 0:1] * h_ref[span, :] - columns[:, 1:2] * hd
        g_ref[span, :] = g.astype(BF)
    own_at = pl.multiple_of(place[0] * 256, 256)
    oth_at = pl.multiple_of((1 - place[0]) * 256, 256)
    g_own = g_ref[pl.ds(own_at, 256), :]
    g_oth = g_ref[pl.ds(oth_at, 256), :]
    for zl in range(ZL):
        cols = slice(zl * 256, zl * 256 + 256)
        part = lax.dot_general(
            own_ref[:, :, cols].reshape(256, 256), g_own, CONTRACT0, preferred_element_type=F32
        ) + lax.dot_general(
            oth_ref[:, :, cols].reshape(256, 256), g_oth, CONTRACT0, preferred_element_type=F32
        )
        for x in range(X):
            o_ref[x, zl] = part[x * 64 : x * 64 + 64].astype(BF)


def swap(x, axis):
    return lax.ppermute(x, axis, [(0, 1), (1, 0)])


def deal(x, axis):
    return lax.all_to_all(x, axis, 0, 0, tiled=True)


def spread(x, axis, n):
    return deal(jnp.broadcast_to(x[None], (n,) + x.shape), axis)


def local(queries, keys, values, stream, out_proj, norm_gain, tag_proj, direction, starts, tags):
    core = lax.axis_index("c")
    ypos = lax.axis_index("y")
    zhpos = lax.axis_index("zh")
    offset = ((ypos * ZH + zhpos) * C + core) * 32
    place = jnp.stack([core, offset, lax.axis_index("x")]).astype(jnp.int32)
    own_tags = tags[0].reshape(Y, ZH, C, 32).transpose(2, 0, 1, 3).reshape(C * Y, 64)[core * Y + ypos]
    own_tags = own_tags[:, None]
    toks = stream[0].reshape(Y, ZH, C, 32, COLS)
    gain = norm_gain[None]

    by_zl = deal(call(direction_kernel, shape(ZL, 64, WIDE, dtype=BF), direction), "zl")
    mine = call(
        attend_kernel, shape(32, ROWS, dtype=BF), place, starts, queries[0], keys[0], values[0], smem=2
    )
    theirs, by_zl = lax.optimization_barrier((swap(mine, "zh"), by_zl))
    u0 = [by_zl] + [
        lax.ppermute(by_zl, "x", [(i, (i + r) % X) for i in range(X)]) for r in range(1, X)
    ]
    low = zhpos == 0
    pair = jnp.stack([jnp.where(low, mine, theirs), jnp.where(low, theirs, mine)])
    own, *u0 = lax.optimization_barrier((spread(pair.reshape(64, ROWS), "y", Y), *u0))
    other = swap(own, "c")

    def product(second, *args):
        sent = call(
            functools.partial(product_kernel, second, scratch=[pltpu.VMEM((512, COLS), BF)]),
            shape(X, ZL, 64, COLS, dtype=BF),
            place,
            *args,
            own,
            other,
            gain,
            tag_proj,
            smem=1,
        )
        part = call(sum_x_kernel, shape(ZL, 64, COLS, dtype=BF), deal(sent, "x"))
        return deal(part, "zl")

    def token_sum(load, kernel, outs, *args):
        part = call(sum_parts_kernel, shape(load.shape[1], 128), deal(load, ("c", "y")))
        return call(kernel, outs, part, swap(part, "zh"), *args, own_tags)

    rows_scratch = [pltpu.VMEM((ZL, X, 64, WIDE), BF), pltpu.SemaphoreType.DMA((X,))]
    h_loc, hdot0, load = call(
        functools.partial(first_kernel, scratch=rows_scratch),
        (shape(512, COLS), shape(512, COLS), shape(8, 136, 128)),
        place,
        *u0,
        own,
        other,
        out_proj.T,
        toks,
        gain,
        tag_proj,
        smem=1,
        far=X,
    )
    total, mixed = token_sum(load, tokens0_kernel, (shape(136, 128), shape(8, 72, 128)))
    rows0, sent = call(
        sum_rows_kernel,
        (shape(64, COLS), shape(ZL, 64, WIDE, dtype=BF)),
        product(False, deal(mixed, ("c", "y")), h_loc, hdot0),
    )
    full0 = spread(deal(sent, "zl").reshape(ZL * 64, WIDE), "x", X).reshape(X, ZL, 64, WIDE)
    moved, load = call(
        functools.partial(moved_kernel, scratch=rows_scratch),
        (shape(512, COLS), shape(8, 72, 128)),
        place,
        full0,
        own,
        other,
        h_loc,
        gain,
        tag_proj,
        smem=1,
        far=1,
    )
    mixed, inv = token_sum(load, tokens1_kernel, (shape(8, 72, 128), shape(8, 128)), total)
    arrived = product(True, deal(mixed, ("c", "y")), h_loc, hdot0, moved, inv)
    return call(last_kernel, shape(64, COLS), arrived, rows0, direction, inv)


def solution(mesh):
    fine = Mesh(mesh.devices.reshape(ZL, X, Y, ZH, C), ("zl", "x", "y", "zh", "c"))
    dp, mp = ("zl", "x"), ("y", "zh", "c")
    return jax.shard_map(
        local,
        mesh=fine,
        in_specs=(
            P(dp, mp, None),
            P(dp, None, None),
            P(dp, None, None),
            P(dp, None, mp),
            P(None, mp),
            P(mp),
            P(mp, None),
            P(dp, mp),
            P(dp, None),
            P(dp, None),
        ),
        out_specs=P(dp, mp),
        check_vma=False,
    )
```

```python
import functools

import jax
import jax.numpy as jnp
from jax import lax
from jax.experimental import pallas as pl
from jax.experimental.pallas import tpu as pltpu
from jax.sharding import Mesh, PartitionSpec as P

D = 3584
HD = 256
HQ = 8
HK = 4
TAGS = 128
WINDOW = 256
DAMP = 0.01
KEEP = 2.0 - DAMP
NORM_EPS = 1e-06
MEAN_EPS = 1e-06
ZL, X, Y, ZH, C = 8, 4, 4, 2, 2
ROWS = HQ * HD
COLS = 224
WIDE = 256
COUNT = HQ * HD * D
SPAN = 288
PACK = 112
BF = jnp.bfloat16
F32 = jnp.float32
CONTRACT0 = (((0,), (0,)), ((), ()))
CONTRACT1 = (((1,), (1,)), ((), ()))


def call(kernel, out_shape, *args, smem=0, far=0):
    specs = [pl.BlockSpec(memory_space=pltpu.SMEM)] * smem
    specs += [pl.BlockSpec(memory_space=pl.ANY)] * far
    args = [
        pltpu.with_memory_space_constraint(a, pltpu.HBM) if smem <= i < smem + far else a
        for i, a in enumerate(args)
    ]
    specs += [pl.BlockSpec(memory_space=pltpu.VMEM)] * (len(args) - smem - far)
    scratch = kernel.keywords.pop("scratch", ()) if isinstance(kernel, functools.partial) else ()
    many = isinstance(out_shape, (tuple, list))
    vmem = pl.BlockSpec(memory_space=pltpu.VMEM)
    return pl.pallas_call(
        kernel,
        out_shape=out_shape,
        in_specs=specs,
        out_specs=[vmem] * len(out_shape) if many else vmem,
        scratch_shapes=scratch,
        compiler_params=pltpu.CompilerParams(vmem_limit_bytes=40 * 2**20),
    )(*args)


def shape(*dims, dtype=F32):
    return jax.ShapeDtypeStruct(dims, dtype)


def dot(a, b):
    return jnp.dot(a, b, preferred_element_type=F32)


def three(x):
    a = x.astype(BF)
    rest = x - a.astype(F32)
    b = rest.astype(BF)
    return a, b, (rest - b.astype(F32)).astype(BF)


def attend_kernel(place, starts, k_far, v_far, q_ref, o_ref, k_ref, v_ref, sems):
    offset = place[1]
    first = pl.multiple_of(jnp.maximum(offset - WINDOW, 0), 32)
    k_copy = pltpu.make_async_copy(k_far.at[pl.ds(first, SPAN)], k_ref, sems.at[0])
    v_copy = pltpu.make_async_copy(v_far.at[pl.ds(first, SPAN)], v_ref, sems.at[1])
    k_copy.start()
    v_copy.start()
    q_row = lax.broadcasted_iota(jnp.int32, (64, 1), 0)
    q_pos = offset + jnp.where(q_row < 32, q_row, q_row - 32)
    k_pos = first + lax.broadcasted_iota(jnp.int32, (1, SPAN), 1)
    q_file = jnp.zeros((64, 1), jnp.int32)
    k_file = jnp.zeros((1, SPAN), jnp.int32)
    for f in range(4):
        q_file += jnp.where(starts[0, f] <= q_pos, 1, 0)
        k_file += jnp.where(starts[0, f] <= k_pos, 1, 0)
    allowed = (q_file == k_file) & (k_pos <= q_pos) & (q_pos - k_pos < WINDOW)
    k_copy.wait()
    v_copy.wait()
    for g in range(HK):
        q = jnp.concatenate(
            [q_ref[:, (2 * g + r) * HD : (2 * g + r + 1) * HD] for r in range(2)], 0
        )
        cols = slice(g * HD, (g + 1) * HD)
        scores = lax.dot_general(
            q, k_ref[:, cols], CONTRACT1, preferred_element_type=F32
        )
        scores = 50.0 * jnp.tanh(scores * (1.0 / 16.0) / 50.0)
        expo = jnp.where(allowed, jnp.exp(scores), 0.0)
        weights = (expo / jnp.sum(expo, -1, keepdims=True)).astype(BF)
        out = dot(weights, v_ref[:, cols]).astype(BF)
        for r in range(2):
            o_ref[:, (2 * g + r) * HD : (2 * g + r + 1) * HD] = out[r * 32 : r * 32 + 32]


def row_block(block):
    total = jnp.sum(block * block, -1, keepdims=True)
    hi = total.astype(BF)
    lo = (total - hi.astype(F32)).astype(BF)
    lane = lax.broadcasted_iota(jnp.int32, (64, WIDE - COLS), 1)
    tail = jnp.where(lane == 0, hi.astype(F32), jnp.where(lane == 1, lo.astype(F32), 0.0))
    return jnp.concatenate([block, tail], 1).astype(BF)


def packed(block):
    last = jnp.concatenate([block[48:64, at : at + 32] for at in (128, 160, 192)], 0)
    tail = jnp.concatenate([block[0:48, 128:COLS], last], 1)
    return jnp.concatenate([block[:, 0:128], tail], 0)


def unpacked(block):
    last = jnp.concatenate([block[at : at + 16, 96:128] for at in (64, 80, 96)], 1)
    tail = jnp.concatenate([block[64:112, 0:96], last], 0)
    return jnp.concatenate([block[0:64], tail], 1)


def direction_kernel(d_ref, o_ref):
    load = row_block(d_ref[...])
    for i in range(ZL):
        o_ref[i] = load


def sum_x_kernel(i_ref, o_ref):
    total = i_ref[0].astype(F32)
    for i in range(1, X):
        total += i_ref[i].astype(F32)
    o_ref[...] = total.astype(BF)


def sum_zl(i_ref):
    total = i_ref[0].astype(F32)
    for i in range(1, ZL):
        total += i_ref[i].astype(F32)
    return unpacked(total)


def sum_rows_kernel(i_ref, rows_ref, o_ref):
    total = sum_zl(i_ref)
    rows_ref[...] = total
    load = row_block(total)
    for i in range(ZL):
        o_ref[i] = load


def last_kernel(i_ref, rows_ref, d_ref, inv_ref, o_ref):
    damp = 1.0 - DAMP
    inv = inv_ref[0:1, 0:1]
    o_ref[...] = (1.0 + damp * KEEP) * d_ref[...] - (
        damp * rows_ref[...] + sum_zl(i_ref)
    ) * inv


def start_rows(u_refs, xs, rows_ref, sems):
    copies = [
        pltpu.make_async_copy(u, rows_ref.at[:, x], sems.at[i]) for i, (u, x) in enumerate(zip(u_refs, xs))
    ]
    for copy in copies:
        copy.start()
    return copies


def await_rows(copies, rows_ref):
    for copy in copies:
        copy.wait()
    return (
        rows_ref[...].reshape(ROWS, WIDE),
        jnp.sum(rows_ref[:, :, :, COLS : COLS + 2].astype(F32)),
    )


def scores_of(x, gain, tag_ref):
    return sum(dot(part, tag_ref[...]) for part in three(x * gain))


def put_sums(load_ref, block, row, sums, scalar):
    lane = lax.broadcasted_iota(jnp.int32, (256, 128), 1)
    table = jnp.full((256, 128), scalar, F32)
    for i, s in enumerate(sums):
        table = jnp.where(lane == i, s, table)
    table = table.T
    for i in range(Y):
        load_ref[block + i, row : row + 8, 0:64] = table[0:8, i * 64 : (i + 1) * 64]
        load_ref[block + i, row : row + 8, 64:128] = table[0:8, 0:64]


def first_kernel(
    place, proj_far, u0, u1, u2, u3, own_ref, oth_ref, s_ref, gain_ref, tag_ref, h_ref, hd_ref, load_ref,
    proj_ref, rows_ref, sems,
):
    proj_copy = pltpu.make_async_copy(proj_far, proj_ref, sems.at[X])
    proj_copy.start()
    xs = [lax.rem(place[2] + X - r, X) for r in range(X)]
    copies = start_rows((u0, u1, u2, u3), xs, rows_ref, sems)
    gain = gain_ref[...]
    halves = []
    proj_copy.wait()
    for half, a_ref in enumerate((own_ref, oth_ref)):
        c = place[0] if half == 0 else 1 - place[0]
        at = pl.multiple_of(c * 256, 256)
        a = a_ref[...].reshape(256, ROWS)
        s = jnp.concatenate(
            [s_ref[y, zh, pl.ds(c, 1)][0] for y in range(Y) for zh in range(ZH)], 0
        )
        h = s.astype(F32) + dot(a, proj_ref[...])
        h_ref[pl.ds(at, 256), :] = h
        z = scores_of(h, gain, tag_ref)
        for i in range(Y):
            load_ref[c * Y + i, 0:64, :] = z[i * 64 : i * 64 + 64]
        halves.append((c, at, a_ref))
    rows, norm = await_rows(copies, rows_ref)
    for c, at, a_ref in halves:
        h = h_ref[pl.ds(at, 256), :]
        hd = dot(a_ref[...].reshape(256, ROWS), rows)[:, :COLS]
        hd_ref[pl.ds(at, 256), :] = hd
        zd = scores_of(hd, gain, tag_ref)
        for i in range(Y):
            load_ref[c * Y + i, 64:128, :] = zd[i * 64 : i * 64 + 64]
        sums = (jnp.sum(h * h, -1, keepdims=True), jnp.sum(h * hd, -1, keepdims=True))
        put_sums(load_ref, c * Y, 128, sums, norm)


def moved_kernel(
    place, u_ref, own_ref, oth_ref, h_ref, gain_ref, tag_ref, mv_ref, load_ref, rows_ref, sems
):
    copies = start_rows([u_ref.at[x] for x in range(X)], range(X), rows_ref, sems)
    rows, norm = await_rows(copies, rows_ref)
    gain = gain_ref[...]
    for half, a_ref in enumerate((own_ref, oth_ref)):
        c = place[0] if half == 0 else 1 - place[0]
        at = pl.multiple_of(c * 256, 256)
        moved = dot(a_ref[...].reshape(256, ROWS), rows)[:, :COLS]
        mv_ref[pl.ds(at, 256), :] = moved
        z = scores_of(moved, gain, tag_ref)
        for i in range(Y):
            load_ref[c * Y + i, 0:64, :] = z[i * 64 : i * 64 + 64]
        sums = (jnp.sum(h_ref[pl.ds(at, 256), :] * moved, -1, keepdims=True),)
        put_sums(load_ref, c * Y, 64, sums, norm)


def sum_parts_kernel(i_ref, o_ref):
    total = i_ref[0]
    for i in range(1, 8):
        total += i_ref[i]
    o_ref[...] = total


def columns_of(rows):
    return jnp.concatenate([rows, jnp.zeros((120, 128), F32)], 0).T[:64]


def backward(zval, sumsq, tags, along, zdot, o_ref):
    rscale = lax.rsqrt(sumsq / D + NORM_EPS)
    tanh_val = jnp.tanh(rscale * zval / 30.0)
    slope = 1.0 - tanh_val * tanh_val
    expo = jnp.exp(30.0 * tanh_val)
    probs = expo / jnp.sum(expo, -1, keepdims=True)
    onehot = (tags == lax.broadcasted_iota(jnp.int32, (64, TAGS), 1)).astype(F32)
    dlogit = probs - onehot
    wgrad = dlogit * slope
    rho = jnp.sum(wgrad * zval, -1, keepdims=True)
    cube = rscale * rscale * rscale / D
    rdot = -cube * along
    mdot = rdot * zval + rscale * zdot
    ldot = slope * mdot
    pdot = probs * (ldot - jnp.sum(probs * ldot, -1, keepdims=True))
    wdot = pdot * slope - dlogit * 2.0 * tanh_val * slope * mdot / 30.0
    rhodot = jnp.sum(wdot * zval + wgrad * zdot, -1, keepdims=True)
    mixed = rdot * wgrad + rscale * wdot
    coeff = rhodot * cube + 3.0 * rho * rscale * rscale * rdot / D
    lane = lax.broadcasted_iota(jnp.int32, (64, 128), 1)
    table = jnp.where(lane == 0, coeff, jnp.where(lane == 1, rho * cube, 0.0))
    tail = jnp.concatenate([table, jnp.zeros((64, 128), F32)], 0).T[0:8]
    for i in range(8):
        o_ref[i, 0:64, :] = mixed
        o_ref[i, 64:72, :] = tail


def tokens0_kernel(mine_ref, their_ref, tag_ref, total_ref, o_ref):
    total_ref[...] = mine_ref[...] + their_ref[...]
    columns = columns_of(total_ref[128:136, :])
    backward(
        total_ref[0:64, :], columns[:, 0:1], tag_ref[...], columns[:, 1:2], total_ref[64:128, :], o_ref
    )


def tokens1_kernel(mine_ref, their_ref, total_ref, tag_ref, o_ref, inv_ref):
    moved = mine_ref[...] + their_ref[...]
    product_sq = moved[65:66, 0:1]
    norm_sq = total_ref[130:131, 0:1]
    sigma = 2.0 * jnp.sqrt((product_sq / COUNT + MEAN_EPS) / (norm_sq / COUNT + MEAN_EPS))
    inv = 1.0 / sigma
    inv_ref[...] = jnp.broadcast_to(inv, (8, 128))
    columns0 = columns_of(total_ref[128:136, :])
    columns1 = columns_of(moved[64:72])
    along = KEEP * columns0[:, 1:2] - columns1[:, 0:1] * inv
    zdot = KEEP * total_ref[64:128, :] - moved[0:64] * inv
    backward(total_ref[0:64, :], columns0[:, 0:1], tag_ref[...], along, zdot, o_ref)


def product_kernel(second, place, m_ref, h_ref, hd_ref, *rest):
    if second:
        mv_ref, inv_ref, *rest = rest
    own_ref, oth_ref, gain_ref, tag_ref, o_ref, g_ref = rest
    gain = gain_ref[...]
    for c in range(C):
        span = slice(c * 256, c * 256 + 256)
        mixed = jnp.concatenate([m_ref[c * Y + i, 0:64, :] for i in range(Y)], 0)
        back = sum(
            lax.dot_general(part, tag_ref[...], CONTRACT1, preferred_element_type=F32)
            for part in three(mixed)
        )
        columns = jnp.concatenate([columns_of(m_ref[c * Y + i, 64:72, :]) for i in range(Y)], 0)
        hd = hd_ref[span, :]
        if second:
            hd = KEEP * hd - mv_ref[span, :] * inv_ref[0:1, 0:1]
        g = back * gain - columns[:, 0:1] * h_ref[span, :] - columns[:, 1:2] * hd
        g_ref[span, :] = g.astype(BF)
    own_at = pl.multiple_of(place[0] * 256, 256)
    oth_at = pl.multiple_of((1 - place[0]) * 256, 256)
    g_own = g_ref[pl.ds(own_at, 256), :]
    g_oth = g_ref[pl.ds(oth_at, 256), :]
    for zl in range(ZL):
        cols = slice(zl * 256, zl * 256 + 256)
        part = lax.dot_general(
            own_ref[:, :, cols].reshape(256, 256), g_own, CONTRACT0, preferred_element_type=F32
        ) + lax.dot_general(
            oth_ref[:, :, cols].reshape(256, 256), g_oth, CONTRACT0, preferred_element_type=F32
        )
        for x in range(X):
            o_ref[x, zl] = packed(part[x * 64 : x * 64 + 64]).astype(BF)


def swap(x, axis):
    return lax.ppermute(x, axis, [(0, 1), (1, 0)])


def deal(x, axis):
    return lax.all_to_all(x, axis, 0, 0, tiled=True)


def spread(x, axis, n):
    return deal(jnp.broadcast_to(x[None], (n,) + x.shape), axis)


def local(queries, keys, values, stream, out_proj, norm_gain, tag_proj, direction, starts, tags):
    core = lax.axis_index("c")
    ypos = lax.axis_index("y")
    zhpos = lax.axis_index("zh")
    offset = ((ypos * ZH + zhpos) * C + core) * 32
    place = jnp.stack([core, offset, lax.axis_index("x")]).astype(jnp.int32)
    own_tags = tags[0].reshape(Y, ZH, C, 32).transpose(2, 0, 1, 3).reshape(C * Y, 64)[core * Y + ypos]
    own_tags = own_tags[:, None]
    toks = stream[0].reshape(Y, ZH, C, 32, COLS)
    gain = norm_gain[None]

    by_zl = deal(call(direction_kernel, shape(ZL, 64, WIDE, dtype=BF), direction), "zl")
    mine = call(
        functools.partial(
            attend_kernel,
            scratch=[pltpu.VMEM((SPAN, HK * HD), BF)] * 2 + [pltpu.SemaphoreType.DMA((2,))],
        ),
        shape(32, ROWS, dtype=BF),
        place,
        starts,
        keys[0],
        values[0],
        queries[0],
        smem=2,
        far=2,
    )
    mine, by_zl = lax.optimization_barrier((mine, by_zl))
    theirs = swap(mine, "zh")
    u0 = [by_zl] + [
        lax.ppermute(by_zl, "x", [(i, (i + r) % X) for i in range(X)]) for r in range(1, X)
    ]
    theirs, *u0 = lax.optimization_barrier((theirs, *u0))
    low = zhpos == 0
    pair = jnp.stack([jnp.where(low, mine, theirs), jnp.where(low, theirs, mine)])
    own, toks, own_tags, proj = lax.optimization_barrier(
        (spread(pair.reshape(64, ROWS), "y", Y), toks, own_tags, out_proj)
    )
    other = swap(own, "c")

    def product(second, *args):
        sent = call(
            functools.partial(product_kernel, second, scratch=[pltpu.VMEM((512, COLS), BF)]),
            shape(X, ZL, PACK, 128, dtype=BF),
            place,
            *args,
            own,
            other,
            gain,
            tag_proj,
            smem=1,
        )
        part = call(sum_x_kernel, shape(ZL, PACK, 128, dtype=BF), deal(sent, "x"))
        return deal(part, "zl")

    def token_sum(load, kernel, outs, *args):
        part = call(sum_parts_kernel, shape(load.shape[1], 128), deal(load, ("c", "y")))
        return call(kernel, outs, part, swap(part, "zh"), *args, own_tags)

    rows_scratch = [pltpu.VMEM((ZL, X, 64, WIDE), BF), pltpu.SemaphoreType.DMA((X + 1,))]
    h_loc, hdot0, load = call(
        functools.partial(first_kernel, scratch=[pltpu.VMEM((ROWS, COLS), BF)] + rows_scratch),
        (shape(512, COLS), shape(512, COLS), shape(8, 136, 128)),
        place,
        proj,
        *u0,
        own,
        other,
        toks,
        gain,
        tag_proj,
        smem=1,
        far=X + 1,
    )
    total, mixed = token_sum(load, tokens0_kernel, (shape(136, 128), shape(8, 72, 128)))
    rows0, sent = call(
        sum_rows_kernel,
        (shape(64, COLS), shape(ZL, 64, WIDE, dtype=BF)),
        product(False, deal(mixed, ("c", "y")), h_loc, hdot0),
    )
    full0 = spread(deal(sent, "zl").reshape(ZL * 64, WIDE), "x", X).reshape(X, ZL, 64, WIDE)
    moved, load = call(
        functools.partial(moved_kernel, scratch=rows_scratch),
        (shape(512, COLS), shape(8, 72, 128)),
        place,
        full0,
        own,
        other,
        h_loc,
        gain,
        tag_proj,
        smem=1,
        far=1,
    )
    mixed, inv = token_sum(load, tokens1_kernel, (shape(8, 72, 128), shape(8, 128)), total)
    arrived = product(True, deal(mixed, ("c", "y")), h_loc, hdot0, moved, inv)
    return call(last_kernel, shape(64, COLS), arrived, rows0, direction, inv)


def solution(mesh):
    fine = Mesh(mesh.devices.reshape(ZL, X, Y, ZH, C), ("zl", "x", "y", "zh", "c"))
    dp, mp = ("zl", "x"), ("y", "zh", "c")
    return jax.shard_map(
        local,
        mesh=fine,
        in_specs=(
            P(dp, mp, None),
            P(dp, None, None),
            P(dp, None, None),
            P(dp, None, mp),
            P(None, mp),
            P(mp),
            P(mp, None),
            P(dp, mp),
            P(dp, None),
            P(dp, None),
        ),
        out_specs=P(dp, mp),
        check_vma=False,
    )
```

```python
import functools

import jax
import jax.numpy as jnp
from jax import lax
from jax.experimental import pallas as pl
from jax.experimental.pallas import tpu as pltpu
from jax.sharding import Mesh, PartitionSpec as P

D = 3584
HD = 256
HQ = 8
HK = 4
TAGS = 128
WINDOW = 256
DAMP = 0.01
KEEP = 2.0 - DAMP
NORM_EPS = 1e-06
MEAN_EPS = 1e-06
ZL, X, Y, ZH, C = 8, 4, 4, 2, 2
ROWS = HQ * HD
COLS = 224
WIDE = 256
COUNT = HQ * HD * D
SPAN = 352
PACK = 112
BF = jnp.bfloat16
F32 = jnp.float32
CONTRACT0 = (((0,), (0,)), ((), ()))
CONTRACT1 = (((1,), (1,)), ((), ()))


def call(kernel, out_shape, *args, smem=0, far=0):
    specs = [pl.BlockSpec(memory_space=pltpu.SMEM)] * smem
    specs += [pl.BlockSpec(memory_space=pl.ANY)] * far
    args = [
        pltpu.with_memory_space_constraint(a, pltpu.HBM) if smem <= i < smem + far else a
        for i, a in enumerate(args)
    ]
    specs += [pl.BlockSpec(memory_space=pltpu.VMEM)] * (len(args) - smem - far)
    scratch = kernel.keywords.pop("scratch", ()) if isinstance(kernel, functools.partial) else ()
    many = isinstance(out_shape, (tuple, list))
    vmem = pl.BlockSpec(memory_space=pltpu.VMEM)
    return pl.pallas_call(
        kernel,
        out_shape=out_shape,
        in_specs=specs,
        out_specs=[vmem] * len(out_shape) if many else vmem,
        scratch_shapes=scratch,
        compiler_params=pltpu.CompilerParams(vmem_limit_bytes=40 * 2**20),
    )(*args)


def shape(*dims, dtype=F32):
    return jax.ShapeDtypeStruct(dims, dtype)


def dot(a, b):
    return jnp.dot(a, b, preferred_element_type=F32)


def three(x):
    a = x.astype(BF)
    rest = x - a.astype(F32)
    b = rest.astype(BF)
    return a, b, (rest - b.astype(F32)).astype(BF)


def attend_kernel(place, starts, k_far, v_far, own_ref, oth_ref, o_ref, k_ref, v_ref, sems):
    own_at, oth_at, zh = place[1], place[2], place[3]
    first = pl.multiple_of(jnp.maximum(jnp.minimum(own_at, oth_at) - WINDOW, 0), 32)
    k_copy = pltpu.make_async_copy(k_far.at[pl.ds(first, SPAN)], k_ref, sems.at[0])
    v_copy = pltpu.make_async_copy(v_far.at[pl.ds(first, SPAN)], v_ref, sems.at[1])
    k_copy.start()
    v_copy.start()
    row = lax.broadcasted_iota(jnp.int32, (128, 1), 0)
    within = jnp.where(row < 64, row, row - 64)
    q_pos = jnp.where(within < 32, within + own_at, within - 32 + oth_at)
    k_pos = first + lax.broadcasted_iota(jnp.int32, (1, SPAN), 1)
    q_file = jnp.zeros((128, 1), jnp.int32)
    k_file = jnp.zeros((1, SPAN), jnp.int32)
    for f in range(4):
        q_file += jnp.where(starts[0, f] <= q_pos, 1, 0)
        k_file += jnp.where(starts[0, f] <= k_pos, 1, 0)
    allowed = (q_file == k_file) & (k_pos <= q_pos) & (q_pos - k_pos < WINDOW)
    k_copy.wait()
    v_copy.wait()
    for g in range(HK):
        heads = [slice((2 * g + r) * HD, (2 * g + r + 1) * HD) for r in range(2)]
        q = jnp.concatenate([ref[:, head] for head in heads for ref in (own_ref, oth_ref)], 0)
        cols = slice(g * HD, (g + 1) * HD)
        scores = lax.dot_general(q, k_ref[:, cols], CONTRACT1, preferred_element_type=F32)
        scores = 50.0 * jnp.tanh(scores * (1.0 / 16.0) / 50.0)
        expo = jnp.where(allowed, jnp.exp(scores), 0.0)
        weights = (expo / jnp.sum(expo, -1, keepdims=True)).astype(BF)
        out = dot(weights, v_ref[:, cols]).astype(BF)
        for r, head in enumerate(heads):
            for y in range(Y):
                o_ref[y, zh, :, head] = out[r * 64 : r * 64 + 32]
                o_ref[y, 1 - zh, :, head] = out[r * 64 + 32 : r * 64 + 64]


def row_block(block):
    total = jnp.sum(block * block, -1, keepdims=True)
    hi = total.astype(BF)
    lo = (total - hi.astype(F32)).astype(BF)
    lane = lax.broadcasted_iota(jnp.int32, (64, WIDE - COLS), 1)
    tail = jnp.where(lane == 0, hi.astype(F32), jnp.where(lane == 1, lo.astype(F32), 0.0))
    return jnp.concatenate([block, tail], 1).astype(BF)


def packed(block):
    last = jnp.concatenate([block[48:64, at : at + 32] for at in (128, 160, 192)], 0)
    tail = jnp.concatenate([block[0:48, 128:COLS], last], 1)
    return jnp.concatenate([block[:, 0:128], tail], 0)


def unpacked(block):
    last = jnp.concatenate([block[at : at + 16, 96:128] for at in (64, 80, 96)], 1)
    tail = jnp.concatenate([block[64:112, 0:96], last], 0)
    return jnp.concatenate([block[0:64], tail], 1)


def direction_kernel(d_ref, o_ref):
    load = row_block(d_ref[...])
    for i in range(ZL):
        o_ref[i] = load


def sum_x_kernel(i_ref, o_ref):
    total = i_ref[0].astype(F32)
    for i in range(1, X):
        total += i_ref[i].astype(F32)
    o_ref[...] = total.astype(BF)


def sum_zl(i_ref):
    total = i_ref[0].astype(F32)
    for i in range(1, ZL):
        total += i_ref[i].astype(F32)
    return unpacked(total)


def sum_rows_kernel(i_ref, rows_ref, o_ref):
    total = sum_zl(i_ref)
    rows_ref[...] = total
    load = row_block(total)
    for i in range(ZL):
        o_ref[i] = load


def last_kernel(i_ref, rows_ref, d_ref, inv_ref, o_ref):
    damp = 1.0 - DAMP
    inv = inv_ref[0:1, 0:1]
    o_ref[...] = (1.0 + damp * KEEP) * d_ref[...] - (
        damp * rows_ref[...] + sum_zl(i_ref)
    ) * inv


def start_rows(u_refs, xs, rows_ref, sems):
    copies = [
        pltpu.make_async_copy(u, rows_ref.at[:, x], sems.at[i]) for i, (u, x) in enumerate(zip(u_refs, xs))
    ]
    for copy in copies:
        copy.start()
    return copies


def await_rows(copies, rows_ref):
    for copy in copies:
        copy.wait()
    return (
        rows_ref[...].reshape(ROWS, WIDE),
        jnp.sum(rows_ref[:, :, :, COLS : COLS + 2].astype(F32)),
    )


def scores_of(x, gain, tag_ref):
    return sum(dot(part, tag_ref[...]) for part in three(x * gain))


def put_sums(load_ref, block, row, sums, scalar):
    lane = lax.broadcasted_iota(jnp.int32, (256, 128), 1)
    table = jnp.full((256, 128), scalar, F32)
    for i, s in enumerate(sums):
        table = jnp.where(lane == i, s, table)
    table = table.T
    for i in range(Y):
        load_ref[block + i, row : row + 8, 0:64] = table[0:8, i * 64 : (i + 1) * 64]
        load_ref[block + i, row : row + 8, 64:128] = table[0:8, 0:64]


def first_kernel(
    place, proj_far, u0, u1, u2, u3, own_ref, oth_ref, s_ref, gain_ref, tag_ref, h_ref, hd_ref, load_ref,
    proj_ref, rows_ref, sems,
):
    proj_copy = pltpu.make_async_copy(proj_far, proj_ref, sems.at[X])
    proj_copy.start()
    xs = [lax.rem(place[4] + X - r, X) for r in range(X)]
    copies = start_rows((u0, u1, u2, u3), xs, rows_ref, sems)
    gain = gain_ref[...]
    halves = []
    proj_copy.wait()
    for half, a_ref in enumerate((own_ref, oth_ref)):
        c = place[0] if half == 0 else 1 - place[0]
        at = pl.multiple_of(c * 256, 256)
        a = a_ref[...].reshape(256, ROWS)
        s = jnp.concatenate(
            [s_ref[y, zh, pl.ds(c, 1)][0] for y in range(Y) for zh in range(ZH)], 0
        )
        h = s.astype(F32) + dot(a, proj_ref[...])
        h_ref[pl.ds(at, 256), :] = h
        z = scores_of(h, gain, tag_ref)
        for i in range(Y):
            load_ref[c * Y + i, 0:64, :] = z[i * 64 : i * 64 + 64]
        halves.append((c, at, a_ref))
    rows, norm = await_rows(copies, rows_ref)
    for c, at, a_ref in halves:
        h = h_ref[pl.ds(at, 256), :]
        hd = dot(a_ref[...].reshape(256, ROWS), rows)[:, :COLS]
        hd_ref[pl.ds(at, 256), :] = hd
        zd = scores_of(hd, gain, tag_ref)
        for i in range(Y):
            load_ref[c * Y + i, 64:128, :] = zd[i * 64 : i * 64 + 64]
        sums = (jnp.sum(h * h, -1, keepdims=True), jnp.sum(h * hd, -1, keepdims=True))
        put_sums(load_ref, c * Y, 128, sums, norm)


def moved_kernel(
    place, u_ref, own_ref, oth_ref, h_ref, gain_ref, tag_ref, mv_ref, load_ref, rows_ref
):
    for x in range(X):
        rows_ref[:, x] = u_ref[x]
    rows, norm = await_rows((), rows_ref)
    gain = gain_ref[...]
    for half, a_ref in enumerate((own_ref, oth_ref)):
        c = place[0] if half == 0 else 1 - place[0]
        at = pl.multiple_of(c * 256, 256)
        moved = dot(a_ref[...].reshape(256, ROWS), rows)[:, :COLS]
        mv_ref[pl.ds(at, 256), :] = moved
        z = scores_of(moved, gain, tag_ref)
        for i in range(Y):
            load_ref[c * Y + i, 0:64, :] = z[i * 64 : i * 64 + 64]
        sums = (jnp.sum(h_ref[pl.ds(at, 256), :] * moved, -1, keepdims=True),)
        put_sums(load_ref, c * Y, 64, sums, norm)


def sum_parts_kernel(i_ref, o_ref):
    total = i_ref[0]
    for i in range(1, 8):
        total += i_ref[i]
    o_ref[...] = total


def columns_of(rows):
    return jnp.concatenate([rows, jnp.zeros((120, 128), F32)], 0).T[:64]


def backward(zval, sumsq, tags, along, zdot, o_ref):
    rscale = lax.rsqrt(sumsq / D + NORM_EPS)
    tanh_val = jnp.tanh(rscale * zval / 30.0)
    slope = 1.0 - tanh_val * tanh_val
    expo = jnp.exp(30.0 * tanh_val)
    probs = expo / jnp.sum(expo, -1, keepdims=True)
    onehot = (tags == lax.broadcasted_iota(jnp.int32, (64, TAGS), 1)).astype(F32)
    dlogit = probs - onehot
    wgrad = dlogit * slope
    rho = jnp.sum(wgrad * zval, -1, keepdims=True)
    cube = rscale * rscale * rscale / D
    rdot = -cube * along
    mdot = rdot * zval + rscale * zdot
    ldot = slope * mdot
    pdot = probs * (ldot - jnp.sum(probs * ldot, -1, keepdims=True))
    wdot = pdot * slope - dlogit * 2.0 * tanh_val * slope * mdot / 30.0
    rhodot = jnp.sum(wdot * zval + wgrad * zdot, -1, keepdims=True)
    mixed = rdot * wgrad + rscale * wdot
    coeff = rhodot * cube + 3.0 * rho * rscale * rscale * rdot / D
    lane = lax.broadcasted_iota(jnp.int32, (64, 128), 1)
    table = jnp.where(lane == 0, coeff, jnp.where(lane == 1, rho * cube, 0.0))
    tail = jnp.concatenate([table, jnp.zeros((64, 128), F32)], 0).T[0:8]
    for i in range(8):
        o_ref[i, 0:64, :] = mixed
        o_ref[i, 64:72, :] = tail


def tokens0_kernel(mine_ref, their_ref, tag_ref, total_ref, o_ref):
    total_ref[...] = mine_ref[...] + their_ref[...]
    columns = columns_of(total_ref[128:136, :])
    backward(
        total_ref[0:64, :], columns[:, 0:1], tag_ref[...], columns[:, 1:2], total_ref[64:128, :], o_ref
    )


def tokens1_kernel(mine_ref, their_ref, total_ref, tag_ref, o_ref, inv_ref):
    moved = mine_ref[...] + their_ref[...]
    product_sq = moved[65:66, 0:1]
    norm_sq = total_ref[130:131, 0:1]
    sigma = 2.0 * jnp.sqrt((product_sq / COUNT + MEAN_EPS) / (norm_sq / COUNT + MEAN_EPS))
    inv = 1.0 / sigma
    inv_ref[...] = jnp.broadcast_to(inv, (8, 128))
    columns0 = columns_of(total_ref[128:136, :])
    columns1 = columns_of(moved[64:72])
    along = KEEP * columns0[:, 1:2] - columns1[:, 0:1] * inv
    zdot = KEEP * total_ref[64:128, :] - moved[0:64] * inv
    backward(total_ref[0:64, :], columns0[:, 0:1], tag_ref[...], along, zdot, o_ref)


def product_kernel(second, place, m_ref, h_ref, hd_ref, *rest):
    if second:
        mv_ref, inv_ref, *rest = rest
    own_ref, oth_ref, gain_ref, tag_ref, o_ref, g_ref = rest
    gain = gain_ref[...]
    for c in range(C):
        span = slice(c * 256, c * 256 + 256)
        mixed = jnp.concatenate([m_ref[c * Y + i, 0:64, :] for i in range(Y)], 0)
        back = sum(
            lax.dot_general(part, tag_ref[...], CONTRACT1, preferred_element_type=F32)
            for part in three(mixed)
        )
        columns = jnp.concatenate([columns_of(m_ref[c * Y + i, 64:72, :]) for i in range(Y)], 0)
        hd = hd_ref[span, :]
        if second:
            hd = KEEP * hd - mv_ref[span, :] * inv_ref[0:1, 0:1]
        g = back * gain - columns[:, 0:1] * h_ref[span, :] - columns[:, 1:2] * hd
        g_ref[span, :] = g.astype(BF)
    own_at = pl.multiple_of(place[0] * 256, 256)
    oth_at = pl.multiple_of((1 - place[0]) * 256, 256)
    g_own = g_ref[pl.ds(own_at, 256), :]
    g_oth = g_ref[pl.ds(oth_at, 256), :]
    for zl in range(ZL):
        cols = slice(zl * 256, zl * 256 + 256)
        part = lax.dot_general(
            own_ref[:, :, cols].reshape(256, 256), g_own, CONTRACT0, preferred_element_type=F32
        ) + lax.dot_general(
            oth_ref[:, :, cols].reshape(256, 256), g_oth, CONTRACT0, preferred_element_type=F32
        )
        for x in range(X):
            o_ref[x, zl] = packed(part[x * 64 : x * 64 + 64]).astype(BF)


def swap(x, axis):
    return lax.ppermute(x, axis, [(0, 1), (1, 0)])


def deal(x, axis):
    return lax.all_to_all(x, axis, 0, 0, tiled=True)


def spread(x, axis, n):
    return deal(jnp.broadcast_to(x[None], (n,) + x.shape), axis)


def local(queries, keys, values, stream, out_proj, norm_gain, tag_proj, direction, starts, tags):
    core = lax.axis_index("c")
    ypos = lax.axis_index("y")
    zhpos = lax.axis_index("zh")
    own_at = ((ypos * ZH + zhpos) * C + core) * 32
    oth_at = ((ypos * ZH + 1 - zhpos) * C + core) * 32
    place = jnp.stack([core, own_at, oth_at, zhpos, lax.axis_index("x")]).astype(jnp.int32)
    own_tags = tags[0].reshape(Y, ZH, C, 32).transpose(2, 0, 1, 3).reshape(C * Y, 64)[core * Y + ypos]
    own_tags = own_tags[:, None]
    toks = stream[0].reshape(Y, ZH, C, 32, COLS)
    gain = norm_gain[None]

    by_zl = deal(call(direction_kernel, shape(ZL, 64, WIDE, dtype=BF), direction), "zl")
    pair = call(
        functools.partial(
            attend_kernel,
            scratch=[pltpu.VMEM((SPAN, HK * HD), BF)] * 2 + [pltpu.SemaphoreType.DMA((2,))],
        ),
        shape(Y, ZH, 32, ROWS, dtype=BF),
        place,
        starts,
        keys[0],
        values[0],
        queries[0],
        swap(queries[0], "zh"),
        smem=2,
        far=2,
    )
    u0 = [by_zl] + [
        lax.ppermute(by_zl, "x", [(i, (i + r) % X) for i in range(X)]) for r in range(1, X)
    ]
    own, toks, own_tags, proj, *u0 = lax.optimization_barrier(
        (deal(pair.reshape(Y, 64, ROWS), "y"), toks, own_tags, out_proj, *u0)
    )
    other = swap(own, "c")

    def product(second, *args):
        sent = call(
            functools.partial(product_kernel, second, scratch=[pltpu.VMEM((512, COLS), BF)]),
            shape(X, ZL, PACK, 128, dtype=BF),
            place,
            *args,
            own,
            other,
            gain,
            tag_proj,
            smem=1,
        )
        part = call(sum_x_kernel, shape(ZL, PACK, 128, dtype=BF), deal(sent, "x"))
        return deal(part, "zl")

    def token_sum(load, kernel, outs, *args):
        part = call(sum_parts_kernel, shape(load.shape[1], 128), deal(load, ("c", "y")))
        return call(kernel, outs, part, swap(part, "zh"), *args, own_tags)

    rows_scratch = [pltpu.VMEM((ZL, X, 64, WIDE), BF), pltpu.SemaphoreType.DMA((X + 1,))]
    h_loc, hdot0, load = call(
        functools.partial(first_kernel, scratch=[pltpu.VMEM((ROWS, COLS), BF)] + rows_scratch),
        (shape(512, COLS), shape(512, COLS), shape(8, 136, 128)),
        place,
        proj,
        *u0,
        own,
        other,
        toks,
        gain,
        tag_proj,
        smem=1,
        far=X + 1,
    )
    total, mixed = token_sum(load, tokens0_kernel, (shape(136, 128), shape(8, 72, 128)))
    rows0, sent = call(
        sum_rows_kernel,
        (shape(64, COLS), shape(ZL, 64, WIDE, dtype=BF)),
        product(False, deal(mixed, ("c", "y")), h_loc, hdot0),
    )
    full0 = spread(deal(sent, "zl").reshape(ZL * 64, WIDE), "x", X).reshape(X, ZL, 64, WIDE)
    moved, load = call(
        functools.partial(moved_kernel, scratch=rows_scratch[:1]),
        (shape(512, COLS), shape(8, 72, 128)),
        place,
        full0,
        own,
        other,
        h_loc,
        gain,
        tag_proj,
        smem=1,
    )
    mixed, inv = token_sum(load, tokens1_kernel, (shape(8, 72, 128), shape(8, 128)), total)
    arrived = product(True, deal(mixed, ("c", "y")), h_loc, hdot0, moved, inv)
    return call(last_kernel, shape(64, COLS), arrived, rows0, direction, inv)


def solution(mesh):
    fine = Mesh(mesh.devices.reshape(ZL, X, Y, ZH, C), ("zl", "x", "y", "zh", "c"))
    dp, mp = ("zl", "x"), ("y", "zh", "c")
    return jax.shard_map(
        local,
        mesh=fine,
        in_specs=(
            P(dp, mp, None),
            P(dp, None, None),
            P(dp, None, None),
            P(dp, None, mp),
            P(None, mp),
            P(mp),
            P(mp, None),
            P(dp, mp),
            P(dp, None),
            P(dp, None),
        ),
        out_specs=P(dp, mp),
        check_vma=False,
    )
```

```python
import functools

import jax
import jax.numpy as jnp
from jax import lax
from jax.experimental import pallas as pl
from jax.experimental.pallas import tpu as pltpu
from jax.sharding import Mesh, PartitionSpec as P

D = 3584
HD = 256
HQ = 8
HK = 4
TAGS = 128
WINDOW = 256
DAMP = 0.01
KEEP = 2.0 - DAMP
NORM_EPS = 1e-06
MEAN_EPS = 1e-06
ZL, X, Y, ZH, C = 8, 4, 4, 2, 2
ROWS = HQ * HD
COLS = 224
WIDE = 256
COUNT = HQ * HD * D
SPAN = 352
PACK = 112
BF = jnp.bfloat16
F32 = jnp.float32
CONTRACT0 = (((0,), (0,)), ((), ()))
CONTRACT1 = (((1,), (1,)), ((), ()))


def call(kernel, out_shape, *args, smem=0, far=0):
    specs = [pl.BlockSpec(memory_space=pltpu.SMEM)] * smem
    specs += [pl.BlockSpec(memory_space=pl.ANY)] * far
    args = [
        pltpu.with_memory_space_constraint(a, pltpu.HBM) if smem <= i < smem + far else a
        for i, a in enumerate(args)
    ]
    specs += [pl.BlockSpec(memory_space=pltpu.VMEM)] * (len(args) - smem - far)
    scratch = kernel.keywords.pop("scratch", ()) if isinstance(kernel, functools.partial) else ()
    many = isinstance(out_shape, (tuple, list))
    vmem = pl.BlockSpec(memory_space=pltpu.VMEM)
    return pl.pallas_call(
        kernel,
        out_shape=out_shape,
        in_specs=specs,
        out_specs=[vmem] * len(out_shape) if many else vmem,
        scratch_shapes=scratch,
        compiler_params=pltpu.CompilerParams(vmem_limit_bytes=40 * 2**20),
    )(*args)


def shape(*dims, dtype=F32):
    return jax.ShapeDtypeStruct(dims, dtype)


def dot(a, b):
    return jnp.dot(a, b, preferred_element_type=F32)


def three(x):
    a = x.astype(BF)
    rest = x - a.astype(F32)
    b = rest.astype(BF)
    return a, b, (rest - b.astype(F32)).astype(BF)


def attend_kernel(place, starts, k_far, v_far, own_ref, oth_ref, o_ref, k_ref, v_ref, sems):
    own_at, oth_at, zh = place[1], place[2], place[3]
    first = pl.multiple_of(jnp.maximum(jnp.minimum(own_at, oth_at) - WINDOW, 0), 32)
    k_copy = pltpu.make_async_copy(k_far.at[pl.ds(first, SPAN)], k_ref, sems.at[0])
    v_copy = pltpu.make_async_copy(v_far.at[pl.ds(first, SPAN)], v_ref, sems.at[1])
    k_copy.start()
    v_copy.start()
    row = lax.broadcasted_iota(jnp.int32, (128, 1), 0)
    within = jnp.where(row < 64, row, row - 64)
    q_pos = jnp.where(within < 32, within + own_at, within - 32 + oth_at)
    k_pos = first + lax.broadcasted_iota(jnp.int32, (1, SPAN), 1)
    q_file = jnp.zeros((128, 1), jnp.int32)
    k_file = jnp.zeros((1, SPAN), jnp.int32)
    for f in range(4):
        q_file += jnp.where(starts[0, f] <= q_pos, 1, 0)
        k_file += jnp.where(starts[0, f] <= k_pos, 1, 0)
    allowed = (q_file == k_file) & (k_pos <= q_pos) & (q_pos - k_pos < WINDOW)
    k_copy.wait()
    v_copy.wait()
    for g in range(HK):
        heads = [slice((2 * g + r) * HD, (2 * g + r + 1) * HD) for r in range(2)]
        q = jnp.concatenate([ref[:, head] for head in heads for ref in (own_ref, oth_ref)], 0)
        cols = slice(g * HD, (g + 1) * HD)
        scores = lax.dot_general(q, k_ref[:, cols], CONTRACT1, preferred_element_type=F32)
        scores = 50.0 * jnp.tanh(scores * (1.0 / 16.0) / 50.0)
        expo = jnp.where(allowed, jnp.exp(scores), 0.0)
        weights = (expo / jnp.sum(expo, -1, keepdims=True)).astype(BF)
        out = dot(weights, v_ref[:, cols]).astype(BF)
        for r, head in enumerate(heads):
            for y in range(Y):
                o_ref[y, zh, :, head] = out[r * 64 : r * 64 + 32]
                o_ref[y, 1 - zh, :, head] = out[r * 64 + 32 : r * 64 + 64]


def row_block(block):
    total = jnp.sum(block * block, -1, keepdims=True)
    hi = total.astype(BF)
    lo = (total - hi.astype(F32)).astype(BF)
    lane = lax.broadcasted_iota(jnp.int32, (64, WIDE - COLS), 1)
    tail = jnp.where(lane == 0, hi.astype(F32), jnp.where(lane == 1, lo.astype(F32), 0.0))
    return jnp.concatenate([block, tail], 1).astype(BF)


def packed(block):
    tail = block[:, 128:256]
    lane = lax.broadcasted_iota(jnp.int32, (16, 128), 1)
    parts = [
        jnp.where(lane < 96, tail[16 * i : 16 * i + 16], pltpu.roll(tail[48:64], 96 - 32 * i, 1))
        for i in range(3)
    ]
    return jnp.concatenate([block[:, 0:128], *parts], 0)


def unpacked(block):
    last = jnp.concatenate([block[at : at + 16, 96:128] for at in (64, 80, 96)], 1)
    tail = jnp.concatenate([block[64:112, 0:96], last], 0)
    return jnp.concatenate([block[0:64], tail], 1)


def direction_kernel(d_ref, o_ref):
    load = row_block(d_ref[...])
    for i in range(ZL):
        o_ref[i] = load


def sum_x_kernel(i_ref, o_ref):
    total = i_ref[0].astype(F32)
    for i in range(1, X):
        total += i_ref[i].astype(F32)
    o_ref[...] = total.astype(BF)


def sum_zl(i_ref):
    total = i_ref[0].astype(F32)
    for i in range(1, ZL):
        total += i_ref[i].astype(F32)
    return unpacked(total)


def sum_rows_kernel(i_ref, rows_ref, o_ref):
    total = sum_zl(i_ref)
    rows_ref[...] = total
    load = row_block(total)
    for i in range(ZL):
        o_ref[i] = load


def last_kernel(i_ref, rows_ref, d_ref, inv_ref, o_ref):
    damp = 1.0 - DAMP
    inv = inv_ref[0:1, 0:1]
    o_ref[...] = (1.0 + damp * KEEP) * d_ref[...] - (
        damp * rows_ref[...] + sum_zl(i_ref)
    ) * inv


def turn_kernel(proj_ref, s_ref, oproj_ref, os_ref):
    for i in range(4):
        span = slice(i * 512, i * 512 + 512)
        oproj_ref[span, :] = proj_ref[:, span].astype(F32).T.astype(BF)
    s = s_ref[...].astype(F32).T.astype(BF)
    for i in range(Y * ZH):
        for c in range(C):
            at = (i * C + c) * 32
            os_ref[c, i * 32 : i * 32 + 32, :] = s[at : at + 32]


def start_rows(u_refs, xs, rows_ref, sems):
    copies = [
        pltpu.make_async_copy(u, rows_ref.at[:, x], sems.at[i]) for i, (u, x) in enumerate(zip(u_refs, xs))
    ]
    for copy in copies:
        copy.start()
    return copies


def await_rows(copies, rows_ref):
    for copy in copies:
        copy.wait()
    return (
        rows_ref[...].reshape(ROWS, WIDE),
        jnp.sum(rows_ref[:, :, :, COLS : COLS + 2].astype(F32)),
    )


def scores_of(x, gain, tag_ref):
    return sum(dot(part, tag_ref[...]) for part in three(x * gain))


def put_sums(load_ref, block, row, sums, scalar):
    lane = lax.broadcasted_iota(jnp.int32, (256, 128), 1)
    table = jnp.full((256, 128), scalar, F32)
    for i, s in enumerate(sums):
        table = jnp.where(lane == i, s, table)
    table = table.T
    for i in range(Y):
        load_ref[block + i, row : row + 8, 0:64] = table[0:8, i * 64 : (i + 1) * 64]
        load_ref[block + i, row : row + 8, 64:128] = table[0:8, 0:64]


def first_kernel(
    place, u0, u1, u2, u3, own_ref, oth_ref, proj_ref, s_ref, gain_ref, tag_ref, h_ref, hd_ref, load_ref,
    rows_ref, sems,
):
    xs = [lax.rem(place[4] + X - r, X) for r in range(X)]
    copies = start_rows((u0, u1, u2, u3), xs, rows_ref, sems)
    gain = gain_ref[...]
    halves = []
    for half, a_ref in enumerate((own_ref, oth_ref)):
        c = place[0] if half == 0 else 1 - place[0]
        at = pl.multiple_of(c * 256, 256)
        a = a_ref[...].reshape(256, ROWS)
        h = s_ref[c].astype(F32) + dot(a, proj_ref[...])
        h_ref[pl.ds(at, 256), :] = h
        z = scores_of(h, gain, tag_ref)
        for i in range(Y):
            load_ref[c * Y + i, 0:64, :] = z[i * 64 : i * 64 + 64]
        halves.append((c, at, a_ref))
    rows, norm = await_rows(copies, rows_ref)
    for c, at, a_ref in halves:
        h = h_ref[pl.ds(at, 256), :]
        hd = dot(a_ref[...].reshape(256, ROWS), rows)[:, :COLS]
        hd_ref[pl.ds(at, 256), :] = hd
        zd = scores_of(hd, gain, tag_ref)
        for i in range(Y):
            load_ref[c * Y + i, 64:128, :] = zd[i * 64 : i * 64 + 64]
        sums = (jnp.sum(h * h, -1, keepdims=True), jnp.sum(h * hd, -1, keepdims=True))
        put_sums(load_ref, c * Y, 128, sums, norm)


def moved_kernel(
    place, u_ref, own_ref, oth_ref, h_ref, gain_ref, tag_ref, mv_ref, load_ref, rows_ref
):
    for x in range(X):
        rows_ref[:, x] = u_ref[x]
    rows, norm = await_rows((), rows_ref)
    gain = gain_ref[...]
    for half, a_ref in enumerate((own_ref, oth_ref)):
        c = place[0] if half == 0 else 1 - place[0]
        at = pl.multiple_of(c * 256, 256)
        moved = dot(a_ref[...].reshape(256, ROWS), rows)[:, :COLS]
        mv_ref[pl.ds(at, 256), :] = moved
        z = scores_of(moved, gain, tag_ref)
        for i in range(Y):
            load_ref[c * Y + i, 0:64, :] = z[i * 64 : i * 64 + 64]
        sums = (jnp.sum(h_ref[pl.ds(at, 256), :] * moved, -1, keepdims=True),)
        put_sums(load_ref, c * Y, 64, sums, norm)


def sum_parts_kernel(i_ref, o_ref):
    total = i_ref[0]
    for i in range(1, 8):
        total += i_ref[i]
    o_ref[...] = total


def columns_of(rows):
    return jnp.concatenate([rows, jnp.zeros((120, 128), F32)], 0).T[:64]


def backward(zval, sumsq, tags, along, zdot, o_ref):
    rscale = lax.rsqrt(sumsq / D + NORM_EPS)
    tanh_val = jnp.tanh(rscale * zval / 30.0)
    slope = 1.0 - tanh_val * tanh_val
    expo = jnp.exp(30.0 * tanh_val)
    probs = expo / jnp.sum(expo, -1, keepdims=True)
    onehot = (tags == lax.broadcasted_iota(jnp.int32, (64, TAGS), 1)).astype(F32)
    dlogit = probs - onehot
    wgrad = dlogit * slope
    rho = jnp.sum(wgrad * zval, -1, keepdims=True)
    cube = rscale * rscale * rscale / D
    rdot = -cube * along
    mdot = rdot * zval + rscale * zdot
    ldot = slope * mdot
    pdot = probs * (ldot - jnp.sum(probs * ldot, -1, keepdims=True))
    wdot = pdot * slope - dlogit * 2.0 * tanh_val * slope * mdot / 30.0
    rhodot = jnp.sum(wdot * zval + wgrad * zdot, -1, keepdims=True)
    mixed = rdot * wgrad + rscale * wdot
    coeff = rhodot * cube + 3.0 * rho * rscale * rscale * rdot / D
    lane = lax.broadcasted_iota(jnp.int32, (64, 128), 1)
    table = jnp.where(lane == 0, coeff, jnp.where(lane == 1, rho * cube, 0.0))
    tail = jnp.concatenate([table, jnp.zeros((64, 128), F32)], 0).T[0:8]
    for i in range(8):
        o_ref[i, 0:64, :] = mixed
        o_ref[i, 64:72, :] = tail


def tokens0_kernel(mine_ref, their_ref, tag_ref, total_ref, o_ref):
    total_ref[...] = mine_ref[...] + their_ref[...]
    columns = columns_of(total_ref[128:136, :])
    backward(
        total_ref[0:64, :], columns[:, 0:1], tag_ref[...], columns[:, 1:2], total_ref[64:128, :], o_ref
    )


def tokens1_kernel(mine_ref, their_ref, total_ref, tag_ref, o_ref, inv_ref):
    moved = mine_ref[...] + their_ref[...]
    product_sq = moved[65:66, 0:1]
    norm_sq = total_ref[130:131, 0:1]
    sigma = 2.0 * jnp.sqrt((product_sq / COUNT + MEAN_EPS) / (norm_sq / COUNT + MEAN_EPS))
    inv = 1.0 / sigma
    inv_ref[...] = jnp.broadcast_to(inv, (8, 128))
    columns0 = columns_of(total_ref[128:136, :])
    columns1 = columns_of(moved[64:72])
    along = KEEP * columns0[:, 1:2] - columns1[:, 0:1] * inv
    zdot = KEEP * total_ref[64:128, :] - moved[0:64] * inv
    backward(total_ref[0:64, :], columns0[:, 0:1], tag_ref[...], along, zdot, o_ref)


def product_kernel(second, place, m_ref, h_ref, hd_ref, *rest):
    if second:
        mv_ref, inv_ref, *rest = rest
    own_ref, oth_ref, gain_ref, tag_ref, o_ref, g_ref = rest
    gain = gain_ref[...]
    for c in range(C):
        span = slice(c * 256, c * 256 + 256)
        mixed = jnp.concatenate([m_ref[c * Y + i, 0:64, :] for i in range(Y)], 0)
        back = sum(
            lax.dot_general(part, tag_ref[...], CONTRACT1, preferred_element_type=F32)
            for part in three(mixed)
        )
        columns = jnp.concatenate([columns_of(m_ref[c * Y + i, 64:72, :]) for i in range(Y)], 0)
        hd = hd_ref[span, :]
        if second:
            hd = KEEP * hd - mv_ref[span, :] * inv_ref[0:1, 0:1]
        g = back * gain - columns[:, 0:1] * h_ref[span, :] - columns[:, 1:2] * hd
        g_ref[span, 0:COLS] = g.astype(BF)
        g_ref[span, COLS:WIDE] = jnp.zeros((256, WIDE - COLS), BF)
    own_at = pl.multiple_of(place[0] * 256, 256)
    oth_at = pl.multiple_of((1 - place[0]) * 256, 256)
    g_own = g_ref[pl.ds(own_at, 256), :]
    g_oth = g_ref[pl.ds(oth_at, 256), :]
    for zl in range(ZL):
        cols = slice(zl * 256, zl * 256 + 256)
        part = lax.dot_general(
            own_ref[:, :, cols].reshape(256, 256), g_own, CONTRACT0, preferred_element_type=F32
        ) + lax.dot_general(
            oth_ref[:, :, cols].reshape(256, 256), g_oth, CONTRACT0, preferred_element_type=F32
        )
        for x in range(X):
            o_ref[x, zl] = packed(part[x * 64 : x * 64 + 64]).astype(BF)


def swap(x, axis):
    return lax.ppermute(x, axis, [(0, 1), (1, 0)])


def deal(x, axis):
    return lax.all_to_all(x, axis, 0, 0, tiled=True)


def spread(x, axis, n):
    return deal(jnp.broadcast_to(x[None], (n,) + x.shape), axis)


def local(queries, keys, values, stream, out_proj, norm_gain, tag_proj, direction, starts, tags):
    core = lax.axis_index("c")
    ypos = lax.axis_index("y")
    zhpos = lax.axis_index("zh")
    own_at = ((ypos * ZH + zhpos) * C + core) * 32
    oth_at = ((ypos * ZH + 1 - zhpos) * C + core) * 32
    place = jnp.stack([core, own_at, oth_at, zhpos, lax.axis_index("x")]).astype(jnp.int32)
    own_tags = tags[0].reshape(Y, ZH, C, 32).transpose(2, 0, 1, 3).reshape(C * Y, 64)[core * Y + ypos]
    own_tags = own_tags[:, None]
    gain = norm_gain[None]

    by_zl = deal(call(direction_kernel, shape(ZL, 64, WIDE, dtype=BF), direction), "zl")
    proj, toks = call(
        turn_kernel,
        (shape(ROWS, COLS, dtype=BF), shape(C, 256, COLS, dtype=BF)),
        out_proj.T,
        stream[0].T,
    )
    theirs, proj, toks, own_tags = lax.optimization_barrier(
        (swap(queries[0], "zh"), proj, toks, own_tags)
    )
    pair = call(
        functools.partial(
            attend_kernel,
            scratch=[pltpu.VMEM((SPAN, HK * HD), BF)] * 2 + [pltpu.SemaphoreType.DMA((2,))],
        ),
        shape(Y, ZH, 32, ROWS, dtype=BF),
        place,
        starts,
        keys[0],
        values[0],
        queries[0],
        theirs,
        smem=2,
        far=2,
    )
    u0 = [by_zl] + [
        lax.ppermute(by_zl, "x", [(i, (i + r) % X) for i in range(X)]) for r in range(1, X)
    ]
    own, *u0 = lax.optimization_barrier((deal(pair.reshape(Y, 64, ROWS), "y"), *u0))
    other = swap(own, "c")

    def product(second, *args):
        sent = call(
            functools.partial(product_kernel, second, scratch=[pltpu.VMEM((512, WIDE), BF)]),
            shape(X, ZL, PACK, 128, dtype=BF),
            place,
            *args,
            own,
            other,
            gain,
            tag_proj,
            smem=1,
        )
        part = call(sum_x_kernel, shape(ZL, PACK, 128, dtype=BF), deal(sent, "x"))
        return deal(part, "zl")

    def token_sum(load, kernel, outs, *args):
        part = call(sum_parts_kernel, shape(load.shape[1], 128), deal(load, ("c", "y")))
        return call(kernel, outs, part, swap(part, "zh"), *args, own_tags)

    rows_scratch = [pltpu.VMEM((ZL, X, 64, WIDE), BF), pltpu.SemaphoreType.DMA((X,))]
    h_loc, hdot0, load = call(
        functools.partial(first_kernel, scratch=rows_scratch),
        (shape(512, COLS), shape(512, COLS), shape(8, 136, 128)),
        place,
        *u0,
        own,
        other,
        proj,
        toks,
        gain,
        tag_proj,
        smem=1,
        far=X,
    )
    total, mixed = token_sum(load, tokens0_kernel, (shape(136, 128), shape(8, 72, 128)))
    rows0, sent = call(
        sum_rows_kernel,
        (shape(64, COLS), shape(ZL, 64, WIDE, dtype=BF)),
        product(False, deal(mixed, ("c", "y")), h_loc, hdot0),
    )
    full0 = spread(deal(sent, "zl").reshape(ZL * 64, WIDE), "x", X).reshape(X, ZL, 64, WIDE)
    moved, load = call(
        functools.partial(moved_kernel, scratch=rows_scratch[:1]),
        (shape(512, COLS), shape(8, 72, 128)),
        place,
        full0,
        own,
        other,
        h_loc,
        gain,
        tag_proj,
        smem=1,
    )
    mixed, inv = token_sum(load, tokens1_kernel, (shape(8, 72, 128), shape(8, 128)), total)
    arrived = product(True, deal(mixed, ("c", "y")), h_loc, hdot0, moved, inv)
    return call(last_kernel, shape(64, COLS), arrived, rows0, direction, inv)


def solution(mesh):
    fine = Mesh(mesh.devices.reshape(ZL, X, Y, ZH, C), ("zl", "x", "y", "zh", "c"))
    dp, mp = ("zl", "x"), ("y", "zh", "c")
    return jax.shard_map(
        local,
        mesh=fine,
        in_specs=(
            P(dp, mp, None),
            P(dp, None, None),
            P(dp, None, None),
            P(dp, None, mp),
            P(None, mp),
            P(mp),
            P(mp, None),
            P(dp, mp),
            P(dp, None),
            P(dp, None),
        ),
        out_specs=P(dp, mp),
        check_vma=False,
    )
```

```python
import functools

import jax
import jax.numpy as jnp
from jax import lax
from jax.experimental import pallas as pl
from jax.experimental.pallas import tpu as pltpu
from jax.sharding import Mesh, PartitionSpec as P

D = 3584
HD = 256
HQ = 8
HK = 4
TAGS = 128
WINDOW = 256
DAMP = 0.01
KEEP = 2.0 - DAMP
NORM_EPS = 1e-06
MEAN_EPS = 1e-06
ZL, X, Y, ZH, C = 8, 4, 4, 2, 2
ROWS = HQ * HD
COLS = 224
WIDE = 256
COUNT = HQ * HD * D
SPAN = 352
PACK = 112
BF = jnp.bfloat16
F32 = jnp.float32
CONTRACT0 = (((0,), (0,)), ((), ()))
CONTRACT1 = (((1,), (1,)), ((), ()))


def call(kernel, out_shape, *args, smem=0, far=0):
    specs = [pl.BlockSpec(memory_space=pltpu.SMEM)] * smem
    specs += [pl.BlockSpec(memory_space=pl.ANY)] * far
    args = [
        pltpu.with_memory_space_constraint(a, pltpu.HBM) if smem <= i < smem + far else a
        for i, a in enumerate(args)
    ]
    specs += [pl.BlockSpec(memory_space=pltpu.VMEM)] * (len(args) - smem - far)
    scratch = kernel.keywords.pop("scratch", ()) if isinstance(kernel, functools.partial) else ()
    many = isinstance(out_shape, (tuple, list))
    vmem = pl.BlockSpec(memory_space=pltpu.VMEM)
    return pl.pallas_call(
        kernel,
        out_shape=out_shape,
        in_specs=specs,
        out_specs=[vmem] * len(out_shape) if many else vmem,
        scratch_shapes=scratch,
        compiler_params=pltpu.CompilerParams(vmem_limit_bytes=40 * 2**20),
    )(*args)


def shape(*dims, dtype=F32):
    return jax.ShapeDtypeStruct(dims, dtype)


def dot(a, b):
    return jnp.dot(a, b, preferred_element_type=F32)


def three(x):
    a = x.astype(BF)
    rest = x - a.astype(F32)
    b = rest.astype(BF)
    return a, b, (rest - b.astype(F32)).astype(BF)


def attend_kernel(place, starts, k_far, v_far, own_ref, oth_ref, o_ref, k_ref, v_ref, sems):
    own_at, oth_at, zh = place[1], place[2], place[3]
    first = pl.multiple_of(jnp.maximum(jnp.minimum(own_at, oth_at) - WINDOW, 0), 32)
    k_copy = pltpu.make_async_copy(k_far.at[pl.ds(first, SPAN)], k_ref, sems.at[0])
    v_copy = pltpu.make_async_copy(v_far.at[pl.ds(first, SPAN)], v_ref, sems.at[1])
    k_copy.start()
    v_copy.start()
    row = lax.broadcasted_iota(jnp.int32, (128, 1), 0)
    within = jnp.where(row < 64, row, row - 64)
    q_pos = jnp.where(within < 32, within + own_at, within - 32 + oth_at)
    k_pos = first + lax.broadcasted_iota(jnp.int32, (1, SPAN), 1)
    q_file = jnp.zeros((128, 1), jnp.int32)
    k_file = jnp.zeros((1, SPAN), jnp.int32)
    for f in range(4):
        q_file += jnp.where(starts[0, f] <= q_pos, 1, 0)
        k_file += jnp.where(starts[0, f] <= k_pos, 1, 0)
    allowed = (q_file == k_file) & (k_pos <= q_pos) & (q_pos - k_pos < WINDOW)
    k_copy.wait()
    v_copy.wait()
    for g in range(HK):
        heads = [slice((2 * g + r) * HD, (2 * g + r + 1) * HD) for r in range(2)]
        q = jnp.concatenate([ref[:, head] for head in heads for ref in (own_ref, oth_ref)], 0)
        cols = slice(g * HD, (g + 1) * HD)
        scores = lax.dot_general(q, k_ref[:, cols], CONTRACT1, preferred_element_type=F32)
        scores = 50.0 * jnp.tanh(scores * (1.0 / 16.0) / 50.0)
        expo = jnp.where(allowed, jnp.exp(scores), 0.0)
        weights = (expo / jnp.sum(expo, -1, keepdims=True)).astype(BF)
        out = dot(weights, v_ref[:, cols])
        for x in range(X):
            span = slice(x * 64, x * 64 + 64)
            both = jnp.concatenate([out[0:64, span], out[64:128, span]], 1).astype(BF)
            at = x * 512 + g * 128
            for y in range(Y):
                o_ref[y, zh, :, at : at + 128] = both[0:32]
                o_ref[y, 1 - zh, :, at : at + 128] = both[32:64]


def row_block(block):
    total = jnp.sum(block * block, -1, keepdims=True)
    hi = total.astype(BF)
    lo = (total - hi.astype(F32)).astype(BF)
    lane = lax.broadcasted_iota(jnp.int32, (64, WIDE - COLS), 1)
    tail = jnp.where(lane == 0, hi.astype(F32), jnp.where(lane == 1, lo.astype(F32), 0.0))
    return jnp.concatenate([block, tail], 1).astype(BF)


def packed(block):
    tail = block[:, 128:256]
    lane = lax.broadcasted_iota(jnp.int32, (16, 128), 1)
    parts = [
        jnp.where(lane < 96, tail[16 * i : 16 * i + 16], pltpu.roll(tail[48:64], 96 - 32 * i, 1))
        for i in range(3)
    ]
    return jnp.concatenate([block[:, 0:128], *parts], 0)


def unpacked(block):
    last = jnp.concatenate([block[at : at + 16, 96:128] for at in (64, 80, 96)], 1)
    tail = jnp.concatenate([block[64:112, 0:96], last], 0)
    return jnp.concatenate([block[0:64], tail], 1)


def direction_kernel(d_ref, o_ref):
    load = row_block(d_ref[...])
    for i in range(ZL):
        o_ref[i] = load


def sum_x_kernel(i_ref, o_ref):
    total = i_ref[0].astype(F32)
    for i in range(1, X):
        total += i_ref[i].astype(F32)
    o_ref[...] = total.astype(BF)


def sum_zl(i_ref):
    total = i_ref[0].astype(F32)
    for i in range(1, ZL):
        total += i_ref[i].astype(F32)
    return unpacked(total)


def sum_rows_kernel(i_ref, rows_ref, o_ref):
    total = sum_zl(i_ref)
    rows_ref[...] = total
    load = row_block(total)
    for i in range(ZL):
        o_ref[i] = load


def last_kernel(i_ref, rows_ref, d_ref, inv_ref, o_ref):
    damp = 1.0 - DAMP
    inv = inv_ref[0:1, 0:1]
    o_ref[...] = (1.0 + damp * KEEP) * d_ref[...] - (
        damp * rows_ref[...] + sum_zl(i_ref)
    ) * inv


def turn_kernel(proj_ref, s_ref, oproj_ref, os_ref):
    for i in range(4):
        span = slice(i * 512, i * 512 + 512)
        rows = proj_ref[:, span].astype(F32).T.astype(BF)
        for j in range(8):
            at = (j % X) * 512 + (2 * i + j // X) * 64
            oproj_ref[at : at + 64, :] = rows[j * 64 : j * 64 + 64]
    s = s_ref[...].astype(F32).T.astype(BF)
    for i in range(Y * ZH):
        for c in range(C):
            at = (i * C + c) * 32
            os_ref[c, i * 32 : i * 32 + 32, :] = s[at : at + 32]


def square_of(rows):
    return jnp.sum(rows[:, COLS : COLS + 2].astype(F32))


def scores_of(x, gain, tag_ref):
    return sum(dot(part, tag_ref[...]) for part in three(x * gain))


def two(x):
    hi = x.astype(BF).astype(F32)
    return hi, (x - hi).astype(BF).astype(F32)


def rows_of(columns, count):
    lane = lax.broadcasted_iota(jnp.int32, (count, 128), 1)
    table = jnp.zeros((count, 128), F32)
    for i, column in enumerate(columns):
        hi, lo = two(column)
        table = jnp.where(lane == 2 * i, hi, jnp.where(lane == 2 * i + 1, lo, table))
    if count < 128:
        table = jnp.concatenate([table, jnp.zeros((128 - count, 128), F32)], 0)
    return table.T[0:16]


def put_scores(load_ref, block, row, z):
    for i in range(Y):
        load_ref[block + i, row : row + 64, :] = z[i * 64 : i * 64 + 64].astype(BF)


def put_sums(load_ref, block, row, sums, scalar):
    rows = rows_of((*sums, jnp.full((256, 1), scalar, F32)), 256)
    for i in range(Y):
        own = rows[:, i * 64 : i * 64 + 64]
        load_ref[block + i, row : row + 16, :] = jnp.concatenate([own, own], 1).astype(BF)


def first_kernel(
    place, proj_far, u0, u1, u2, u3, own_ref, oth_ref, s_ref, gain_ref, tag_ref, h_ref, hd_ref, load_ref,
    proj_ref, rows_ref, sems,
):
    copies = []
    for r in range(X):
        span = pl.ds(r * 512, 512)
        copies.append(pltpu.make_async_copy(proj_far.at[span], proj_ref.at[span], sems.at[r]))
    for r, u in enumerate((u0, u1, u2, u3)):
        copies.append(pltpu.make_async_copy(u, rows_ref.at[r], sems.at[X + r]))
    for copy in copies:
        copy.start()
    gain = gain_ref[...]
    halves = []
    for half, a_ref in enumerate((own_ref, oth_ref)):
        c = place[0] if half == 0 else 1 - place[0]
        halves.append((c, pl.multiple_of(c * 256, 256), a_ref))
    hs = [s_ref[c].astype(F32) for c, _, _ in halves]
    for r in range(X):
        copies[r].wait()
        span = slice(r * 512, r * 512 + 512)
        for i, (_, _, a_ref) in enumerate(halves):
            hs[i] += dot(a_ref[:, :, span].reshape(256, 512), proj_ref[span, :])
    for h, (c, at, _) in zip(hs, halves):
        h_ref[pl.ds(at, 256), :] = h
        z = scores_of(h, gain, tag_ref)
        z_hi = z.astype(BF).astype(F32)
        put_scores(load_ref, c * Y, 0, z_hi)
        put_scores(load_ref, c * Y, 64, z - z_hi)
    hds = [jnp.zeros((256, WIDE), F32)] * 2
    norm = 0.0
    for r in range(X):
        copies[X + r].wait()
        x = lax.rem(place[4] + X - r, X)
        span = pl.ds(pl.multiple_of(x * 512, 512), 512)
        norm += square_of(rows_ref[r])
        for i, (_, _, a_ref) in enumerate(halves):
            hds[i] += dot(a_ref[:, :, span].reshape(256, 512), rows_ref[r])
    for h, hd, (c, at, _) in zip(hs, hds, halves):
        hd = hd[:, :COLS]
        hd_ref[pl.ds(at, 256), :] = hd
        put_scores(load_ref, c * Y, 128, scores_of(hd, gain, tag_ref))
        sums = (jnp.sum(h * h, -1, keepdims=True), jnp.sum(h * hd, -1, keepdims=True))
        put_sums(load_ref, c * Y, 192, sums, norm)


def moved_kernel(place, u_ref, own_ref, oth_ref, h_ref, gain_ref, tag_ref, mv_ref, load_ref):
    norm = square_of(u_ref[...])
    gain = gain_ref[...]
    for half, a_ref in enumerate((own_ref, oth_ref)):
        c = place[0] if half == 0 else 1 - place[0]
        at = pl.multiple_of(c * 256, 256)
        moved = dot(a_ref[...].reshape(256, ROWS), u_ref[...])[:, :COLS]
        mv_ref[pl.ds(at, 256), :] = moved
        put_scores(load_ref, c * Y, 0, scores_of(moved, gain, tag_ref))
        sums = (jnp.sum(h_ref[pl.ds(at, 256), :] * moved, -1, keepdims=True),)
        put_sums(load_ref, c * Y, 64, sums, norm)


def sum_parts_kernel(i_ref, o_ref):
    total = i_ref[0].astype(F32)
    for i in range(1, 8):
        total += i_ref[i].astype(F32)
    scores = total[: total.shape[0] - 16]
    if scores.shape[0] == 192:
        scores = jnp.concatenate([scores[0:64] + scores[64:128], scores[128:192]], 0)
    sums = total[total.shape[0] - 16 :]
    joined = [sums[2 * i : 2 * i + 1] + sums[2 * i + 1 : 2 * i + 2] for i in range(8)]
    o_ref[...] = jnp.concatenate([scores, *joined], 0)


def columns_of(rows):
    return jnp.concatenate([rows, jnp.zeros((120, 128), F32)], 0).T[:64]


def backward(zval, sumsq, tags, along, zdot, o_ref):
    rscale = lax.rsqrt(sumsq / D + NORM_EPS)
    tanh_val = jnp.tanh(rscale * zval / 30.0)
    slope = 1.0 - tanh_val * tanh_val
    expo = jnp.exp(30.0 * tanh_val)
    probs = expo / jnp.sum(expo, -1, keepdims=True)
    onehot = (tags == lax.broadcasted_iota(jnp.int32, (64, TAGS), 1)).astype(F32)
    dlogit = probs - onehot
    wgrad = dlogit * slope
    rho = jnp.sum(wgrad * zval, -1, keepdims=True)
    cube = rscale * rscale * rscale / D
    rdot = -cube * along
    mdot = rdot * zval + rscale * zdot
    ldot = slope * mdot
    pdot = probs * (ldot - jnp.sum(probs * ldot, -1, keepdims=True))
    wdot = pdot * slope - dlogit * 2.0 * tanh_val * slope * mdot / 30.0
    rhodot = jnp.sum(wdot * zval + wgrad * zdot, -1, keepdims=True)
    mixed = rdot * wgrad + rscale * wdot
    coeff = rhodot * cube + 3.0 * rho * rscale * rscale * rdot / D
    mixed = mixed.astype(BF)
    tail = rows_of((coeff, rho * cube), 64).astype(BF)
    for i in range(8):
        o_ref[i, 0:64, :] = mixed
        o_ref[i, 64:80, :] = tail


def tokens0_kernel(mine_ref, their_ref, tag_ref, total_ref, o_ref):
    total_ref[...] = mine_ref[...] + their_ref[...]
    columns = columns_of(total_ref[128:136, :])
    backward(
        total_ref[0:64, :], columns[:, 0:1], tag_ref[...], columns[:, 1:2], total_ref[64:128, :], o_ref
    )


def tokens1_kernel(mine_ref, their_ref, total_ref, tag_ref, o_ref, inv_ref):
    moved = mine_ref[...] + their_ref[...]
    product_sq = moved[65:66, 0:1]
    norm_sq = total_ref[130:131, 0:1]
    sigma = 2.0 * jnp.sqrt((product_sq / COUNT + MEAN_EPS) / (norm_sq / COUNT + MEAN_EPS))
    inv = 1.0 / sigma
    inv_ref[...] = jnp.broadcast_to(inv, (8, 128))
    columns0 = columns_of(total_ref[128:136, :])
    columns1 = columns_of(moved[64:72])
    along = KEEP * columns0[:, 1:2] - columns1[:, 0:1] * inv
    zdot = KEEP * total_ref[64:128, :] - moved[0:64] * inv
    backward(total_ref[0:64, :], columns0[:, 0:1], tag_ref[...], along, zdot, o_ref)


def product_kernel(second, place, m_ref, h_ref, hd_ref, *rest):
    if second:
        mv_ref, inv_ref, *rest = rest
    own_ref, oth_ref, gain_ref, tag_ref, o_ref, g_ref = rest
    gain = gain_ref[...]
    for c in range(C):
        span = slice(c * 256, c * 256 + 256)
        mixed = jnp.concatenate([m_ref[c * Y + i, 0:64, :] for i in range(Y)], 0)
        back = lax.dot_general(mixed, tag_ref[...], CONTRACT1, preferred_element_type=F32)
        columns = jnp.concatenate(
            [columns_of(m_ref[c * Y + i, 64:80, :].astype(F32)[0:8]) for i in range(Y)], 0
        )
        coeff, cubed = columns[:, 0:1] + columns[:, 1:2], columns[:, 2:3] + columns[:, 3:4]
        hd = hd_ref[span, :]
        if second:
            hd = KEEP * hd - mv_ref[span, :] * inv_ref[0:1, 0:1]
        g = back * gain - coeff * h_ref[span, :] - cubed * hd
        g_ref[span, 0:COLS] = g.astype(BF)
        g_ref[span, COLS:WIDE] = jnp.zeros((256, WIDE - COLS), BF)
    own_at = pl.multiple_of(place[0] * 256, 256)
    oth_at = pl.multiple_of((1 - place[0]) * 256, 256)
    g_own = g_ref[pl.ds(own_at, 256), :]
    g_oth = g_ref[pl.ds(oth_at, 256), :]
    for j in range(8):
        cols = slice(j * 256, j * 256 + 256)
        part = lax.dot_general(
            own_ref[:, :, cols].reshape(256, 256), g_own, CONTRACT0, preferred_element_type=F32
        ) + lax.dot_general(
            oth_ref[:, :, cols].reshape(256, 256), g_oth, CONTRACT0, preferred_element_type=F32
        )
        for i in range(4):
            o_ref[j // 2, (j % 2) * 4 + i] = packed(part[i * 64 : i * 64 + 64]).astype(BF)


def swap(x, axis):
    return lax.ppermute(x, axis, [(0, 1), (1, 0)])


def deal(x, axis):
    return lax.all_to_all(x, axis, 0, 0, tiled=True)


def spread(x, axis, n):
    return deal(jnp.broadcast_to(x[None], (n,) + x.shape), axis)


def local(queries, keys, values, stream, out_proj, norm_gain, tag_proj, direction, starts, tags):
    core = lax.axis_index("c")
    ypos = lax.axis_index("y")
    zhpos = lax.axis_index("zh")
    own_at = ((ypos * ZH + zhpos) * C + core) * 32
    oth_at = ((ypos * ZH + 1 - zhpos) * C + core) * 32
    place = jnp.stack([core, own_at, oth_at, zhpos, lax.axis_index("x")]).astype(jnp.int32)
    own_tags = tags[0].reshape(Y, ZH, C, 32).transpose(2, 0, 1, 3).reshape(C * Y, 64)[core * Y + ypos]
    own_tags = own_tags[:, None]
    gain = norm_gain[None]

    by_zl = deal(call(direction_kernel, shape(ZL, 64, WIDE, dtype=BF), direction), "zl")
    by_zl = by_zl.reshape(ZL * 64, WIDE)
    proj, toks = call(
        turn_kernel,
        (shape(ROWS, COLS, dtype=BF), shape(C, 256, COLS, dtype=BF)),
        out_proj.T,
        stream[0].T,
    )
    theirs, proj, toks, own_tags = lax.optimization_barrier(
        (swap(queries[0], "zh"), proj, toks, own_tags)
    )
    pair = call(
        functools.partial(
            attend_kernel,
            scratch=[pltpu.VMEM((SPAN, HK * HD), BF)] * 2 + [pltpu.SemaphoreType.DMA((2,))],
        ),
        shape(Y, ZH, 32, ROWS, dtype=BF),
        place,
        starts,
        keys[0],
        values[0],
        queries[0],
        theirs,
        smem=2,
        far=2,
    )
    u0 = [by_zl] + [
        lax.ppermute(by_zl, "x", [(i, (i + r) % X) for i in range(X)]) for r in range(1, X)
    ]
    own, *u0 = lax.optimization_barrier((deal(pair.reshape(Y, 64, ROWS), "y"), *u0))
    other = swap(own, "c")

    def product(second, *args):
        sent = call(
            functools.partial(product_kernel, second, scratch=[pltpu.VMEM((512, WIDE), BF)]),
            shape(X, ZL, PACK, 128, dtype=BF),
            place,
            *args,
            own,
            other,
            gain,
            tag_proj,
            smem=1,
        )
        part = call(sum_x_kernel, shape(ZL, PACK, 128, dtype=BF), deal(sent, "x"))
        return deal(part, "zl")

    def token_sum(load, rows, kernel, outs, *args):
        part = call(sum_parts_kernel, shape(rows, 128), deal(load, ("c", "y")))
        return call(kernel, outs, part, swap(part, "zh"), *args, own_tags)

    h_loc, hdot0, load = call(
        functools.partial(
            first_kernel,
            scratch=[
                pltpu.VMEM((ROWS, COLS), BF),
                pltpu.VMEM((X, ZL * 64, WIDE), BF),
                pltpu.SemaphoreType.DMA((2 * X,)),
            ],
        ),
        (shape(512, COLS), shape(512, COLS), shape(8, 208, 128, dtype=BF)),
        place,
        proj,
        *u0,
        own,
        other,
        toks,
        gain,
        tag_proj,
        smem=1,
        far=X + 1,
    )
    total, mixed = token_sum(load, 136, tokens0_kernel, (shape(136, 128), shape(8, 80, 128, dtype=BF)))
    rows0, sent = call(
        sum_rows_kernel,
        (shape(64, COLS), shape(ZL, 64, WIDE, dtype=BF)),
        product(False, deal(mixed, ("c", "y")), h_loc, hdot0),
    )
    full0 = spread(deal(sent, "zl").reshape(ZL * 64, WIDE), "x", X).reshape(ROWS, WIDE)
    moved, load = call(
        moved_kernel,
        (shape(512, COLS), shape(8, 80, 128, dtype=BF)),
        place,
        full0,
        own,
        other,
        h_loc,
        gain,
        tag_proj,
        smem=1,
    )
    mixed, inv = token_sum(
        load, 72, tokens1_kernel, (shape(8, 80, 128, dtype=BF), shape(8, 128)), total
    )
    arrived = product(True, deal(mixed, ("c", "y")), h_loc, hdot0, moved, inv)
    return call(last_kernel, shape(64, COLS), arrived, rows0, direction, inv)


def solution(mesh):
    fine = Mesh(mesh.devices.reshape(ZL, X, Y, ZH, C), ("zl", "x", "y", "zh", "c"))
    dp, mp = ("zl", "x"), ("y", "zh", "c")
    return jax.shard_map(
        local,
        mesh=fine,
        in_specs=(
            P(dp, mp, None),
            P(dp, None, None),
            P(dp, None, None),
            P(dp, None, mp),
            P(None, mp),
            P(mp),
            P(mp, None),
            P(dp, mp),
            P(dp, None),
            P(dp, None),
        ),
        out_specs=P(dp, mp),
        check_vma=False,
    )
```

```python
import functools

import jax
import jax.numpy as jnp
from jax import lax
from jax.experimental import pallas as pl
from jax.experimental.pallas import tpu as pltpu
from jax.sharding import Mesh, PartitionSpec as P

D = 3584
HD = 256
HQ = 8
HK = 4
TAGS = 128
WINDOW = 256
DAMP = 0.01
KEEP = 2.0 - DAMP
NORM_EPS = 1e-06
MEAN_EPS = 1e-06
ZL, X, Y, ZH, C = 8, 4, 4, 2, 2
ZA, ZB = 2, 4
ROWS = HQ * HD
COLS = 224
WIDE = 256
COUNT = HQ * HD * D
SPAN = 352
PACK = 112
BF = jnp.bfloat16
F32 = jnp.float32
ZAXES = ("za", "zb")
CONTRACT0 = (((0,), (0,)), ((), ()))
CONTRACT1 = (((1,), (1,)), ((), ()))


def call(kernel, out_shape, *args, smem=0, far=0):
    specs = [pl.BlockSpec(memory_space=pltpu.SMEM)] * smem
    specs += [pl.BlockSpec(memory_space=pl.ANY)] * far
    args = [
        pltpu.with_memory_space_constraint(a, pltpu.HBM) if smem <= i < smem + far else a
        for i, a in enumerate(args)
    ]
    specs += [pl.BlockSpec(memory_space=pltpu.VMEM)] * (len(args) - smem - far)
    scratch = kernel.keywords.pop("scratch", ()) if isinstance(kernel, functools.partial) else ()
    many = isinstance(out_shape, (tuple, list))
    vmem = pl.BlockSpec(memory_space=pltpu.VMEM)
    return pl.pallas_call(
        kernel,
        out_shape=out_shape,
        in_specs=specs,
        out_specs=[vmem] * len(out_shape) if many else vmem,
        scratch_shapes=scratch,
        compiler_params=pltpu.CompilerParams(vmem_limit_bytes=40 * 2**20),
    )(*args)


def shape(*dims, dtype=F32):
    return jax.ShapeDtypeStruct(dims, dtype)


def dot(a, b):
    return jnp.dot(a, b, preferred_element_type=F32)


def three(x):
    a = x.astype(BF)
    rest = x - a.astype(F32)
    b = rest.astype(BF)
    return a, b, (rest - b.astype(F32)).astype(BF)


def attend_kernel(place, starts, k_far, v_far, own_ref, oth_ref, o_ref, k_ref, v_ref, sems):
    own_at, oth_at, zh = place[1], place[2], place[3]
    first = pl.multiple_of(jnp.maximum(jnp.minimum(own_at, oth_at) - WINDOW, 0), 32)
    k_copy = pltpu.make_async_copy(k_far.at[pl.ds(first, SPAN)], k_ref, sems.at[0])
    v_copy = pltpu.make_async_copy(v_far.at[pl.ds(first, SPAN)], v_ref, sems.at[1])
    k_copy.start()
    v_copy.start()
    row = lax.broadcasted_iota(jnp.int32, (128, 1), 0)
    within = jnp.where(row < 64, row, row - 64)
    q_pos = jnp.where(within < 32, within + own_at, within - 32 + oth_at)
    k_pos = first + lax.broadcasted_iota(jnp.int32, (1, SPAN), 1)
    q_file = jnp.zeros((128, 1), jnp.int32)
    k_file = jnp.zeros((1, SPAN), jnp.int32)
    for f in range(4):
        q_file += jnp.where(starts[0, f] <= q_pos, 1, 0)
        k_file += jnp.where(starts[0, f] <= k_pos, 1, 0)
    allowed = (q_file == k_file) & (k_pos <= q_pos) & (q_pos - k_pos < WINDOW)
    k_copy.wait()
    v_copy.wait()
    for g in range(HK):
        heads = [slice((2 * g + r) * HD, (2 * g + r + 1) * HD) for r in range(2)]
        q = jnp.concatenate([ref[:, head] for head in heads for ref in (own_ref, oth_ref)], 0)
        cols = slice(g * HD, (g + 1) * HD)
        scores = lax.dot_general(q, k_ref[:, cols], CONTRACT1, preferred_element_type=F32)
        scores = 50.0 * jnp.tanh(scores * (1.0 / 16.0) / 50.0)
        expo = jnp.where(allowed, jnp.exp(scores), 0.0)
        weights = (expo / jnp.sum(expo, -1, keepdims=True)).astype(BF)
        out = dot(weights, v_ref[:, cols])
        for x in range(X):
            span = slice(x * 64, x * 64 + 64)
            both = jnp.concatenate([out[0:64, span], out[64:128, span]], 1).astype(BF)
            at = x * 512 + g * 128
            for y in range(Y):
                o_ref[y, zh, :, at : at + 128] = both[0:32]
                o_ref[y, 1 - zh, :, at : at + 128] = both[32:64]


def row_block(block):
    total = jnp.sum(block * block, -1, keepdims=True)
    hi = total.astype(BF)
    lo = (total - hi.astype(F32)).astype(BF)
    lane = lax.broadcasted_iota(jnp.int32, (64, WIDE - COLS), 1)
    tail = jnp.where(lane == 0, hi.astype(F32), jnp.where(lane == 1, lo.astype(F32), 0.0))
    return jnp.concatenate([block, tail], 1).astype(BF)


def packed(block):
    tail = block[:, 128:256]
    lane = lax.broadcasted_iota(jnp.int32, (16, 128), 1)
    parts = [
        jnp.where(lane < 96, tail[16 * i : 16 * i + 16], pltpu.roll(tail[48:64], 96 - 32 * i, 1))
        for i in range(3)
    ]
    return jnp.concatenate([block[:, 0:128], *parts], 0)


def unpacked(block):
    last = jnp.concatenate([block[at : at + 16, 96:128] for at in (64, 80, 96)], 1)
    tail = jnp.concatenate([block[64:112, 0:96], last], 0)
    return jnp.concatenate([block[0:64], tail], 1)


def direction_kernel(d_ref, o_ref):
    o_ref[...] = row_block(d_ref[...])


def pair_kernel(place, mine_ref, their_ref, o_ref):
    za = place[5]
    for i in range(ZB):
        o_ref[i, za] = mine_ref[...]
        o_ref[i, 1 - za] = their_ref[...]


def sum_x_kernel(i_ref, o_ref):
    total = i_ref[0].astype(F32)
    for i in range(1, X):
        total += i_ref[i].astype(F32)
    o_ref[...] = total.astype(BF)


def sum_zl(i_ref):
    total = i_ref[0].astype(F32)
    for i in range(1, ZL):
        total += i_ref[i].astype(F32)
    return unpacked(total)


def sum_rows_kernel(i_ref, rows_ref, o_ref):
    total = sum_zl(i_ref)
    rows_ref[...] = total
    load = row_block(total)
    for i in range(ZL):
        o_ref[i] = load


def last_kernel(i_ref, rows_ref, d_ref, inv_ref, o_ref):
    damp = 1.0 - DAMP
    inv = inv_ref[0:1, 0:1]
    o_ref[...] = (1.0 + damp * KEEP) * d_ref[...] - (
        damp * rows_ref[...] + sum_zl(i_ref)
    ) * inv


def turn_kernel(proj_ref, s_ref, oproj_ref, os_ref):
    for i in range(4):
        span = slice(i * 512, i * 512 + 512)
        rows = proj_ref[:, span].astype(F32).T.astype(BF)
        for j in range(8):
            at = (j % X) * 512 + (2 * i + j // X) * 64
            oproj_ref[at : at + 64, :] = rows[j * 64 : j * 64 + 64]
    s = s_ref[...].astype(F32).T.astype(BF)
    for i in range(Y * ZH):
        for c in range(C):
            at = (i * C + c) * 32
            os_ref[c, i * 32 : i * 32 + 32, :] = s[at : at + 32]


def square_of(rows):
    return jnp.sum(rows[:, COLS : COLS + 2].astype(F32))


def scores_of(x, gain, tag_ref):
    return sum(dot(part, tag_ref[...]) for part in three(x * gain))


def two(x):
    hi = x.astype(BF).astype(F32)
    return hi, (x - hi).astype(BF).astype(F32)


def rows_of(columns, count):
    lane = lax.broadcasted_iota(jnp.int32, (count, 128), 1)
    table = jnp.zeros((count, 128), F32)
    for i, column in enumerate(columns):
        hi, lo = two(column)
        table = jnp.where(lane == 2 * i, hi, jnp.where(lane == 2 * i + 1, lo, table))
    if count < 128:
        table = jnp.concatenate([table, jnp.zeros((128 - count, 128), F32)], 0)
    return table.T[0:16]


def put_scores(load_ref, block, row, z):
    for i in range(Y):
        load_ref[block + i, row : row + 64, :] = z[i * 64 : i * 64 + 64].astype(BF)


def put_sums(load_ref, block, row, sums, scalar):
    rows = rows_of((*sums, jnp.full((256, 1), scalar, F32)), 256)
    for i in range(Y):
        own = rows[:, i * 64 : i * 64 + 64]
        load_ref[block + i, row : row + 16, :] = jnp.concatenate([own, own], 1).astype(BF)


def first_kernel(
    place, proj_far, u0, u1, u2, u3, own_ref, oth_ref, s_ref, gain_ref, tag_ref, h_ref, hd_ref, load_ref,
    proj_ref, rows_ref, sems,
):
    copies = []
    for r in range(X):
        span = pl.ds(r * 512, 512)
        copies.append(pltpu.make_async_copy(proj_far.at[span], proj_ref.at[span], sems.at[r]))
    for r, u in enumerate((u0, u1, u2, u3)):
        for za in range(ZA):
            copies.append(
                pltpu.make_async_copy(u.at[:, za], rows_ref.at[r, za], sems.at[X + ZA * r + za])
            )
    for copy in copies:
        copy.start()
    gain = gain_ref[...]
    halves = []
    for half, a_ref in enumerate((own_ref, oth_ref)):
        c = place[0] if half == 0 else 1 - place[0]
        halves.append((c, pl.multiple_of(c * 256, 256), a_ref))
    hs = [s_ref[c].astype(F32) for c, _, _ in halves]
    for r in range(X):
        copies[r].wait()
        span = slice(r * 512, r * 512 + 512)
        for i, (_, _, a_ref) in enumerate(halves):
            hs[i] += dot(a_ref[:, :, span].reshape(256, 512), proj_ref[span, :])
    for h, (c, at, _) in zip(hs, halves):
        h_ref[pl.ds(at, 256), :] = h
        z = scores_of(h, gain, tag_ref)
        z_hi = z.astype(BF).astype(F32)
        put_scores(load_ref, c * Y, 0, z_hi)
        put_scores(load_ref, c * Y, 64, z - z_hi)
    hds = [jnp.zeros((256, WIDE), F32)] * 2
    norm = 0.0
    for r in range(X):
        copies[X + ZA * r].wait()
        copies[X + ZA * r + 1].wait()
        rows = rows_ref[r].reshape(512, WIDE)
        x = lax.rem(place[4] + X - r, X)
        span = pl.ds(pl.multiple_of(x * 512, 512), 512)
        norm += square_of(rows)
        for i, (_, _, a_ref) in enumerate(halves):
            hds[i] += dot(a_ref[:, :, span].reshape(256, 512), rows)
    for h, hd, (c, at, _) in zip(hs, hds, halves):
        hd = hd[:, :COLS]
        hd_ref[pl.ds(at, 256), :] = hd
        put_scores(load_ref, c * Y, 128, scores_of(hd, gain, tag_ref))
        sums = (jnp.sum(h * h, -1, keepdims=True), jnp.sum(h * hd, -1, keepdims=True))
        put_sums(load_ref, c * Y, 192, sums, norm)


def moved_kernel(place, u_ref, own_ref, oth_ref, h_ref, gain_ref, tag_ref, mv_ref, load_ref):
    norm = square_of(u_ref[...])
    gain = gain_ref[...]
    for half, a_ref in enumerate((own_ref, oth_ref)):
        c = place[0] if half == 0 else 1 - place[0]
        at = pl.multiple_of(c * 256, 256)
        moved = dot(a_ref[...].reshape(256, ROWS), u_ref[...])[:, :COLS]
        mv_ref[pl.ds(at, 256), :] = moved
        put_scores(load_ref, c * Y, 0, scores_of(moved, gain, tag_ref))
        sums = (jnp.sum(h_ref[pl.ds(at, 256), :] * moved, -1, keepdims=True),)
        put_sums(load_ref, c * Y, 64, sums, norm)


def sum_parts_kernel(i_ref, o_ref):
    total = i_ref[0].astype(F32)
    for i in range(1, 8):
        total += i_ref[i].astype(F32)
    scores = total[: total.shape[0] - 16]
    if scores.shape[0] == 192:
        scores = jnp.concatenate([scores[0:64] + scores[64:128], scores[128:192]], 0)
    sums = total[total.shape[0] - 16 :]
    joined = [sums[2 * i : 2 * i + 1] + sums[2 * i + 1 : 2 * i + 2] for i in range(8)]
    o_ref[...] = jnp.concatenate([scores, *joined], 0)


def columns_of(rows):
    return jnp.concatenate([rows, jnp.zeros((120, 128), F32)], 0).T[:64]


def backward(zval, sumsq, tags, along, zdot, o_ref):
    rscale = lax.rsqrt(sumsq / D + NORM_EPS)
    tanh_val = jnp.tanh(rscale * zval / 30.0)
    slope = 1.0 - tanh_val * tanh_val
    expo = jnp.exp(30.0 * tanh_val)
    probs = expo / jnp.sum(expo, -1, keepdims=True)
    onehot = (tags == lax.broadcasted_iota(jnp.int32, (64, TAGS), 1)).astype(F32)
    dlogit = probs - onehot
    wgrad = dlogit * slope
    rho = jnp.sum(wgrad * zval, -1, keepdims=True)
    cube = rscale * rscale * rscale / D
    rdot = -cube * along
    mdot = rdot * zval + rscale * zdot
    ldot = slope * mdot
    pdot = probs * (ldot - jnp.sum(probs * ldot, -1, keepdims=True))
    wdot = pdot * slope - dlogit * 2.0 * tanh_val * slope * mdot / 30.0
    rhodot = jnp.sum(wdot * zval + wgrad * zdot, -1, keepdims=True)
    mixed = rdot * wgrad + rscale * wdot
    coeff = rhodot * cube + 3.0 * rho * rscale * rscale * rdot / D
    mixed = mixed.astype(BF)
    tail = rows_of((coeff, rho * cube), 64).astype(BF)
    for i in range(8):
        o_ref[i, 0:64, :] = mixed
        o_ref[i, 64:80, :] = tail


def tokens0_kernel(mine_ref, their_ref, tag_ref, total_ref, o_ref):
    total_ref[...] = mine_ref[...] + their_ref[...]
    columns = columns_of(total_ref[128:136, :])
    backward(
        total_ref[0:64, :], columns[:, 0:1], tag_ref[...], columns[:, 1:2], total_ref[64:128, :], o_ref
    )


def tokens1_kernel(mine_ref, their_ref, total_ref, tag_ref, o_ref, inv_ref):
    moved = mine_ref[...] + their_ref[...]
    product_sq = moved[65:66, 0:1]
    norm_sq = total_ref[130:131, 0:1]
    sigma = 2.0 * jnp.sqrt((product_sq / COUNT + MEAN_EPS) / (norm_sq / COUNT + MEAN_EPS))
    inv = 1.0 / sigma
    inv_ref[...] = jnp.broadcast_to(inv, (8, 128))
    columns0 = columns_of(total_ref[128:136, :])
    columns1 = columns_of(moved[64:72])
    along = KEEP * columns0[:, 1:2] - columns1[:, 0:1] * inv
    zdot = KEEP * total_ref[64:128, :] - moved[0:64] * inv
    backward(total_ref[0:64, :], columns0[:, 0:1], tag_ref[...], along, zdot, o_ref)


def product_kernel(second, place, m_ref, h_ref, hd_ref, *rest):
    if second:
        mv_ref, inv_ref, *rest = rest
    own_ref, oth_ref, gain_ref, tag_ref, o_ref, g_ref = rest
    gain = gain_ref[...]
    for c in range(C):
        span = slice(c * 256, c * 256 + 256)
        mixed = jnp.concatenate([m_ref[c * Y + i, 0:64, :] for i in range(Y)], 0)
        back = lax.dot_general(mixed, tag_ref[...], CONTRACT1, preferred_element_type=F32)
        columns = jnp.concatenate(
            [columns_of(m_ref[c * Y + i, 64:80, :].astype(F32)[0:8]) for i in range(Y)], 0
        )
        coeff, cubed = columns[:, 0:1] + columns[:, 1:2], columns[:, 2:3] + columns[:, 3:4]
        hd = hd_ref[span, :]
        if second:
            hd = KEEP * hd - mv_ref[span, :] * inv_ref[0:1, 0:1]
        g = back * gain - coeff * h_ref[span, :] - cubed * hd
        g_ref[span, 0:COLS] = g.astype(BF)
        g_ref[span, COLS:WIDE] = jnp.zeros((256, WIDE - COLS), BF)
    own_at = pl.multiple_of(place[0] * 256, 256)
    oth_at = pl.multiple_of((1 - place[0]) * 256, 256)
    g_own = g_ref[pl.ds(own_at, 256), :]
    g_oth = g_ref[pl.ds(oth_at, 256), :]
    for j in range(8):
        cols = slice(j * 256, j * 256 + 256)
        part = lax.dot_general(
            own_ref[:, :, cols].reshape(256, 256), g_own, CONTRACT0, preferred_element_type=F32
        ) + lax.dot_general(
            oth_ref[:, :, cols].reshape(256, 256), g_oth, CONTRACT0, preferred_element_type=F32
        )
        for i in range(4):
            o_ref[j // 2, (j % 2) * 4 + i] = packed(part[i * 64 : i * 64 + 64]).astype(BF)


def swap(x, axis):
    return lax.ppermute(x, axis, [(0, 1), (1, 0)])


def deal(x, axis):
    return lax.all_to_all(x, axis, 0, 0, tiled=True)


def spread(x, axis, n):
    return deal(jnp.broadcast_to(x[None], (n,) + x.shape), axis)


def local(queries, keys, values, stream, out_proj, norm_gain, tag_proj, direction, starts, tags):
    core = lax.axis_index("c")
    ypos = lax.axis_index("y")
    zhpos = lax.axis_index("zh")
    own_at = ((ypos * ZH + zhpos) * C + core) * 32
    oth_at = ((ypos * ZH + 1 - zhpos) * C + core) * 32
    place = jnp.stack([core, own_at, oth_at, zhpos, lax.axis_index("x"), lax.axis_index("za")]).astype(jnp.int32)
    own_tags = tags[0].reshape(Y, ZH, C, 32).transpose(2, 0, 1, 3).reshape(C * Y, 64)[core * Y + ypos]
    own_tags = own_tags[:, None]
    gain = norm_gain[None]

    row = call(direction_kernel, shape(64, WIDE, dtype=BF), direction)
    proj, toks = call(
        turn_kernel,
        (shape(ROWS, COLS, dtype=BF), shape(C, 256, COLS, dtype=BF)),
        out_proj.T,
        stream[0].T,
    )
    theirs, far, proj, toks, own_tags = lax.optimization_barrier(
        (swap(queries[0], "zh"), swap(row, "za"), proj, toks, own_tags)
    )
    pairs = call(pair_kernel, shape(ZB, ZA, 64, WIDE, dtype=BF), place, row, far, smem=1)
    by_zl = deal(pairs, "zb")
    pair = call(
        functools.partial(
            attend_kernel,
            scratch=[pltpu.VMEM((SPAN, HK * HD), BF)] * 2 + [pltpu.SemaphoreType.DMA((2,))],
        ),
        shape(Y, ZH, 32, ROWS, dtype=BF),
        place,
        starts,
        keys[0],
        values[0],
        queries[0],
        theirs,
        smem=2,
        far=2,
    )
    u0 = [by_zl] + [
        lax.ppermute(by_zl, "x", [(i, (i + r) % X) for i in range(X)]) for r in range(1, X)
    ]
    own, *u0 = lax.optimization_barrier((deal(pair.reshape(Y, 64, ROWS), "y"), *u0))
    other = swap(own, "c")

    def product(second, *args):
        sent = call(
            functools.partial(product_kernel, second, scratch=[pltpu.VMEM((512, WIDE), BF)]),
            shape(X, ZL, PACK, 128, dtype=BF),
            place,
            *args,
            own,
            other,
            gain,
            tag_proj,
            smem=1,
        )
        part = call(sum_x_kernel, shape(ZL, PACK, 128, dtype=BF), deal(sent, "x"))
        return deal(part, ZAXES)

    def token_sum(load, rows, kernel, outs, *args):
        part = call(sum_parts_kernel, shape(rows, 128), deal(load, ("c", "y")))
        return call(kernel, outs, part, swap(part, "zh"), *args, own_tags)

    h_loc, hdot0, load = call(
        functools.partial(
            first_kernel,
            scratch=[
                pltpu.VMEM((ROWS, COLS), BF),
                pltpu.VMEM((X, ZA, ZB, 64, WIDE), BF),
                pltpu.SemaphoreType.DMA((3 * X,)),
            ],
        ),
        (shape(512, COLS), shape(512, COLS), shape(8, 208, 128, dtype=BF)),
        place,
        proj,
        *u0,
        own,
        other,
        toks,
        gain,
        tag_proj,
        smem=1,
        far=X + 1,
    )
    total, mixed = token_sum(load, 136, tokens0_kernel, (shape(136, 128), shape(8, 80, 128, dtype=BF)))
    rows0, sent = call(
        sum_rows_kernel,
        (shape(64, COLS), shape(ZL, 64, WIDE, dtype=BF)),
        product(False, deal(mixed, ("c", "y")), h_loc, hdot0),
    )
    full0 = spread(deal(sent, ZAXES).reshape(ZL * 64, WIDE), "x", X).reshape(ROWS, WIDE)
    moved, load = call(
        moved_kernel,
        (shape(512, COLS), shape(8, 80, 128, dtype=BF)),
        place,
        full0,
        own,
        other,
        h_loc,
        gain,
        tag_proj,
        smem=1,
    )
    mixed, inv = token_sum(
        load, 72, tokens1_kernel, (shape(8, 80, 128, dtype=BF), shape(8, 128)), total
    )
    arrived = product(True, deal(mixed, ("c", "y")), h_loc, hdot0, moved, inv)
    return call(last_kernel, shape(64, COLS), arrived, rows0, direction, inv)


def solution(mesh):
    fine = Mesh(mesh.devices.reshape(ZA, ZB, X, Y, ZH, C), ("za", "zb", "x", "y", "zh", "c"))
    dp, mp = ("za", "zb", "x"), ("y", "zh", "c")
    return jax.shard_map(
        local,
        mesh=fine,
        in_specs=(
            P(dp, mp, None),
            P(dp, None, None),
            P(dp, None, None),
            P(dp, None, mp),
            P(None, mp),
            P(mp),
            P(mp, None),
            P(dp, mp),
            P(dp, None),
            P(dp, None),
        ),
        out_specs=P(dp, mp),
        check_vma=False,
    )
```

```python
import functools

import jax
import jax.numpy as jnp
from jax import lax
from jax.experimental import pallas as pl
from jax.experimental.pallas import tpu as pltpu
from jax.sharding import Mesh, PartitionSpec as P

D = 3584
HD = 256
HQ = 8
HK = 4
TAGS = 128
WINDOW = 256
DAMP = 0.01
KEEP = 2.0 - DAMP
NORM_EPS = 1e-06
MEAN_EPS = 1e-06
ZL, X, Y, ZH, C = 8, 4, 4, 2, 2
ZA, ZB = 2, 4
ROWS = HQ * HD
COLS = 224
WIDE = 256
COUNT = HQ * HD * D
SPAN = 352
PACK = 112
BF = jnp.bfloat16
F32 = jnp.float32
ZAXES = ("za", "zb")
CONTRACT0 = (((0,), (0,)), ((), ()))
CONTRACT1 = (((1,), (1,)), ((), ()))


def call(kernel, out_shape, *args, smem=0, far=0):
    specs = [pl.BlockSpec(memory_space=pltpu.SMEM)] * smem
    specs += [pl.BlockSpec(memory_space=pl.ANY)] * far
    args = [
        pltpu.with_memory_space_constraint(a, pltpu.HBM) if smem <= i < smem + far else a
        for i, a in enumerate(args)
    ]
    specs += [pl.BlockSpec(memory_space=pltpu.VMEM)] * (len(args) - smem - far)
    scratch = kernel.keywords.pop("scratch", ()) if isinstance(kernel, functools.partial) else ()
    many = isinstance(out_shape, (tuple, list))
    vmem = pl.BlockSpec(memory_space=pltpu.VMEM)
    return pl.pallas_call(
        kernel,
        out_shape=out_shape,
        in_specs=specs,
        out_specs=[vmem] * len(out_shape) if many else vmem,
        scratch_shapes=scratch,
        compiler_params=pltpu.CompilerParams(vmem_limit_bytes=40 * 2**20),
    )(*args)


def shape(*dims, dtype=F32):
    return jax.ShapeDtypeStruct(dims, dtype)


def dot(a, b):
    return jnp.dot(a, b, preferred_element_type=F32)


def three(x):
    a = x.astype(BF)
    rest = x - a.astype(F32)
    b = rest.astype(BF)
    return a, b, (rest - b.astype(F32)).astype(BF)


def attend_kernel(place, starts, k_far, v_far, own_ref, oth_ref, o_ref, k_ref, v_ref, sems):
    own_at, oth_at, zh = place[1], place[2], place[3]
    first = pl.multiple_of(jnp.maximum(jnp.minimum(own_at, oth_at) - WINDOW, 0), 32)
    k_copy = pltpu.make_async_copy(k_far.at[pl.ds(first, SPAN)], k_ref, sems.at[0])
    v_copy = pltpu.make_async_copy(v_far.at[pl.ds(first, SPAN)], v_ref, sems.at[1])
    k_copy.start()
    v_copy.start()
    row = lax.broadcasted_iota(jnp.int32, (128, 1), 0)
    within = jnp.where(row < 64, row, row - 64)
    q_pos = jnp.where(within < 32, within + own_at, within - 32 + oth_at)
    k_pos = first + lax.broadcasted_iota(jnp.int32, (1, SPAN), 1)
    q_file = jnp.zeros((128, 1), jnp.int32)
    k_file = jnp.zeros((1, SPAN), jnp.int32)
    for f in range(4):
        q_file += jnp.where(starts[0, f] <= q_pos, 1, 0)
        k_file += jnp.where(starts[0, f] <= k_pos, 1, 0)
    allowed = (q_file == k_file) & (k_pos <= q_pos) & (q_pos - k_pos < WINDOW)
    k_copy.wait()
    v_copy.wait()
    for g in range(HK):
        heads = [slice((2 * g + r) * HD, (2 * g + r + 1) * HD) for r in range(2)]
        q = jnp.concatenate([ref[:, head] for head in heads for ref in (own_ref, oth_ref)], 0)
        cols = slice(g * HD, (g + 1) * HD)
        scores = lax.dot_general(q, k_ref[:, cols], CONTRACT1, preferred_element_type=F32)
        scores = 50.0 * jnp.tanh(scores * (1.0 / 16.0) / 50.0)
        expo = jnp.where(allowed, jnp.exp(scores), 0.0)
        weights = (expo / jnp.sum(expo, -1, keepdims=True)).astype(BF)
        out = dot(weights, v_ref[:, cols])
        for x in range(X):
            span = slice(x * 64, x * 64 + 64)
            both = jnp.concatenate([out[0:64, span], out[64:128, span]], 1).astype(BF)
            at = x * 512 + g * 128
            for y in range(Y):
                o_ref[y, zh, :, at : at + 128] = both[0:32]
                o_ref[y, 1 - zh, :, at : at + 128] = both[32:64]


def row_block(block):
    total = jnp.sum(block * block, -1, keepdims=True)
    hi = total.astype(BF)
    lo = (total - hi.astype(F32)).astype(BF)
    lane = lax.broadcasted_iota(jnp.int32, (64, WIDE - COLS), 1)
    tail = jnp.where(lane == 0, hi.astype(F32), jnp.where(lane == 1, lo.astype(F32), 0.0))
    return jnp.concatenate([block, tail], 1).astype(BF)


def packed(block):
    tail = block[:, 128:256]
    lane = lax.broadcasted_iota(jnp.int32, (16, 128), 1)
    parts = [
        jnp.where(lane < 96, tail[16 * i : 16 * i + 16], pltpu.roll(tail[48:64], 96 - 32 * i, 1))
        for i in range(3)
    ]
    return jnp.concatenate([block[:, 0:128], *parts], 0)


def unpacked(block):
    last = jnp.concatenate([block[at : at + 16, 96:128] for at in (64, 80, 96)], 1)
    tail = jnp.concatenate([block[64:112, 0:96], last], 0)
    return jnp.concatenate([block[0:64], tail], 1)


def direction_kernel(d_ref, o_ref):
    o_ref[...] = row_block(d_ref[...])


def pair_kernel(place, mine_ref, their_ref, o_ref):
    za = place[5]
    for i in range(ZB):
        o_ref[i, za] = mine_ref[...]
        o_ref[i, 1 - za] = their_ref[...]


def sum_x_kernel(i_ref, o_ref):
    total = i_ref[0].astype(F32)
    for i in range(1, X):
        total += i_ref[i].astype(F32)
    o_ref[...] = total.astype(BF)


def sum_zl(i_ref):
    total = i_ref[0].astype(F32)
    for i in range(1, ZL):
        total += i_ref[i].astype(F32)
    return unpacked(total)


def sum_rows_kernel(i_ref, rows_ref, o_ref):
    total = sum_zl(i_ref)
    rows_ref[...] = total
    load = row_block(total)
    for i in range(ZL):
        o_ref[i] = load


def last_kernel(i_ref, rows_ref, d_ref, inv_ref, o_ref):
    damp = 1.0 - DAMP
    inv = inv_ref[0:1, 0:1]
    o_ref[...] = (1.0 + damp * KEEP) * d_ref[...] - (
        damp * rows_ref[...] + sum_zl(i_ref)
    ) * inv


def turn_kernel(proj_ref, s_ref, oproj_ref, os_ref):
    for i in range(4):
        span = slice(i * 512, i * 512 + 512)
        rows = proj_ref[:, span].astype(F32).T.astype(BF)
        for j in range(8):
            at = (j % X) * 512 + (2 * i + j // X) * 64
            oproj_ref[at : at + 64, :] = rows[j * 64 : j * 64 + 64]
    s = s_ref[...].astype(F32).T.astype(BF)
    for i in range(Y * ZH):
        for c in range(C):
            at = (i * C + c) * 32
            os_ref[c, i * 32 : i * 32 + 32, :] = s[at : at + 32]


def square_of(rows):
    return jnp.sum(rows[:, COLS : COLS + 2].astype(F32))


def scores_of(x, gain, tag_ref):
    return sum(dot(part, tag_ref[...]) for part in three(x * gain))


def two(x):
    hi = x.astype(BF).astype(F32)
    return hi, (x - hi).astype(BF).astype(F32)


def rows_of(columns, count):
    lane = lax.broadcasted_iota(jnp.int32, (count, 128), 1)
    table = jnp.zeros((count, 128), F32)
    for i, column in enumerate(columns):
        hi, lo = two(column)
        table = jnp.where(lane == 2 * i, hi, jnp.where(lane == 2 * i + 1, lo, table))
    if count < 128:
        table = jnp.concatenate([table, jnp.zeros((128 - count, 128), F32)], 0)
    return table.T[0:16]


def put_scores(load_ref, block, row, z):
    for i in range(Y):
        load_ref[block + i, row : row + 64, :] = z[i * 64 : i * 64 + 64].astype(BF)


def put_sums(load_ref, block, row, sums, scalar):
    rows = rows_of((*sums, jnp.full((256, 1), scalar, F32)), 256)
    for i in range(Y):
        own = rows[:, i * 64 : i * 64 + 64]
        load_ref[block + i, row : row + 16, :] = jnp.concatenate([own, own], 1).astype(BF)


def first_kernel(
    place, proj_far, u0, u1, u2, u3, own_ref, oth_ref, s_ref, gain_ref, tag_ref, h_ref, hd_ref, load_ref,
    proj_ref, rows_ref, sems,
):
    copies = []
    for r in range(X):
        span = pl.ds(r * 512, 512)
        copies.append(pltpu.make_async_copy(proj_far.at[span], proj_ref.at[span], sems.at[r]))
    for r, u in enumerate((u0, u1, u2, u3)):
        for za in range(ZA):
            copies.append(
                pltpu.make_async_copy(u.at[:, za], rows_ref.at[r, za], sems.at[X + ZA * r + za])
            )
    for copy in copies:
        copy.start()
    gain = gain_ref[...]
    halves = []
    for half, a_ref in enumerate((own_ref, oth_ref)):
        c = place[0] if half == 0 else 1 - place[0]
        halves.append((c, pl.multiple_of(c * 256, 256), a_ref))
    hs = [s_ref[c].astype(F32) for c, _, _ in halves]
    for r in range(X):
        copies[r].wait()
        span = slice(r * 512, r * 512 + 512)
        for i, (_, _, a_ref) in enumerate(halves):
            hs[i] += dot(a_ref[:, :, span].reshape(256, 512), proj_ref[span, :])
    for h, (c, at, _) in zip(hs, halves):
        h_ref[pl.ds(at, 256), :] = h
        z = scores_of(h, gain, tag_ref)
        z_hi = z.astype(BF).astype(F32)
        put_scores(load_ref, c * Y, 0, z_hi)
        put_scores(load_ref, c * Y, 64, z - z_hi)
    hds = [jnp.zeros((256, WIDE), F32)] * 2
    norm = 0.0
    for r in range(X):
        copies[X + ZA * r].wait()
        copies[X + ZA * r + 1].wait()
        rows = rows_ref[r].reshape(512, WIDE)
        x = lax.rem(place[4] + X - r, X)
        span = pl.ds(pl.multiple_of(x * 512, 512), 512)
        norm += square_of(rows)
        for i, (_, _, a_ref) in enumerate(halves):
            hds[i] += dot(a_ref[:, :, span].reshape(256, 512), rows)
    for h, hd, (c, at, _) in zip(hs, hds, halves):
        hd = hd[:, :COLS]
        hd_ref[pl.ds(at, 256), :] = hd
        put_scores(load_ref, c * Y, 128, scores_of(hd, gain, tag_ref))
        sums = (jnp.sum(h * h, -1, keepdims=True), jnp.sum(h * hd, -1, keepdims=True))
        put_sums(load_ref, c * Y, 192, sums, norm)


def moved_kernel(place, u_ref, own_ref, oth_ref, h_ref, gain_ref, tag_ref, mv_ref, load_ref):
    norm = square_of(u_ref[...])
    gain = gain_ref[...]
    for half, a_ref in enumerate((own_ref, oth_ref)):
        c = place[0] if half == 0 else 1 - place[0]
        at = pl.multiple_of(c * 256, 256)
        moved = dot(a_ref[...].reshape(256, ROWS), u_ref[...])[:, :COLS]
        mv_ref[pl.ds(at, 256), :] = moved
        z = scores_of(moved, gain, tag_ref)
        sums = (jnp.sum(h_ref[pl.ds(at, 256), :] * moved, -1, keepdims=True),)
        for zh in range(ZH):
            put_scores(load_ref, (zh * C + c) * Y, 0, z)
            put_sums(load_ref, (zh * C + c) * Y, 64, sums, norm)


def sum_parts(i_ref):
    total = i_ref[0].astype(F32)
    for i in range(1, i_ref.shape[0]):
        total += i_ref[i].astype(F32)
    scores = total[: total.shape[0] - 16]
    if scores.shape[0] == 192:
        scores = jnp.concatenate([scores[0:64] + scores[64:128], scores[128:192]], 0)
    sums = total[total.shape[0] - 16 :]
    joined = [sums[2 * i : 2 * i + 1] + sums[2 * i + 1 : 2 * i + 2] for i in range(8)]
    return jnp.concatenate([scores, *joined], 0)


def sum_parts_kernel(i_ref, o_ref):
    o_ref[...] = sum_parts(i_ref)


def columns_of(rows):
    return jnp.concatenate([rows, jnp.zeros((120, 128), F32)], 0).T[:64]


def backward(zval, sumsq, tags, along, zdot, o_ref):
    rscale = lax.rsqrt(sumsq / D + NORM_EPS)
    tanh_val = jnp.tanh(rscale * zval / 30.0)
    slope = 1.0 - tanh_val * tanh_val
    expo = jnp.exp(30.0 * tanh_val)
    probs = expo / jnp.sum(expo, -1, keepdims=True)
    onehot = (tags == lax.broadcasted_iota(jnp.int32, (64, TAGS), 1)).astype(F32)
    dlogit = probs - onehot
    wgrad = dlogit * slope
    rho = jnp.sum(wgrad * zval, -1, keepdims=True)
    cube = rscale * rscale * rscale / D
    rdot = -cube * along
    mdot = rdot * zval + rscale * zdot
    ldot = slope * mdot
    pdot = probs * (ldot - jnp.sum(probs * ldot, -1, keepdims=True))
    wdot = pdot * slope - dlogit * 2.0 * tanh_val * slope * mdot / 30.0
    rhodot = jnp.sum(wdot * zval + wgrad * zdot, -1, keepdims=True)
    mixed = rdot * wgrad + rscale * wdot
    coeff = rhodot * cube + 3.0 * rho * rscale * rscale * rdot / D
    mixed = mixed.astype(BF)
    tail = rows_of((coeff, rho * cube), 64).astype(BF)
    for i in range(8):
        o_ref[i, 0:64, :] = mixed
        o_ref[i, 64:80, :] = tail


def tokens0_kernel(mine_ref, their_ref, tag_ref, total_ref, o_ref):
    total_ref[...] = mine_ref[...] + their_ref[...]
    columns = columns_of(total_ref[128:136, :])
    backward(
        total_ref[0:64, :], columns[:, 0:1], tag_ref[...], columns[:, 1:2], total_ref[64:128, :], o_ref
    )


def tokens1_kernel(i_ref, total_ref, tag_ref, o_ref, inv_ref):
    moved = sum_parts(i_ref)
    product_sq = moved[65:66, 0:1]
    norm_sq = total_ref[130:131, 0:1]
    sigma = 2.0 * jnp.sqrt((product_sq / COUNT + MEAN_EPS) / (norm_sq / COUNT + MEAN_EPS))
    inv = 1.0 / sigma
    inv_ref[...] = jnp.broadcast_to(inv, (8, 128))
    columns0 = columns_of(total_ref[128:136, :])
    columns1 = columns_of(moved[64:72])
    along = KEEP * columns0[:, 1:2] - columns1[:, 0:1] * inv
    zdot = KEEP * total_ref[64:128, :] - moved[0:64] * inv
    backward(total_ref[0:64, :], columns0[:, 0:1], tag_ref[...], along, zdot, o_ref)


def product_kernel(second, place, m_ref, h_ref, hd_ref, *rest):
    if second:
        mv_ref, inv_ref, *rest = rest
    own_ref, oth_ref, gain_ref, tag_ref, o_ref, g_ref = rest
    gain = gain_ref[...]
    for c in range(C):
        span = slice(c * 256, c * 256 + 256)
        mixed = jnp.concatenate([m_ref[c * Y + i, 0:64, :] for i in range(Y)], 0)
        back = lax.dot_general(mixed, tag_ref[...], CONTRACT1, preferred_element_type=F32)
        columns = jnp.concatenate(
            [columns_of(m_ref[c * Y + i, 64:80, :].astype(F32)[0:8]) for i in range(Y)], 0
        )
        coeff, cubed = columns[:, 0:1] + columns[:, 1:2], columns[:, 2:3] + columns[:, 3:4]
        hd = hd_ref[span, :]
        if second:
            hd = KEEP * hd - mv_ref[span, :] * inv_ref[0:1, 0:1]
        g = back * gain - coeff * h_ref[span, :] - cubed * hd
        g_ref[span, 0:COLS] = g.astype(BF)
        g_ref[span, COLS:WIDE] = jnp.zeros((256, WIDE - COLS), BF)
    own_at = pl.multiple_of(place[0] * 256, 256)
    oth_at = pl.multiple_of((1 - place[0]) * 256, 256)
    g_own = g_ref[pl.ds(own_at, 256), :]
    g_oth = g_ref[pl.ds(oth_at, 256), :]
    for j in range(8):
        cols = slice(j * 256, j * 256 + 256)
        part = lax.dot_general(
            own_ref[:, :, cols].reshape(256, 256), g_own, CONTRACT0, preferred_element_type=F32
        ) + lax.dot_general(
            oth_ref[:, :, cols].reshape(256, 256), g_oth, CONTRACT0, preferred_element_type=F32
        )
        for i in range(4):
            o_ref[j // 2, (j % 2) * 4 + i] = packed(part[i * 64 : i * 64 + 64]).astype(BF)


def swap(x, axis):
    return lax.ppermute(x, axis, [(0, 1), (1, 0)])


def deal(x, axis):
    return lax.all_to_all(x, axis, 0, 0, tiled=True)


def spread(x, axis, n):
    return deal(jnp.broadcast_to(x[None], (n,) + x.shape), axis)


def local(queries, keys, values, stream, out_proj, norm_gain, tag_proj, direction, starts, tags):
    core = lax.axis_index("c")
    ypos = lax.axis_index("y")
    zhpos = lax.axis_index("zh")
    own_at = ((ypos * ZH + zhpos) * C + core) * 32
    oth_at = ((ypos * ZH + 1 - zhpos) * C + core) * 32
    place = jnp.stack([core, own_at, oth_at, zhpos, lax.axis_index("x"), lax.axis_index("za")]).astype(jnp.int32)
    own_tags = tags[0].reshape(Y, ZH, C, 32).transpose(2, 0, 1, 3).reshape(C * Y, 64)[core * Y + ypos]
    own_tags = own_tags[:, None]
    gain = norm_gain[None]

    row = call(direction_kernel, shape(64, WIDE, dtype=BF), direction)
    proj, toks = call(
        turn_kernel,
        (shape(ROWS, COLS, dtype=BF), shape(C, 256, COLS, dtype=BF)),
        out_proj.T,
        stream[0].T,
    )
    theirs, far, proj, toks, own_tags = lax.optimization_barrier(
        (swap(queries[0], "zh"), swap(row, "za"), proj, toks, own_tags)
    )
    pairs = call(pair_kernel, shape(ZB, ZA, 64, WIDE, dtype=BF), place, row, far, smem=1)
    by_zl = deal(pairs, "zb")
    pair = call(
        functools.partial(
            attend_kernel,
            scratch=[pltpu.VMEM((SPAN, HK * HD), BF)] * 2 + [pltpu.SemaphoreType.DMA((2,))],
        ),
        shape(Y, ZH, 32, ROWS, dtype=BF),
        place,
        starts,
        keys[0],
        values[0],
        queries[0],
        theirs,
        smem=2,
        far=2,
    )
    u0 = [by_zl] + [
        lax.ppermute(by_zl, "x", [(i, (i + r) % X) for i in range(X)]) for r in range(1, X)
    ]
    own, *u0 = lax.optimization_barrier((deal(pair.reshape(Y, 64, ROWS), "y"), *u0))
    other = swap(own, "c")

    def product(second, *args):
        sent = call(
            functools.partial(product_kernel, second, scratch=[pltpu.VMEM((512, WIDE), BF)]),
            shape(X, ZL, PACK, 128, dtype=BF),
            place,
            *args,
            own,
            other,
            gain,
            tag_proj,
            smem=1,
        )
        part = call(sum_x_kernel, shape(ZL, PACK, 128, dtype=BF), deal(sent, "x"))
        return deal(part, ZAXES)

    h_loc, hdot0, load = call(
        functools.partial(
            first_kernel,
            scratch=[
                pltpu.VMEM((ROWS, COLS), BF),
                pltpu.VMEM((X, ZA, ZB, 64, WIDE), BF),
                pltpu.SemaphoreType.DMA((3 * X,)),
            ],
        ),
        (shape(512, COLS), shape(512, COLS), shape(8, 208, 128, dtype=BF)),
        place,
        proj,
        *u0,
        own,
        other,
        toks,
        gain,
        tag_proj,
        smem=1,
        far=X + 1,
    )
    part = call(sum_parts_kernel, shape(136, 128), deal(load, ("c", "y")))
    total, mixed = call(
        tokens0_kernel,
        (shape(136, 128), shape(8, 80, 128, dtype=BF)),
        part,
        swap(part, "zh"),
        own_tags,
    )
    rows0, sent = call(
        sum_rows_kernel,
        (shape(64, COLS), shape(ZL, 64, WIDE, dtype=BF)),
        product(False, deal(mixed, ("c", "y")), h_loc, hdot0),
    )
    full0 = spread(deal(sent, ZAXES).reshape(ZL * 64, WIDE), "x", X).reshape(ROWS, WIDE)
    moved, load = call(
        moved_kernel,
        (shape(512, COLS), shape(16, 80, 128, dtype=BF)),
        place,
        full0,
        own,
        other,
        h_loc,
        gain,
        tag_proj,
        smem=1,
    )
    mixed, inv = call(
        tokens1_kernel,
        (shape(8, 80, 128, dtype=BF), shape(8, 128)),
        deal(load, ("zh", "c", "y")),
        total,
        own_tags,
    )
    arrived = product(True, deal(mixed, ("c", "y")), h_loc, hdot0, moved, inv)
    return call(last_kernel, shape(64, COLS), arrived, rows0, direction, inv)


def solution(mesh):
    fine = Mesh(mesh.devices.reshape(ZA, ZB, X, Y, ZH, C), ("za", "zb", "x", "y", "zh", "c"))
    dp, mp = ("za", "zb", "x"), ("y", "zh", "c")
    return jax.shard_map(
        local,
        mesh=fine,
        in_specs=(
            P(dp, mp, None),
            P(dp, None, None),
            P(dp, None, None),
            P(dp, None, mp),
            P(None, mp),
            P(mp),
            P(mp, None),
            P(dp, mp),
            P(dp, None),
            P(dp, None),
        ),
        out_specs=P(dp, mp),
        check_vma=False,
    )
```

```python
import functools

import jax
import jax.numpy as jnp
from jax import lax
from jax.experimental import pallas as pl
from jax.experimental.pallas import tpu as pltpu
from jax.sharding import Mesh, PartitionSpec as P

D = 3584
HD = 256
HQ = 8
HK = 4
TAGS = 128
WINDOW = 256
DAMP = 0.01
KEEP = 2.0 - DAMP
NORM_EPS = 1e-06
MEAN_EPS = 1e-06
ZL, X, Y, ZH, C = 8, 4, 4, 2, 2
ZA, ZB = 2, 4
ROWS = HQ * HD
COLS = 224
WIDE = 256
COUNT = HQ * HD * D
SPAN = 352
PACK = 112
BF = jnp.bfloat16
F32 = jnp.float32
ZAXES = ("za", "zb")
CONTRACT0 = (((0,), (0,)), ((), ()))
CONTRACT1 = (((1,), (1,)), ((), ()))


def call(kernel, out_shape, *args, smem=0, far=0):
    specs = [pl.BlockSpec(memory_space=pltpu.SMEM)] * smem
    specs += [pl.BlockSpec(memory_space=pl.ANY)] * far
    args = [
        pltpu.with_memory_space_constraint(a, pltpu.HBM) if smem <= i < smem + far else a
        for i, a in enumerate(args)
    ]
    specs += [pl.BlockSpec(memory_space=pltpu.VMEM)] * (len(args) - smem - far)
    scratch = kernel.keywords.pop("scratch", ()) if isinstance(kernel, functools.partial) else ()
    many = isinstance(out_shape, (tuple, list))
    vmem = pl.BlockSpec(memory_space=pltpu.VMEM)
    return pl.pallas_call(
        kernel,
        out_shape=out_shape,
        in_specs=specs,
        out_specs=[vmem] * len(out_shape) if many else vmem,
        scratch_shapes=scratch,
        compiler_params=pltpu.CompilerParams(vmem_limit_bytes=40 * 2**20),
    )(*args)


def shape(*dims, dtype=F32):
    return jax.ShapeDtypeStruct(dims, dtype)


def dot(a, b):
    return jnp.dot(a, b, preferred_element_type=F32)


def three(x):
    a = x.astype(BF)
    rest = x - a.astype(F32)
    b = rest.astype(BF)
    return a, b, (rest - b.astype(F32)).astype(BF)


def attend_kernel(place, starts, k_ref, v_ref, own_ref, oth_ref, o_ref):
    own_at, oth_at, zh = place[1], place[2], place[3]
    first = pl.multiple_of(jnp.maximum(jnp.minimum(own_at, oth_at) - WINDOW, 0), 32)
    row = lax.broadcasted_iota(jnp.int32, (128, 1), 0)
    within = jnp.where(row < 64, row, row - 64)
    q_pos = jnp.where(within < 32, within + own_at, within - 32 + oth_at)
    k_pos = first + lax.broadcasted_iota(jnp.int32, (1, SPAN), 1)
    q_file = jnp.zeros((128, 1), jnp.int32)
    k_file = jnp.zeros((1, SPAN), jnp.int32)
    for f in range(4):
        q_file += jnp.where(starts[0, f] <= q_pos, 1, 0)
        k_file += jnp.where(starts[0, f] <= k_pos, 1, 0)
    allowed = (q_file == k_file) & (k_pos <= q_pos) & (q_pos - k_pos < WINDOW)
    keys = pl.ds(first, SPAN)
    for g in range(HK):
        heads = [slice((2 * g + r) * HD, (2 * g + r + 1) * HD) for r in range(2)]
        q = jnp.concatenate([ref[:, head] for head in heads for ref in (own_ref, oth_ref)], 0)
        cols = slice(g * HD, (g + 1) * HD)
        scores = lax.dot_general(q, k_ref[keys, cols], CONTRACT1, preferred_element_type=F32)
        scores = 50.0 * jnp.tanh(scores * (1.0 / 16.0) / 50.0)
        expo = jnp.where(allowed, jnp.exp(scores), 0.0)
        weights = (expo / jnp.sum(expo, -1, keepdims=True)).astype(BF)
        out = dot(weights, v_ref[keys, cols])
        for x in range(X):
            span = slice(x * 64, x * 64 + 64)
            both = jnp.concatenate([out[0:64, span], out[64:128, span]], 1).astype(BF)
            at = x * 512 + g * 128
            for y in range(Y):
                o_ref[y, zh, :, at : at + 128] = both[0:32]
                o_ref[y, 1 - zh, :, at : at + 128] = both[32:64]


def row_block(block):
    total = jnp.sum(block * block, -1, keepdims=True)
    hi = total.astype(BF)
    lo = (total - hi.astype(F32)).astype(BF)
    lane = lax.broadcasted_iota(jnp.int32, (64, WIDE - COLS), 1)
    tail = jnp.where(lane == 0, hi.astype(F32), jnp.where(lane == 1, lo.astype(F32), 0.0))
    return jnp.concatenate([block, tail], 1).astype(BF)


def packed(block):
    tail = block[:, 128:256]
    lane = lax.broadcasted_iota(jnp.int32, (16, 128), 1)
    parts = [
        jnp.where(lane < 96, tail[16 * i : 16 * i + 16], pltpu.roll(tail[48:64], 96 - 32 * i, 1))
        for i in range(3)
    ]
    return jnp.concatenate([block[:, 0:128], *parts], 0)


def unpacked(block):
    last = jnp.concatenate([block[at : at + 16, 96:128] for at in (64, 80, 96)], 1)
    tail = jnp.concatenate([block[64:112, 0:96], last], 0)
    return jnp.concatenate([block[0:64], tail], 1)


def direction_kernel(d_ref, o_ref):
    o_ref[...] = row_block(d_ref[...])


def pair_kernel(place, mine_ref, their_ref, o_ref):
    za = place[5]
    for i in range(ZB):
        o_ref[i, za] = mine_ref[...]
        o_ref[i, 1 - za] = their_ref[...]


def sum_x_kernel(i_ref, o_ref):
    total = i_ref[0].astype(F32)
    for i in range(1, X):
        total += i_ref[i].astype(F32)
    o_ref[...] = total.astype(BF)


def sum_zl(i_ref):
    total = i_ref[0].astype(F32)
    for i in range(1, ZL):
        total += i_ref[i].astype(F32)
    return unpacked(total)


def sum_rows_kernel(i_ref, rows_ref, o_ref):
    total = sum_zl(i_ref)
    rows_ref[...] = total
    load = row_block(total)
    for i in range(ZL):
        o_ref[i] = load


def last_kernel(i_ref, rows_ref, d_ref, inv_ref, o_ref):
    damp = 1.0 - DAMP
    inv = inv_ref[0:1, 0:1]
    o_ref[...] = (1.0 + damp * KEEP) * d_ref[...] - (
        damp * rows_ref[...] + sum_zl(i_ref)
    ) * inv


def turn_kernel(proj_ref, s_ref, oproj_ref, os_ref):
    for i in range(4):
        span = slice(i * 512, i * 512 + 512)
        rows = proj_ref[:, span].astype(F32).T.astype(BF)
        for j in range(8):
            at = (j % X) * 512 + (2 * i + j // X) * 64
            oproj_ref[at : at + 64, :] = rows[j * 64 : j * 64 + 64]
    s = s_ref[...].astype(F32).T.astype(BF)
    for i in range(Y * ZH):
        for c in range(C):
            at = (i * C + c) * 32
            os_ref[c, i * 32 : i * 32 + 32, :] = s[at : at + 32]


def square_of(rows):
    return jnp.sum(rows[:, COLS : COLS + 2].astype(F32))


def scores_of(x, gain, tag_ref):
    return sum(dot(part, tag_ref[...]) for part in three(x * gain))


def two(x):
    hi = x.astype(BF).astype(F32)
    return hi, (x - hi).astype(BF).astype(F32)


def rows_of(columns, count):
    lane = lax.broadcasted_iota(jnp.int32, (count, 128), 1)
    table = jnp.zeros((count, 128), F32)
    for i, column in enumerate(columns):
        hi, lo = two(column)
        table = jnp.where(lane == 2 * i, hi, jnp.where(lane == 2 * i + 1, lo, table))
    if count < 128:
        table = jnp.concatenate([table, jnp.zeros((128 - count, 128), F32)], 0)
    return table.T[0:16]


def put_scores(load_ref, block, row, z):
    for i in range(Y):
        load_ref[block + i, row : row + 64, :] = z[i * 64 : i * 64 + 64].astype(BF)


def put_sums(load_ref, block, row, sums, scalar):
    rows = rows_of((*sums, jnp.full((256, 1), scalar, F32)), 256)
    for i in range(Y):
        own = rows[:, i * 64 : i * 64 + 64]
        load_ref[block + i, row : row + 16, :] = jnp.concatenate([own, own], 1).astype(BF)


def first_kernel(
    place, proj_far, u0, u1, u2, u3, own_ref, oth_ref, s_ref, gain_ref, tag_ref, h_ref, hd_ref, load_ref,
    proj_ref, rows_ref, sems,
):
    copies = []
    for r in range(X):
        span = pl.ds(r * 512, 512)
        copies.append(pltpu.make_async_copy(proj_far.at[span], proj_ref.at[span], sems.at[r]))
    for r, u in enumerate((u0, u1, u2, u3)):
        for za in range(ZA):
            copies.append(
                pltpu.make_async_copy(u.at[:, za], rows_ref.at[r, za], sems.at[X + ZA * r + za])
            )
    for copy in copies:
        copy.start()
    gain = gain_ref[...]
    halves = []
    for half, a_ref in enumerate((own_ref, oth_ref)):
        c = place[0] if half == 0 else 1 - place[0]
        halves.append((c, pl.multiple_of(c * 256, 256), a_ref))
    hs = [s_ref[c].astype(F32) for c, _, _ in halves]
    for r in range(X):
        copies[r].wait()
        span = slice(r * 512, r * 512 + 512)
        for i, (_, _, a_ref) in enumerate(halves):
            hs[i] += dot(a_ref[:, :, span].reshape(256, 512), proj_ref[span, :])
    for h, (c, at, _) in zip(hs, halves):
        h_ref[pl.ds(at, 256), :] = h
        z = scores_of(h, gain, tag_ref)
        z_hi = z.astype(BF).astype(F32)
        put_scores(load_ref, c * Y, 0, z_hi)
        put_scores(load_ref, c * Y, 64, z - z_hi)
    hds = [jnp.zeros((256, WIDE), F32)] * 2
    norm = 0.0
    for r in range(X):
        copies[X + ZA * r].wait()
        copies[X + ZA * r + 1].wait()
        rows = rows_ref[r].reshape(512, WIDE)
        x = lax.rem(place[4] + X - r, X)
        span = pl.ds(pl.multiple_of(x * 512, 512), 512)
        norm += square_of(rows)
        for i, (_, _, a_ref) in enumerate(halves):
            hds[i] += dot(a_ref[:, :, span].reshape(256, 512), rows)
    for h, hd, (c, at, _) in zip(hs, hds, halves):
        hd = hd[:, :COLS]
        hd_ref[pl.ds(at, 256), :] = hd
        put_scores(load_ref, c * Y, 128, scores_of(hd, gain, tag_ref))
        sums = (jnp.sum(h * h, -1, keepdims=True), jnp.sum(h * hd, -1, keepdims=True))
        put_sums(load_ref, c * Y, 192, sums, norm)


def moved_kernel(place, u_ref, own_ref, oth_ref, h_ref, gain_ref, tag_ref, mv_ref, load_ref):
    norm = square_of(u_ref[...])
    gain = gain_ref[...]
    for half, a_ref in enumerate((own_ref, oth_ref)):
        c = place[0] if half == 0 else 1 - place[0]
        at = pl.multiple_of(c * 256, 256)
        moved = dot(a_ref[...].reshape(256, ROWS), u_ref[...])[:, :COLS]
        mv_ref[pl.ds(at, 256), :] = moved
        put_scores(load_ref, c * Y, 0, scores_of(moved, gain, tag_ref))
        sums = (jnp.sum(h_ref[pl.ds(at, 256), :] * moved, -1, keepdims=True),)
        put_sums(load_ref, c * Y, 64, sums, norm)


def sum_parts_kernel(i_ref, o_ref):
    total = i_ref[0].astype(F32)
    for i in range(1, 8):
        total += i_ref[i].astype(F32)
    scores = total[: total.shape[0] - 16]
    if scores.shape[0] == 192:
        scores = jnp.concatenate([scores[0:64] + scores[64:128], scores[128:192]], 0)
    sums = total[total.shape[0] - 16 :]
    joined = [sums[2 * i : 2 * i + 1] + sums[2 * i + 1 : 2 * i + 2] for i in range(8)]
    o_ref[...] = jnp.concatenate([scores, *joined], 0)


def columns_of(rows):
    return jnp.concatenate([rows, jnp.zeros((120, 128), F32)], 0).T[:64]


def backward(zval, sumsq, tags, along, zdot, o_ref):
    rscale = lax.rsqrt(sumsq / D + NORM_EPS)
    tanh_val = jnp.tanh(rscale * zval / 30.0)
    slope = 1.0 - tanh_val * tanh_val
    expo = jnp.exp(30.0 * tanh_val)
    probs = expo / jnp.sum(expo, -1, keepdims=True)
    onehot = (tags == lax.broadcasted_iota(jnp.int32, (64, TAGS), 1)).astype(F32)
    dlogit = probs - onehot
    wgrad = dlogit * slope
    rho = jnp.sum(wgrad * zval, -1, keepdims=True)
    cube = rscale * rscale * rscale / D
    rdot = -cube * along
    mdot = rdot * zval + rscale * zdot
    ldot = slope * mdot
    pdot = probs * (ldot - jnp.sum(probs * ldot, -1, keepdims=True))
    wdot = pdot * slope - dlogit * 2.0 * tanh_val * slope * mdot / 30.0
    rhodot = jnp.sum(wdot * zval + wgrad * zdot, -1, keepdims=True)
    mixed = rdot * wgrad + rscale * wdot
    coeff = rhodot * cube + 3.0 * rho * rscale * rscale * rdot / D
    mixed = mixed.astype(BF)
    tail = rows_of((coeff, rho * cube), 64).astype(BF)
    for i in range(8):
        o_ref[i, 0:64, :] = mixed
        o_ref[i, 64:80, :] = tail


def tokens0_kernel(mine_ref, their_ref, tag_ref, total_ref, o_ref):
    total_ref[...] = mine_ref[...] + their_ref[...]
    columns = columns_of(total_ref[128:136, :])
    backward(
        total_ref[0:64, :], columns[:, 0:1], tag_ref[...], columns[:, 1:2], total_ref[64:128, :], o_ref
    )


def tokens1_kernel(mine_ref, their_ref, total_ref, tag_ref, o_ref, inv_ref):
    moved = mine_ref[...] + their_ref[...]
    product_sq = moved[65:66, 0:1]
    norm_sq = total_ref[130:131, 0:1]
    sigma = 2.0 * jnp.sqrt((product_sq / COUNT + MEAN_EPS) / (norm_sq / COUNT + MEAN_EPS))
    inv = 1.0 / sigma
    inv_ref[...] = jnp.broadcast_to(inv, (8, 128))
    columns0 = columns_of(total_ref[128:136, :])
    columns1 = columns_of(moved[64:72])
    along = KEEP * columns0[:, 1:2] - columns1[:, 0:1] * inv
    zdot = KEEP * total_ref[64:128, :] - moved[0:64] * inv
    backward(total_ref[0:64, :], columns0[:, 0:1], tag_ref[...], along, zdot, o_ref)


def product_kernel(second, place, m_ref, h_ref, hd_ref, *rest):
    if second:
        mv_ref, inv_ref, *rest = rest
    own_ref, oth_ref, gain_ref, tag_ref, o_ref, g_ref = rest
    gain = gain_ref[...]
    for c in range(C):
        span = slice(c * 256, c * 256 + 256)
        mixed = jnp.concatenate([m_ref[c * Y + i, 0:64, :] for i in range(Y)], 0)
        back = lax.dot_general(mixed, tag_ref[...], CONTRACT1, preferred_element_type=F32)
        columns = jnp.concatenate(
            [columns_of(m_ref[c * Y + i, 64:80, :].astype(F32)[0:8]) for i in range(Y)], 0
        )
        coeff, cubed = columns[:, 0:1] + columns[:, 1:2], columns[:, 2:3] + columns[:, 3:4]
        hd = hd_ref[span, :]
        if second:
            hd = KEEP * hd - mv_ref[span, :] * inv_ref[0:1, 0:1]
        g = back * gain - coeff * h_ref[span, :] - cubed * hd
        g_ref[span, 0:COLS] = g.astype(BF)
        g_ref[span, COLS:WIDE] = jnp.zeros((256, WIDE - COLS), BF)
    own_at = pl.multiple_of(place[0] * 256, 256)
    oth_at = pl.multiple_of((1 - place[0]) * 256, 256)
    g_own = g_ref[pl.ds(own_at, 256), :]
    g_oth = g_ref[pl.ds(oth_at, 256), :]
    for j in range(8):
        cols = slice(j * 256, j * 256 + 256)
        part = lax.dot_general(
            own_ref[:, :, cols].reshape(256, 256), g_own, CONTRACT0, preferred_element_type=F32
        ) + lax.dot_general(
            oth_ref[:, :, cols].reshape(256, 256), g_oth, CONTRACT0, preferred_element_type=F32
        )
        for i in range(4):
            o_ref[j // 2, (j % 2) * 4 + i] = packed(part[i * 64 : i * 64 + 64]).astype(BF)


def swap(x, axis):
    return lax.ppermute(x, axis, [(0, 1), (1, 0)])


def deal(x, axis):
    return lax.all_to_all(x, axis, 0, 0, tiled=True)


def spread(x, axis, n):
    return deal(jnp.broadcast_to(x[None], (n,) + x.shape), axis)


def local(queries, keys, values, stream, out_proj, norm_gain, tag_proj, direction, starts, tags):
    core = lax.axis_index("c")
    ypos = lax.axis_index("y")
    zhpos = lax.axis_index("zh")
    own_at = ((ypos * ZH + zhpos) * C + core) * 32
    oth_at = ((ypos * ZH + 1 - zhpos) * C + core) * 32
    place = jnp.stack([core, own_at, oth_at, zhpos, lax.axis_index("x"), lax.axis_index("za")]).astype(jnp.int32)
    own_tags = tags[0].reshape(Y, ZH, C, 32).transpose(2, 0, 1, 3).reshape(C * Y, 64)[core * Y + ypos]
    own_tags = own_tags[:, None]
    gain = norm_gain[None]

    row = call(direction_kernel, shape(64, WIDE, dtype=BF), direction)
    proj, toks = call(
        turn_kernel,
        (shape(ROWS, COLS, dtype=BF), shape(C, 256, COLS, dtype=BF)),
        out_proj.T,
        stream[0].T,
    )
    theirs, far, proj, toks, own_tags = lax.optimization_barrier(
        (swap(queries[0], "zh"), swap(row, "za"), proj, toks, own_tags)
    )
    pairs = call(pair_kernel, shape(ZB, ZA, 64, WIDE, dtype=BF), place, row, far, smem=1)
    by_zl = deal(pairs, "zb")
    pair = call(
        attend_kernel,
        shape(Y, ZH, 32, ROWS, dtype=BF),
        place,
        starts,
        keys[0],
        values[0],
        queries[0],
        theirs,
        smem=2,
    )
    u0 = [by_zl] + [
        lax.ppermute(by_zl, "x", [(i, (i + r) % X) for i in range(X)]) for r in range(1, X)
    ]
    own, *u0[:3] = lax.optimization_barrier((deal(pair.reshape(Y, 64, ROWS), "y"), *u0[:3]))
    other = swap(own, "c")

    def product(second, *args):
        sent = call(
            functools.partial(product_kernel, second, scratch=[pltpu.VMEM((512, WIDE), BF)]),
            shape(X, ZL, PACK, 128, dtype=BF),
            place,
            *args,
            own,
            other,
            gain,
            tag_proj,
            smem=1,
        )
        part = call(sum_x_kernel, shape(ZL, PACK, 128, dtype=BF), deal(sent, "x"))
        return deal(part, ZAXES)

    def token_sum(load, rows, kernel, outs, *args):
        part = call(sum_parts_kernel, shape(rows, 128), deal(load, ("c", "y")))
        return call(kernel, outs, part, swap(part, "zh"), *args, own_tags)

    h_loc, hdot0, load = call(
        functools.partial(
            first_kernel,
            scratch=[
                pltpu.VMEM((ROWS, COLS), BF),
                pltpu.VMEM((X, ZA, ZB, 64, WIDE), BF),
                pltpu.SemaphoreType.DMA((3 * X,)),
            ],
        ),
        (shape(512, COLS), shape(512, COLS), shape(8, 208, 128, dtype=BF)),
        place,
        proj,
        *u0,
        own,
        other,
        toks,
        gain,
        tag_proj,
        smem=1,
        far=X + 1,
    )
    total, mixed = token_sum(load, 136, tokens0_kernel, (shape(136, 128), shape(8, 80, 128, dtype=BF)))
    rows0, sent = call(
        sum_rows_kernel,
        (shape(64, COLS), shape(ZL, 64, WIDE, dtype=BF)),
        product(False, deal(mixed, ("c", "y")), h_loc, hdot0),
    )
    full0 = spread(deal(sent, ZAXES).reshape(ZL * 64, WIDE), "x", X).reshape(ROWS, WIDE)
    moved, load = call(
        moved_kernel,
        (shape(512, COLS), shape(8, 80, 128, dtype=BF)),
        place,
        full0,
        own,
        other,
        h_loc,
        gain,
        tag_proj,
        smem=1,
    )
    mixed, inv = token_sum(
        load, 72, tokens1_kernel, (shape(8, 80, 128, dtype=BF), shape(8, 128)), total
    )
    arrived = product(True, deal(mixed, ("c", "y")), h_loc, hdot0, moved, inv)
    return call(last_kernel, shape(64, COLS), arrived, rows0, direction, inv)


def solution(mesh):
    fine = Mesh(mesh.devices.reshape(ZA, ZB, X, Y, ZH, C), ("za", "zb", "x", "y", "zh", "c"))
    dp, mp = ("za", "zb", "x"), ("y", "zh", "c")
    return jax.shard_map(
        local,
        mesh=fine,
        in_specs=(
            P(dp, mp, None),
            P(dp, None, None),
            P(dp, None, None),
            P(dp, None, mp),
            P(None, mp),
            P(mp),
            P(mp, None),
            P(dp, mp),
            P(dp, None),
            P(dp, None),
        ),
        out_specs=P(dp, mp),
        check_vma=False,
    )
```

```python
import functools

import jax
import jax.numpy as jnp
from jax import lax
from jax.experimental import pallas as pl
from jax.experimental.pallas import tpu as pltpu
from jax.sharding import Mesh, PartitionSpec as P

D = 3584
HD = 256
HQ = 8
HK = 4
TAGS = 128
WINDOW = 256
DAMP = 0.01
KEEP = 2.0 - DAMP
NORM_EPS = 1e-06
MEAN_EPS = 1e-06
ZL, X, Y, ZH, C = 8, 4, 4, 2, 2
ZA, ZB = 2, 4
ROWS = HQ * HD
COLS = 224
WIDE = 256
COUNT = HQ * HD * D
SPAN = 352
PACK = 112
BF = jnp.bfloat16
F32 = jnp.float32
ZAXES = ("za", "zb")
CONTRACT0 = (((0,), (0,)), ((), ()))
CONTRACT1 = (((1,), (1,)), ((), ()))


def call(kernel, out_shape, *args, smem=0, far=0):
    specs = [pl.BlockSpec(memory_space=pltpu.SMEM)] * smem
    specs += [pl.BlockSpec(memory_space=pl.ANY)] * far
    args = [
        pltpu.with_memory_space_constraint(a, pltpu.HBM) if smem <= i < smem + far else a
        for i, a in enumerate(args)
    ]
    specs += [pl.BlockSpec(memory_space=pltpu.VMEM)] * (len(args) - smem - far)
    scratch = kernel.keywords.pop("scratch", ()) if isinstance(kernel, functools.partial) else ()
    many = isinstance(out_shape, (tuple, list))
    vmem = pl.BlockSpec(memory_space=pltpu.VMEM)
    return pl.pallas_call(
        kernel,
        out_shape=out_shape,
        in_specs=specs,
        out_specs=[vmem] * len(out_shape) if many else vmem,
        scratch_shapes=scratch,
        compiler_params=pltpu.CompilerParams(vmem_limit_bytes=40 * 2**20),
    )(*args)


def shape(*dims, dtype=F32):
    return jax.ShapeDtypeStruct(dims, dtype)


def dot(a, b):
    return jnp.dot(a, b, preferred_element_type=F32)


def three(x):
    a = x.astype(BF)
    rest = x - a.astype(F32)
    b = rest.astype(BF)
    return a, b, (rest - b.astype(F32)).astype(BF)


def attend_kernel(place, starts, k_ref, v_ref, own_ref, oth_ref, o_ref):
    own_at, oth_at, zh = place[1], place[2], place[3]
    first = pl.multiple_of(jnp.maximum(jnp.minimum(own_at, oth_at) - WINDOW, 0), 32)
    row = lax.broadcasted_iota(jnp.int32, (128, 1), 0)
    within = jnp.where(row < 64, row, row - 64)
    q_pos = jnp.where(within < 32, within + own_at, within - 32 + oth_at)
    k_pos = first + lax.broadcasted_iota(jnp.int32, (1, SPAN), 1)
    q_file = jnp.zeros((128, 1), jnp.int32)
    k_file = jnp.zeros((1, SPAN), jnp.int32)
    for f in range(4):
        q_file += jnp.where(starts[0, f] <= q_pos, 1, 0)
        k_file += jnp.where(starts[0, f] <= k_pos, 1, 0)
    allowed = (q_file == k_file) & (k_pos <= q_pos) & (q_pos - k_pos < WINDOW)
    keys = pl.ds(first, SPAN)
    for g in range(HK):
        heads = [slice((2 * g + r) * HD, (2 * g + r + 1) * HD) for r in range(2)]
        q = jnp.concatenate([ref[:, head] for head in heads for ref in (own_ref, oth_ref)], 0)
        cols = slice(g * HD, (g + 1) * HD)
        scores = lax.dot_general(q, k_ref[keys, cols], CONTRACT1, preferred_element_type=F32)
        scores = 50.0 * jnp.tanh(scores * (1.0 / 16.0) / 50.0)
        expo = jnp.where(allowed, jnp.exp(scores), 0.0)
        weights = (expo / jnp.sum(expo, -1, keepdims=True)).astype(BF)
        out = dot(weights, v_ref[keys, cols])
        for x in range(X):
            span = slice(x * 64, x * 64 + 64)
            both = jnp.concatenate([out[0:64, span], out[64:128, span]], 1).astype(BF)
            at = x * 512 + g * 128
            for y in range(Y):
                o_ref[y, zh, :, at : at + 128] = both[0:32]
                o_ref[y, 1 - zh, :, at : at + 128] = both[32:64]


def row_block(block):
    total = jnp.sum(block * block, -1, keepdims=True)
    hi = total.astype(BF)
    lo = (total - hi.astype(F32)).astype(BF)
    lane = lax.broadcasted_iota(jnp.int32, (64, WIDE - COLS), 1)
    tail = jnp.where(lane == 0, hi.astype(F32), jnp.where(lane == 1, lo.astype(F32), 0.0))
    return jnp.concatenate([block, tail], 1).astype(BF)


def packed(block):
    tail = block[:, 128:256]
    lane = lax.broadcasted_iota(jnp.int32, (16, 128), 1)
    parts = [
        jnp.where(lane < 96, tail[16 * i : 16 * i + 16], pltpu.roll(tail[48:64], 96 - 32 * i, 1))
        for i in range(3)
    ]
    return jnp.concatenate([block[:, 0:128], *parts], 0)


def unpacked(block):
    last = jnp.concatenate([block[at : at + 16, 96:128] for at in (64, 80, 96)], 1)
    tail = jnp.concatenate([block[64:112, 0:96], last], 0)
    return jnp.concatenate([block[0:64], tail], 1)


def direction_kernel(d_ref, o_ref):
    o_ref[...] = row_block(d_ref[...])


def pair_kernel(place, mine_ref, their_ref, o_ref):
    za = place[5]
    for i in range(ZB):
        o_ref[i, za] = mine_ref[...]
        o_ref[i, 1 - za] = their_ref[...]


def repeat_kernel(i_ref, o_ref):
    for i in range(X):
        o_ref[i] = i_ref[...]


def sum_x_kernel(i_ref, o_ref):
    total = i_ref[0].astype(F32)
    for i in range(1, X):
        total += i_ref[i].astype(F32)
    o_ref[...] = total.astype(BF)


def sum_zl(i_ref):
    total = i_ref[0].astype(F32)
    for i in range(1, ZL):
        total += i_ref[i].astype(F32)
    return unpacked(total)


def sum_rows_kernel(i_ref, rows_ref, o_ref):
    total = sum_zl(i_ref)
    rows_ref[...] = total
    load = row_block(total)
    for i in range(ZL):
        o_ref[i] = load


def last_kernel(i_ref, rows_ref, d_ref, inv_ref, o_ref):
    damp = 1.0 - DAMP
    inv = inv_ref[0:1, 0:1]
    o_ref[...] = (1.0 + damp * KEEP) * d_ref[...] - (
        damp * rows_ref[...] + sum_zl(i_ref)
    ) * inv


def turn_kernel(proj_ref, s_ref, oproj_ref, os_ref):
    for i in range(4):
        span = slice(i * 512, i * 512 + 512)
        rows = proj_ref[:, span].astype(F32).T.astype(BF)
        for j in range(8):
            at = (j % X) * 512 + (2 * i + j // X) * 64
            oproj_ref[at : at + 64, :] = rows[j * 64 : j * 64 + 64]
    s = s_ref[...].astype(F32).T.astype(BF)
    for i in range(Y * ZH):
        for c in range(C):
            at = (i * C + c) * 32
            os_ref[c, i * 32 : i * 32 + 32, :] = s[at : at + 32]


def square_of(rows):
    return jnp.sum(rows[:, COLS : COLS + 2].astype(F32))


def scores_of(x, gain, tag_ref):
    return sum(dot(part, tag_ref[...]) for part in three(x * gain))


def two(x):
    hi = x.astype(BF).astype(F32)
    return hi, (x - hi).astype(BF).astype(F32)


def rows_of(columns, count):
    lane = lax.broadcasted_iota(jnp.int32, (count, 128), 1)
    table = jnp.zeros((count, 128), F32)
    for i, column in enumerate(columns):
        hi, lo = two(column)
        table = jnp.where(lane == 2 * i, hi, jnp.where(lane == 2 * i + 1, lo, table))
    if count < 128:
        table = jnp.concatenate([table, jnp.zeros((128 - count, 128), F32)], 0)
    return table.T[0:16]


def put_scores(load_ref, block, row, z):
    for i in range(Y):
        load_ref[block + i, row : row + 64, :] = z[i * 64 : i * 64 + 64].astype(BF)


def put_sums(load_ref, block, row, sums, scalar):
    rows = rows_of((*sums, jnp.full((256, 1), scalar, F32)), 256)
    for i in range(Y):
        own = rows[:, i * 64 : i * 64 + 64]
        load_ref[block + i, row : row + 16, :] = jnp.concatenate([own, own], 1).astype(BF)


def first_kernel(
    place, proj_far, u0, u1, u2, u3, own_ref, oth_ref, s_ref, gain_ref, tag_ref, h_ref, hd_ref, load_ref,
    proj_ref, rows_ref, sems,
):
    copies = []
    for r in range(X):
        span = pl.ds(r * 512, 512)
        copies.append(pltpu.make_async_copy(proj_far.at[span], proj_ref.at[span], sems.at[r]))
    for r, u in enumerate((u0, u1, u2, u3)):
        for za in range(ZA):
            copies.append(
                pltpu.make_async_copy(u.at[:, za], rows_ref.at[r, za], sems.at[X + ZA * r + za])
            )
    for copy in copies:
        copy.start()
    gain = gain_ref[...]
    halves = []
    for half, a_ref in enumerate((own_ref, oth_ref)):
        c = place[0] if half == 0 else 1 - place[0]
        halves.append((c, pl.multiple_of(c * 256, 256), a_ref))
    hs = [s_ref[c].astype(F32) for c, _, _ in halves]
    for r in range(X):
        copies[r].wait()
        span = slice(r * 512, r * 512 + 512)
        for i, (_, _, a_ref) in enumerate(halves):
            hs[i] += dot(a_ref[:, :, span].reshape(256, 512), proj_ref[span, :])
    for h, (c, at, _) in zip(hs, halves):
        h_ref[pl.ds(at, 256), :] = h
        z = scores_of(h, gain, tag_ref)
        z_hi = z.astype(BF).astype(F32)
        put_scores(load_ref, c * Y, 0, z_hi)
        put_scores(load_ref, c * Y, 64, z - z_hi)
    hds = [jnp.zeros((256, WIDE), F32)] * 2
    norm = 0.0
    for r in range(X):
        copies[X + ZA * r].wait()
        copies[X + ZA * r + 1].wait()
        rows = rows_ref[r].reshape(512, WIDE)
        x = lax.rem(place[4] + X - r, X)
        span = pl.ds(pl.multiple_of(x * 512, 512), 512)
        norm += square_of(rows)
        for i, (_, _, a_ref) in enumerate(halves):
            hds[i] += dot(a_ref[:, :, span].reshape(256, 512), rows)
    for h, hd, (c, at, _) in zip(hs, hds, halves):
        hd = hd[:, :COLS]
        hd_ref[pl.ds(at, 256), :] = hd
        put_scores(load_ref, c * Y, 128, scores_of(hd, gain, tag_ref))
        sums = (jnp.sum(h * h, -1, keepdims=True), jnp.sum(h * hd, -1, keepdims=True))
        put_sums(load_ref, c * Y, 192, sums, norm)


def moved_kernel(place, u_ref, own_ref, oth_ref, h_ref, gain_ref, tag_ref, mv_ref, load_ref):
    norm = square_of(u_ref[...])
    gain = gain_ref[...]
    for half, a_ref in enumerate((own_ref, oth_ref)):
        c = place[0] if half == 0 else 1 - place[0]
        at = pl.multiple_of(c * 256, 256)
        moved = dot(a_ref[...].reshape(256, ROWS), u_ref[...])[:, :COLS]
        mv_ref[pl.ds(at, 256), :] = moved
        put_scores(load_ref, c * Y, 0, scores_of(moved, gain, tag_ref))
        sums = (jnp.sum(h_ref[pl.ds(at, 256), :] * moved, -1, keepdims=True),)
        put_sums(load_ref, c * Y, 64, sums, norm)


def sum_parts_kernel(i_ref, o_ref):
    total = i_ref[0].astype(F32)
    for i in range(1, 8):
        total += i_ref[i].astype(F32)
    scores = total[: total.shape[0] - 16]
    if scores.shape[0] == 192:
        scores = jnp.concatenate([scores[0:64] + scores[64:128], scores[128:192]], 0)
    sums = total[total.shape[0] - 16 :]
    joined = [sums[2 * i : 2 * i + 1] + sums[2 * i + 1 : 2 * i + 2] for i in range(8)]
    o_ref[...] = jnp.concatenate([scores, *joined], 0)


def columns_of(rows):
    return jnp.concatenate([rows, jnp.zeros((120, 128), F32)], 0).T[:64]


def backward(zval, sumsq, tags, along, zdot, o_ref):
    rscale = lax.rsqrt(sumsq / D + NORM_EPS)
    tanh_val = jnp.tanh(rscale * zval / 30.0)
    slope = 1.0 - tanh_val * tanh_val
    expo = jnp.exp(30.0 * tanh_val)
    probs = expo / jnp.sum(expo, -1, keepdims=True)
    onehot = (tags == lax.broadcasted_iota(jnp.int32, (64, TAGS), 1)).astype(F32)
    dlogit = probs - onehot
    wgrad = dlogit * slope
    rho = jnp.sum(wgrad * zval, -1, keepdims=True)
    cube = rscale * rscale * rscale / D
    rdot = -cube * along
    mdot = rdot * zval + rscale * zdot
    ldot = slope * mdot
    pdot = probs * (ldot - jnp.sum(probs * ldot, -1, keepdims=True))
    wdot = pdot * slope - dlogit * 2.0 * tanh_val * slope * mdot / 30.0
    rhodot = jnp.sum(wdot * zval + wgrad * zdot, -1, keepdims=True)
    mixed = rdot * wgrad + rscale * wdot
    coeff = rhodot * cube + 3.0 * rho * rscale * rscale * rdot / D
    mixed = mixed.astype(BF)
    tail = rows_of((coeff, rho * cube), 64).astype(BF)
    for i in range(8):
        o_ref[i, 0:64, :] = mixed
        o_ref[i, 64:80, :] = tail


def tokens0_kernel(mine_ref, their_ref, tag_ref, total_ref, o_ref):
    total_ref[...] = mine_ref[...] + their_ref[...]
    columns = columns_of(total_ref[128:136, :])
    backward(
        total_ref[0:64, :], columns[:, 0:1], tag_ref[...], columns[:, 1:2], total_ref[64:128, :], o_ref
    )


def tokens1_kernel(mine_ref, their_ref, total_ref, tag_ref, o_ref, inv_ref):
    moved = mine_ref[...] + their_ref[...]
    product_sq = moved[65:66, 0:1]
    norm_sq = total_ref[130:131, 0:1]
    sigma = 2.0 * jnp.sqrt((product_sq / COUNT + MEAN_EPS) / (norm_sq / COUNT + MEAN_EPS))
    inv = 1.0 / sigma
    inv_ref[...] = jnp.broadcast_to(inv, (8, 128))
    columns0 = columns_of(total_ref[128:136, :])
    columns1 = columns_of(moved[64:72])
    along = KEEP * columns0[:, 1:2] - columns1[:, 0:1] * inv
    zdot = KEEP * total_ref[64:128, :] - moved[0:64] * inv
    backward(total_ref[0:64, :], columns0[:, 0:1], tag_ref[...], along, zdot, o_ref)


def product_kernel(second, place, m_ref, h_ref, hd_ref, *rest):
    if second:
        mv_ref, inv_ref, *rest = rest
    own_ref, oth_ref, gain_ref, tag_ref, o_ref, g_ref = rest
    gain = gain_ref[...]
    for c in range(C):
        span = slice(c * 256, c * 256 + 256)
        mixed = jnp.concatenate([m_ref[c * Y + i, 0:64, :] for i in range(Y)], 0)
        back = lax.dot_general(mixed, tag_ref[...], CONTRACT1, preferred_element_type=F32)
        columns = jnp.concatenate(
            [columns_of(m_ref[c * Y + i, 64:80, :].astype(F32)[0:8]) for i in range(Y)], 0
        )
        coeff, cubed = columns[:, 0:1] + columns[:, 1:2], columns[:, 2:3] + columns[:, 3:4]
        hd = hd_ref[span, :]
        if second:
            hd = KEEP * hd - mv_ref[span, :] * inv_ref[0:1, 0:1]
        g = back * gain - coeff * h_ref[span, :] - cubed * hd
        g_ref[span, 0:COLS] = g.astype(BF)
        g_ref[span, COLS:WIDE] = jnp.zeros((256, WIDE - COLS), BF)
    own_at = pl.multiple_of(place[0] * 256, 256)
    oth_at = pl.multiple_of((1 - place[0]) * 256, 256)
    g_own = g_ref[pl.ds(own_at, 256), :]
    g_oth = g_ref[pl.ds(oth_at, 256), :]
    for j in range(8):
        cols = slice(j * 256, j * 256 + 256)
        part = lax.dot_general(
            own_ref[:, :, cols].reshape(256, 256), g_own, CONTRACT0, preferred_element_type=F32
        ) + lax.dot_general(
            oth_ref[:, :, cols].reshape(256, 256), g_oth, CONTRACT0, preferred_element_type=F32
        )
        for i in range(4):
            o_ref[j // 2, (j % 2) * 4 + i] = packed(part[i * 64 : i * 64 + 64]).astype(BF)


def swap(x, axis):
    return lax.ppermute(x, axis, [(0, 1), (1, 0)])


def deal(x, axis):
    return lax.all_to_all(x, axis, 0, 0, tiled=True)


def local(queries, keys, values, stream, out_proj, norm_gain, tag_proj, direction, starts, tags):
    core = lax.axis_index("c")
    ypos = lax.axis_index("y")
    zhpos = lax.axis_index("zh")
    own_at = ((ypos * ZH + zhpos) * C + core) * 32
    oth_at = ((ypos * ZH + 1 - zhpos) * C + core) * 32
    place = jnp.stack([core, own_at, oth_at, zhpos, lax.axis_index("x"), lax.axis_index("za")]).astype(jnp.int32)
    own_tags = tags[0].reshape(Y, ZH, C, 32).transpose(2, 0, 1, 3).reshape(C * Y, 64)[core * Y + ypos]
    own_tags = own_tags[:, None]
    gain = norm_gain[None]

    row = call(direction_kernel, shape(64, WIDE, dtype=BF), direction)
    proj, toks = call(
        turn_kernel,
        (shape(ROWS, COLS, dtype=BF), shape(C, 256, COLS, dtype=BF)),
        out_proj.T,
        stream[0].T,
    )
    theirs, far, proj, toks, own_tags = lax.optimization_barrier(
        (swap(queries[0], "zh"), swap(row, "za"), proj, toks, own_tags)
    )
    pairs = call(pair_kernel, shape(ZB, ZA, 64, WIDE, dtype=BF), place, row, far, smem=1)
    by_zl = deal(pairs, "zb")
    pair = call(
        attend_kernel,
        shape(Y, ZH, 32, ROWS, dtype=BF),
        place,
        starts,
        keys[0],
        values[0],
        queries[0],
        theirs,
        smem=2,
    )
    u0 = [by_zl] + [
        lax.ppermute(by_zl, "x", [(i, (i + r) % X) for i in range(X)]) for r in range(1, X)
    ]
    own, *u0 = lax.optimization_barrier((deal(pair.reshape(Y, 64, ROWS), "y"), *u0))
    other = swap(own, "c")

    def product(second, *args):
        sent = call(
            functools.partial(product_kernel, second, scratch=[pltpu.VMEM((512, WIDE), BF)]),
            shape(X, ZL, PACK, 128, dtype=BF),
            place,
            *args,
            own,
            other,
            gain,
            tag_proj,
            smem=1,
        )
        part = call(sum_x_kernel, shape(ZL, PACK, 128, dtype=BF), deal(sent, "x"))
        return deal(part, ZAXES)

    def token_sum(load, rows, kernel, outs, *args):
        part = call(sum_parts_kernel, shape(rows, 128), deal(load, ("c", "y")))
        return call(kernel, outs, part, swap(part, "zh"), *args, own_tags)

    h_loc, hdot0, load = call(
        functools.partial(
            first_kernel,
            scratch=[
                pltpu.VMEM((ROWS, COLS), BF),
                pltpu.VMEM((X, ZA, ZB, 64, WIDE), BF),
                pltpu.SemaphoreType.DMA((3 * X,)),
            ],
        ),
        (shape(512, COLS), shape(512, COLS), shape(8, 208, 128, dtype=BF)),
        place,
        proj,
        *u0,
        own,
        other,
        toks,
        gain,
        tag_proj,
        smem=1,
        far=X + 1,
    )
    total, mixed = token_sum(load, 136, tokens0_kernel, (shape(136, 128), shape(8, 80, 128, dtype=BF)))
    rows0, sent = call(
        sum_rows_kernel,
        (shape(64, COLS), shape(ZL, 64, WIDE, dtype=BF)),
        product(False, deal(mixed, ("c", "y")), h_loc, hdot0),
    )
    rows = deal(sent, ZAXES).reshape(ZL * 64, WIDE)
    full0 = deal(call(repeat_kernel, shape(X, ZL * 64, WIDE, dtype=BF), rows), "x").reshape(ROWS, WIDE)
    moved, load = call(
        moved_kernel,
        (shape(512, COLS), shape(8, 80, 128, dtype=BF)),
        place,
        full0,
        own,
        other,
        h_loc,
        gain,
        tag_proj,
        smem=1,
    )
    mixed, inv = token_sum(
        load, 72, tokens1_kernel, (shape(8, 80, 128, dtype=BF), shape(8, 128)), total
    )
    arrived = product(True, deal(mixed, ("c", "y")), h_loc, hdot0, moved, inv)
    return call(last_kernel, shape(64, COLS), arrived, rows0, direction, inv)


def solution(mesh):
    fine = Mesh(mesh.devices.reshape(ZA, ZB, X, Y, ZH, C), ("za", "zb", "x", "y", "zh", "c"))
    dp, mp = ("za", "zb", "x"), ("y", "zh", "c")
    return jax.shard_map(
        local,
        mesh=fine,
        in_specs=(
            P(dp, mp, None),
            P(dp, None, None),
            P(dp, None, None),
            P(dp, None, mp),
            P(None, mp),
            P(mp),
            P(mp, None),
            P(dp, mp),
            P(dp, None),
            P(dp, None),
        ),
        out_specs=P(dp, mp),
        check_vma=False,
    )
```

```python
import functools

import jax
import jax.numpy as jnp
from jax import lax
from jax.experimental import pallas as pl
from jax.experimental.pallas import tpu as pltpu
from jax.sharding import Mesh, PartitionSpec as P

D = 3584
HD = 256
HQ = 8
HK = 4
TAGS = 128
WINDOW = 256
DAMP = 0.01
KEEP = 2.0 - DAMP
NORM_EPS = 1e-06
MEAN_EPS = 1e-06
ZL, X, Y, ZH, C = 8, 4, 4, 2, 2
ZA, ZB = 2, 4
ROWS = HQ * HD
COLS = 224
WIDE = 256
COUNT = HQ * HD * D
SPAN = 352
PACK = 112
BF = jnp.bfloat16
F32 = jnp.float32
ZAXES = ("za", "zb")
CONTRACT0 = (((0,), (0,)), ((), ()))
CONTRACT1 = (((1,), (1,)), ((), ()))


def call(kernel, out_shape, *args, smem=0, far=0):
    specs = [pl.BlockSpec(memory_space=pltpu.SMEM)] * smem
    specs += [pl.BlockSpec(memory_space=pl.ANY)] * far
    args = [
        pltpu.with_memory_space_constraint(a, pltpu.HBM) if smem <= i < smem + far else a
        for i, a in enumerate(args)
    ]
    specs += [pl.BlockSpec(memory_space=pltpu.VMEM)] * (len(args) - smem - far)
    scratch = kernel.keywords.pop("scratch", ()) if isinstance(kernel, functools.partial) else ()
    many = isinstance(out_shape, (tuple, list))
    vmem = pl.BlockSpec(memory_space=pltpu.VMEM)
    return pl.pallas_call(
        kernel,
        out_shape=out_shape,
        in_specs=specs,
        out_specs=[vmem] * len(out_shape) if many else vmem,
        scratch_shapes=scratch,
        compiler_params=pltpu.CompilerParams(vmem_limit_bytes=40 * 2**20),
    )(*args)


def shape(*dims, dtype=F32):
    return jax.ShapeDtypeStruct(dims, dtype)


def dot(a, b):
    return jnp.dot(a, b, preferred_element_type=F32)


def three(x):
    a = x.astype(BF)
    rest = x - a.astype(F32)
    b = rest.astype(BF)
    return a, b, (rest - b.astype(F32)).astype(BF)


def attend_kernel(place, starts, k_ref, v_ref, own_ref, oth_ref, o_ref):
    own_at, oth_at, zh = place[1], place[2], place[3]
    first = pl.multiple_of(jnp.maximum(jnp.minimum(own_at, oth_at) - WINDOW, 0), 32)
    row = lax.broadcasted_iota(jnp.int32, (128, 1), 0)
    within = jnp.where(row < 64, row, row - 64)
    q_pos = jnp.where(within < 32, within + own_at, within - 32 + oth_at)
    k_pos = first + lax.broadcasted_iota(jnp.int32, (1, SPAN), 1)
    q_file = jnp.zeros((128, 1), jnp.int32)
    k_file = jnp.zeros((1, SPAN), jnp.int32)
    for f in range(4):
        q_file += jnp.where(starts[0, f] <= q_pos, 1, 0)
        k_file += jnp.where(starts[0, f] <= k_pos, 1, 0)
    allowed = (q_file == k_file) & (k_pos <= q_pos) & (q_pos - k_pos < WINDOW)
    keys = pl.ds(first, SPAN)
    for g in range(HK):
        heads = [slice((2 * g + r) * HD, (2 * g + r + 1) * HD) for r in range(2)]
        q = jnp.concatenate([ref[:, head] for head in heads for ref in (own_ref, oth_ref)], 0)
        cols = slice(g * HD, (g + 1) * HD)
        scores = lax.dot_general(q, k_ref[keys, cols], CONTRACT1, preferred_element_type=F32)
        scores = 50.0 * jnp.tanh(scores * (1.0 / 16.0) / 50.0)
        expo = jnp.where(allowed, jnp.exp(scores), 0.0)
        weights = (expo / jnp.sum(expo, -1, keepdims=True)).astype(BF)
        out = dot(weights, v_ref[keys, cols])
        for x in range(X):
            span = slice(x * 64, x * 64 + 64)
            both = jnp.concatenate([out[0:64, span], out[64:128, span]], 1).astype(BF)
            at = x * 512 + g * 128
            for y in range(Y):
                o_ref[y, zh, :, at : at + 128] = both[0:32]
                o_ref[y, 1 - zh, :, at : at + 128] = both[32:64]


def row_block(block):
    total = jnp.sum(block * block, -1, keepdims=True)
    hi = total.astype(BF)
    lo = (total - hi.astype(F32)).astype(BF)
    lane = lax.broadcasted_iota(jnp.int32, (64, WIDE - COLS), 1)
    tail = jnp.where(lane == 0, hi.astype(F32), jnp.where(lane == 1, lo.astype(F32), 0.0))
    return jnp.concatenate([block, tail], 1).astype(BF)


def packed(block):
    tail = block[:, 128:256]
    lane = lax.broadcasted_iota(jnp.int32, (16, 128), 1)
    parts = [
        jnp.where(lane < 96, tail[16 * i : 16 * i + 16], pltpu.roll(tail[48:64], 96 - 32 * i, 1))
        for i in range(3)
    ]
    return jnp.concatenate([block[:, 0:128], *parts], 0)


def unpacked(block):
    last = jnp.concatenate([block[at : at + 16, 96:128] for at in (64, 80, 96)], 1)
    tail = jnp.concatenate([block[64:112, 0:96], last], 0)
    return jnp.concatenate([block[0:64], tail], 1)


def direction_kernel(d_ref, o_ref):
    o_ref[...] = row_block(d_ref[...])


def pair_kernel(place, mine_ref, their_ref, o_ref):
    za = place[5]
    for i in range(ZB):
        o_ref[i, za] = mine_ref[...]
        o_ref[i, 1 - za] = their_ref[...]


def repeat_kernel(i_ref, o_ref):
    for i in range(X):
        o_ref[i] = i_ref[...]


def sum_x_kernel(i_ref, o_ref):
    total = i_ref[0].astype(F32)
    for i in range(1, X):
        total += i_ref[i].astype(F32)
    o_ref[...] = total.astype(BF)


def sum_zl(i_ref):
    total = i_ref[0].astype(F32)
    for i in range(1, ZL):
        total += i_ref[i].astype(F32)
    return unpacked(total)


def sum_rows_kernel(i_ref, rows_ref, o_ref):
    total = sum_zl(i_ref)
    rows_ref[...] = total
    load = row_block(total)
    for i in range(ZL):
        o_ref[i] = load


def last_kernel(i_ref, rows_ref, d_ref, inv_ref, o_ref):
    damp = 1.0 - DAMP
    inv = inv_ref[0:1, 0:1]
    o_ref[...] = (1.0 + damp * KEEP) * d_ref[...] - (
        damp * rows_ref[...] + sum_zl(i_ref)
    ) * inv


def turn_kernel(proj_ref, s_ref, oproj_ref, os_ref):
    for i in range(4):
        span = slice(i * 512, i * 512 + 512)
        rows = proj_ref[:, span].astype(F32).T.astype(BF)
        for j in range(8):
            at = (j % X) * 512 + (2 * i + j // X) * 64
            oproj_ref[at : at + 64, :] = rows[j * 64 : j * 64 + 64]
    s = s_ref[...].astype(F32).T.astype(BF)
    for i in range(Y * ZH):
        for c in range(C):
            at = (i * C + c) * 32
            os_ref[c, i * 32 : i * 32 + 32, :] = s[at : at + 32]


def square_of(rows):
    return jnp.sum(rows[:, COLS : COLS + 2].astype(F32))


def scores_of(x, gain, tag_ref):
    return sum(dot(part, tag_ref[...]) for part in three(x * gain))


def two(x):
    hi = x.astype(BF).astype(F32)
    return hi, (x - hi).astype(BF).astype(F32)


def rows_of(columns, count):
    lane = lax.broadcasted_iota(jnp.int32, (count, 128), 1)
    table = jnp.zeros((count, 128), F32)
    for i, column in enumerate(columns):
        hi, lo = two(column)
        table = jnp.where(lane == 2 * i, hi, jnp.where(lane == 2 * i + 1, lo, table))
    if count < 128:
        table = jnp.concatenate([table, jnp.zeros((128 - count, 128), F32)], 0)
    return table.T[0:16]


def put_scores(load_ref, block, row, z):
    for i in range(Y):
        load_ref[block + i, row : row + 64, :] = z[i * 64 : i * 64 + 64].astype(BF)


def put_sums(load_ref, block, row, sums, scalar):
    rows = rows_of((*sums, jnp.full((256, 1), scalar, F32)), 256)
    for i in range(Y):
        own = rows[:, i * 64 : i * 64 + 64]
        load_ref[block + i, row : row + 16, :] = jnp.concatenate([own, own], 1).astype(BF)


def first_kernel(
    place, proj_far, u0, u1, u2, u3, own_ref, oth_ref, s_ref, gain_ref, tag_ref, h_ref, hd_ref, load_ref,
    proj_ref, rows_ref, sems,
):
    copies = []
    for r in range(X):
        span = pl.ds(r * 512, 512)
        copies.append(pltpu.make_async_copy(proj_far.at[span], proj_ref.at[span], sems.at[r]))
    for r, u in enumerate((u0, u1, u2, u3)):
        for za in range(ZA):
            copies.append(
                pltpu.make_async_copy(u.at[:, za], rows_ref.at[r, za], sems.at[X + ZA * r + za])
            )
    for copy in copies:
        copy.start()
    gain = gain_ref[...]
    halves = []
    for half, a_ref in enumerate((own_ref, oth_ref)):
        c = place[0] if half == 0 else 1 - place[0]
        halves.append((c, pl.multiple_of(c * 256, 256), a_ref))
    hs = [s_ref[c].astype(F32) for c, _, _ in halves]
    for r in range(X):
        copies[r].wait()
        span = slice(r * 512, r * 512 + 512)
        for i, (_, _, a_ref) in enumerate(halves):
            hs[i] += dot(a_ref[:, :, span].reshape(256, 512), proj_ref[span, :])
    for h, (c, at, _) in zip(hs, halves):
        h_ref[pl.ds(at, 256), :] = h
        z = scores_of(h, gain, tag_ref)
        z_hi = z.astype(BF).astype(F32)
        put_scores(load_ref, c * Y, 0, z_hi)
        put_scores(load_ref, c * Y, 64, z - z_hi)
    hds = [jnp.zeros((256, WIDE), F32)] * 2
    norm = 0.0
    for r in range(X):
        copies[X + ZA * r].wait()
        copies[X + ZA * r + 1].wait()
        rows = rows_ref[r].reshape(512, WIDE)
        x = lax.rem(place[4] + X - r, X)
        span = pl.ds(pl.multiple_of(x * 512, 512), 512)
        norm += square_of(rows)
        for i, (_, _, a_ref) in enumerate(halves):
            hds[i] += dot(a_ref[:, :, span].reshape(256, 512), rows)
    for h, hd, (c, at, _) in zip(hs, hds, halves):
        hd = hd[:, :COLS]
        hd_ref[pl.ds(at, 256), :] = hd
        put_scores(load_ref, c * Y, 128, scores_of(hd, gain, tag_ref))
        sums = (jnp.sum(h * h, -1, keepdims=True), jnp.sum(h * hd, -1, keepdims=True))
        put_sums(load_ref, c * Y, 192, sums, norm)


def moved_kernel(place, u_ref, own_ref, oth_ref, h_ref, gain_ref, tag_ref, mv_ref, load_ref):
    norm = square_of(u_ref[...])
    gain = gain_ref[...]
    for half, a_ref in enumerate((own_ref, oth_ref)):
        c = place[0] if half == 0 else 1 - place[0]
        at = pl.multiple_of(c * 256, 256)
        moved = dot(a_ref[...].reshape(256, ROWS), u_ref[...])[:, :COLS]
        mv_ref[pl.ds(at, 256), :] = moved
        put_scores(load_ref, c * Y, 0, scores_of(moved, gain, tag_ref))
        sums = (jnp.sum(h_ref[pl.ds(at, 256), :] * moved, -1, keepdims=True),)
        put_sums(load_ref, c * Y, 64, sums, norm)


def sum_parts_kernel(i_ref, o_ref):
    total = i_ref[0].astype(F32)
    for i in range(1, 8):
        total += i_ref[i].astype(F32)
    scores = total[: total.shape[0] - 16]
    if scores.shape[0] == 192:
        scores = jnp.concatenate([scores[0:64] + scores[64:128], scores[128:192]], 0)
    sums = total[total.shape[0] - 16 :]
    joined = [sums[2 * i : 2 * i + 1] + sums[2 * i + 1 : 2 * i + 2] for i in range(8)]
    o_ref[...] = jnp.concatenate([scores, *joined], 0)


def columns_of(rows):
    return jnp.concatenate([rows, jnp.zeros((120, 128), F32)], 0).T[:64]


def backward(zval, sumsq, tags, along, zdot, o_ref):
    rscale = lax.rsqrt(sumsq / D + NORM_EPS)
    tanh_val = jnp.tanh(rscale * zval / 30.0)
    slope = 1.0 - tanh_val * tanh_val
    expo = jnp.exp(30.0 * tanh_val)
    probs = expo / jnp.sum(expo, -1, keepdims=True)
    onehot = (tags == lax.broadcasted_iota(jnp.int32, (64, TAGS), 1)).astype(F32)
    dlogit = probs - onehot
    wgrad = dlogit * slope
    rho = jnp.sum(wgrad * zval, -1, keepdims=True)
    cube = rscale * rscale * rscale / D
    rdot = -cube * along
    mdot = rdot * zval + rscale * zdot
    ldot = slope * mdot
    pdot = probs * (ldot - jnp.sum(probs * ldot, -1, keepdims=True))
    wdot = pdot * slope - dlogit * 2.0 * tanh_val * slope * mdot / 30.0
    rhodot = jnp.sum(wdot * zval + wgrad * zdot, -1, keepdims=True)
    mixed = rdot * wgrad + rscale * wdot
    coeff = rhodot * cube + 3.0 * rho * rscale * rscale * rdot / D
    mixed = mixed.astype(BF)
    tail = rows_of((coeff, rho * cube), 64).astype(BF)
    for i in range(8):
        o_ref[i, 0:64, :] = mixed
        o_ref[i, 64:80, :] = tail


def tokens0_kernel(mine_ref, their_ref, tag_ref, total_ref, o_ref):
    total_ref[...] = mine_ref[...] + their_ref[...]
    columns = columns_of(total_ref[128:136, :])
    backward(
        total_ref[0:64, :], columns[:, 0:1], tag_ref[...], columns[:, 1:2], total_ref[64:128, :], o_ref
    )


def tokens1_kernel(mine_ref, their_ref, total_ref, tag_ref, o_ref, inv_ref):
    moved = mine_ref[...] + their_ref[...]
    product_sq = moved[65:66, 0:1]
    norm_sq = total_ref[130:131, 0:1]
    sigma = 2.0 * jnp.sqrt((product_sq / COUNT + MEAN_EPS) / (norm_sq / COUNT + MEAN_EPS))
    inv = 1.0 / sigma
    inv_ref[...] = jnp.broadcast_to(inv, (8, 128))
    columns0 = columns_of(total_ref[128:136, :])
    columns1 = columns_of(moved[64:72])
    along = KEEP * columns0[:, 1:2] - columns1[:, 0:1] * inv
    zdot = KEEP * total_ref[64:128, :] - moved[0:64] * inv
    backward(total_ref[0:64, :], columns0[:, 0:1], tag_ref[...], along, zdot, o_ref)


def product_kernel(second, place, m_ref, h_ref, hd_ref, *rest):
    if second:
        mv_ref, inv_ref, *rest = rest
    own_ref, oth_ref, gain_ref, tag_ref, o_ref, g_ref = rest
    gain = gain_ref[...]
    for c in range(C):
        span = slice(c * 256, c * 256 + 256)
        mixed = jnp.concatenate([m_ref[c * Y + i, 0:64, :] for i in range(Y)], 0)
        back = lax.dot_general(mixed, tag_ref[...], CONTRACT1, preferred_element_type=F32)
        columns = jnp.concatenate(
            [columns_of(m_ref[c * Y + i, 64:80, :].astype(F32)[0:8]) for i in range(Y)], 0
        )
        coeff, cubed = columns[:, 0:1] + columns[:, 1:2], columns[:, 2:3] + columns[:, 3:4]
        hd = hd_ref[span, :]
        if second:
            hd = KEEP * hd - mv_ref[span, :] * inv_ref[0:1, 0:1]
        g = back * gain - coeff * h_ref[span, :] - cubed * hd
        g_ref[span, 0:COLS] = g.astype(BF)
        g_ref[span, COLS:WIDE] = jnp.zeros((256, WIDE - COLS), BF)
    own_at = pl.multiple_of(place[0] * 256, 256)
    oth_at = pl.multiple_of((1 - place[0]) * 256, 256)
    g_own = g_ref[pl.ds(own_at, 256), :]
    g_oth = g_ref[pl.ds(oth_at, 256), :]
    for j in range(8):
        cols = slice(j * 256, j * 256 + 256)
        part = lax.dot_general(
            own_ref[:, :, cols].reshape(256, 256), g_own, CONTRACT0, preferred_element_type=F32
        ) + lax.dot_general(
            oth_ref[:, :, cols].reshape(256, 256), g_oth, CONTRACT0, preferred_element_type=F32
        )
        for i in range(4):
            o_ref[j // 2, (j % 2) * 4 + i] = packed(part[i * 64 : i * 64 + 64]).astype(BF)


def swap(x, axis):
    return lax.ppermute(x, axis, [(0, 1), (1, 0)])


def deal(x, axis):
    return lax.all_to_all(x, axis, 0, 0, tiled=True)


def local(queries, keys, values, stream, out_proj, norm_gain, tag_proj, direction, starts, tags):
    core = lax.axis_index("c")
    ypos = lax.axis_index("y")
    zhpos = lax.axis_index("zh")
    own_at = ((ypos * ZH + zhpos) * C + core) * 32
    oth_at = ((ypos * ZH + 1 - zhpos) * C + core) * 32
    place = jnp.stack([core, own_at, oth_at, zhpos, lax.axis_index("x"), lax.axis_index("za")]).astype(jnp.int32)
    own_tags = tags[0].reshape(Y, ZH, C, 32).transpose(2, 0, 1, 3).reshape(C * Y, 64)[core * Y + ypos]
    own_tags = own_tags[:, None]
    gain = norm_gain[None]

    row = call(direction_kernel, shape(64, WIDE, dtype=BF), direction)
    proj, toks = call(
        turn_kernel,
        (shape(ROWS, COLS, dtype=BF), shape(C, 256, COLS, dtype=BF)),
        out_proj.T,
        stream[0].T,
    )
    theirs = swap(queries[0], "zh")
    far, proj, toks, own_tags = lax.optimization_barrier((swap(row, "za"), proj, toks, own_tags))
    pairs = call(pair_kernel, shape(ZB, ZA, 64, WIDE, dtype=BF), place, row, far, smem=1)
    by_zl = deal(pairs, "zb")
    pair = call(
        attend_kernel,
        shape(Y, ZH, 32, ROWS, dtype=BF),
        place,
        starts,
        keys[0],
        values[0],
        queries[0],
        theirs,
        smem=2,
    )
    u0 = [by_zl] + [
        lax.ppermute(by_zl, "x", [(i, (i + r) % X) for i in range(X)]) for r in range(1, X)
    ]
    own, *u0 = lax.optimization_barrier((deal(pair.reshape(Y, 64, ROWS), "y"), *u0))
    other = swap(own, "c")

    def product(second, *args):
        sent = call(
            functools.partial(product_kernel, second, scratch=[pltpu.VMEM((512, WIDE), BF)]),
            shape(X, ZL, PACK, 128, dtype=BF),
            place,
            *args,
            own,
            other,
            gain,
            tag_proj,
            smem=1,
        )
        part = call(sum_x_kernel, shape(ZL, PACK, 128, dtype=BF), deal(sent, "x"))
        return deal(part, ZAXES)

    def token_sum(load, rows, kernel, outs, *args):
        part = call(sum_parts_kernel, shape(rows, 128), deal(load, ("c", "y")))
        return call(kernel, outs, part, swap(part, "zh"), *args, own_tags)

    h_loc, hdot0, load = call(
        functools.partial(
            first_kernel,
            scratch=[
                pltpu.VMEM((ROWS, COLS), BF),
                pltpu.VMEM((X, ZA, ZB, 64, WIDE), BF),
                pltpu.SemaphoreType.DMA((3 * X,)),
            ],
        ),
        (shape(512, COLS), shape(512, COLS), shape(8, 208, 128, dtype=BF)),
        place,
        proj,
        *u0,
        own,
        other,
        toks,
        gain,
        tag_proj,
        smem=1,
        far=X + 1,
    )
    total, mixed = token_sum(load, 136, tokens0_kernel, (shape(136, 128), shape(8, 80, 128, dtype=BF)))
    rows0, sent = call(
        sum_rows_kernel,
        (shape(64, COLS), shape(ZL, 64, WIDE, dtype=BF)),
        product(False, deal(mixed, ("c", "y")), h_loc, hdot0),
    )
    rows = deal(sent, ZAXES).reshape(ZL * 64, WIDE)
    full0 = deal(call(repeat_kernel, shape(X, ZL * 64, WIDE, dtype=BF), rows), "x").reshape(ROWS, WIDE)
    moved, load = call(
        moved_kernel,
        (shape(512, COLS), shape(8, 80, 128, dtype=BF)),
        place,
        full0,
        own,
        other,
        h_loc,
        gain,
        tag_proj,
        smem=1,
    )
    mixed, inv = token_sum(
        load, 72, tokens1_kernel, (shape(8, 80, 128, dtype=BF), shape(8, 128)), total
    )
    arrived = product(True, deal(mixed, ("c", "y")), h_loc, hdot0, moved, inv)
    return call(last_kernel, shape(64, COLS), arrived, rows0, direction, inv)


def solution(mesh):
    fine = Mesh(mesh.devices.reshape(ZA, ZB, X, Y, ZH, C), ("za", "zb", "x", "y", "zh", "c"))
    dp, mp = ("za", "zb", "x"), ("y", "zh", "c")
    return jax.shard_map(
        local,
        mesh=fine,
        in_specs=(
            P(dp, mp, None),
            P(dp, None, None),
            P(dp, None, None),
            P(dp, None, mp),
            P(None, mp),
            P(mp),
            P(mp, None),
            P(dp, mp),
            P(dp, None),
            P(dp, None),
        ),
        out_specs=P(dp, mp),
        check_vma=False,
    )
```
